32 devices in a mesh: shard: 16 (over z, y, x), replica: 2 (over core).
Axes of the slice: x: 2, y: 2, z: 4, core: 2. Of those that a mesh axis runs over, the one named last changes fastest.
Arguments:
- grads: bfloat16 [32, 196608], P(('shard', 'replica')), may hold values from -6 to 6
- master: float32 [196608], P(('shard', 'replica')), may hold values from -120 to 120
- first_moment: float32 [196608], P(('shard', 'replica')), may hold values from -0.15625 to 0.15625
- second_moment: float32 [196608], P(('shard', 'replica')), may hold values from 1e-05 to 0.001
- owners: int32 [24], replicated, may hold values from 0 to 15, as said below
Outputs:
- new_master: float32 [196608], P(('shard', 'replica'))
- new_first: float32 [196608], P(('shard', 'replica'))
- new_second: float32 [196608], P(('shard', 'replica'))
- model_copy: bfloat16 [24, 8192], replicated
The draws below stay inside these ranges and needn't reach their ends.
Inputs may be any that keep to these rules, and one draw needn't show every extreme that they name: owners[c] names the index along shard that owns model column c; no index owns more than 3 columns, and one owns exactly 3.
All inputs are finite; a program needn't handle non-finite values.
Results may differ from the reference program's by a relative error of at most 0.0085.
Values may be sent and summed in bfloat16 or wider, within the bound.
No kernel may reach another device: no remote copies, remote signals or barrier semaphores. Data moves between devices by JAX's collectives and lax.ppermute only.
A program may use at most 64 MiB of HBM per device.

```python
import math
import jax
import jax.numpy as jnp
from jax import lax

D = 8192
NC = 24
P_SIZE = 196608
MAXC = 3
N_SHARD = 16
DEVICES = 32


def draw_master(key, part):
    key = jax.random.fold_in(key, 17)
    base_key, column_key = jax.random.split(key)
    block_index = (jnp.arange(D, dtype=jnp.int32) // (D // DEVICES)).astype(jnp.float32)
    rising = jnp.sqrt(1.0 + 2.0 * block_index / max(DEVICES - 1, 1))
    column_scale = jnp.exp(jax.random.uniform(column_key, (NC,), jnp.float32, 0.0, math.log(10.0)))
    values = jax.random.truncated_normal(base_key, -4.0, 4.0, (D, NC), jnp.float32)
    return (0.1 * values * rising[:, None] * column_scale[None, :]).reshape(D * NC)


def draw_owners(key, part):
    key = jax.random.fold_in(key, 29)
    pick_key, spread_key, order_key = jax.random.split(key, 3)
    busiest = jax.random.randint(pick_key, (), 0, N_SHARD, dtype=jnp.int32)
    slot_owner = (busiest + 1 + jnp.arange((N_SHARD - 1) * MAXC, dtype=jnp.int32) // MAXC) % N_SHARD
    chosen = jax.random.permutation(spread_key, slot_owner)[:NC - MAXC]
    owners_all = jnp.concatenate([jnp.zeros((MAXC,), jnp.int32) + busiest, chosen.astype(jnp.int32)])
    return jax.random.permutation(order_key, owners_all).astype(jnp.int32)


def with_spikes(drawn, stream_key, source, target, parts, factor):
    def block_of(axis_at):
        return (jnp.arange(drawn.shape[axis_at]) // (drawn.shape[axis_at] // parts)).reshape((-1,) + (1,) * (drawn.ndim - 1 - axis_at))

    first = jax.random.permutation(stream_key, parts)[block_of(target)]
    other_side = (block_of(target) + parts // 2) % parts
    return jnp.where((block_of(source) == first) | (block_of(source) == other_side), factor * drawn, drawn)


def steps_of(rng, extent, pieces, low, top_value):
    gain, own = 1.0, jax.random.fold_in(rng, 6)
    for axis_at, parts in pieces:
        heights = jnp.exp(jax.random.uniform(jax.random.fold_in(own, axis_at), (parts,), jnp.float32, low / len(pieces), top_value / len(pieces)))
        gain = gain * jnp.repeat(heights, extent[axis_at] // parts).reshape([-1 if axis == axis_at else 1 for axis in range(len(extent))])
    return gain


def noise(own_key, extent, scale, limit, cuts=(), held_as=jnp.bfloat16):
    factor_of = steps_of(own_key, extent, cuts, -0.22, 0.18) if cuts else 1.0
    result = jax.random.normal(own_key, extent, jnp.float32) * scale * factor_of
    return jnp.minimum(jnp.maximum(result, -limit), limit).astype(held_as)


def gaussian_with(own_key, extent, width, limit, cuts, heavy, kind=jnp.bfloat16):
    drawn = width * jax.random.normal(own_key, extent, jnp.float32)
    if cuts:
        drawn = drawn * steps_of(own_key, extent, cuts, -0.22, 0.18)
    return jnp.clip(with_spikes(drawn, jax.random.fold_in(own_key, 3), *heavy), -limit, limit).astype(kind)


def setup_inputs(seed: int = 0) -> dict:
    splits = jax.random.split(jax.random.key(seed), 6)
    grads = gaussian_with(splits[0], (DEVICES, P_SIZE), 1.0, 6.0, ((0, 32),), (0, 1, 32, 2.75))
    master = draw_master(jax.random.fold_in(splits[5], 71), 0)
    first_moment = noise(splits[2], (P_SIZE,), 0.01, 0.15625, ((0, 32),), jnp.float32)
    second_moment = jnp.clip(jnp.exp(math.log(0.001) - 4.6051703 * jax.random.uniform(splits[3], (P_SIZE,), jnp.float32) ** steps_of(splits[3], (P_SIZE,), ((0, 32),), -0.2, 0.2)), 9.999999747378752e-06, 0.001)
    owners = draw_owners(jax.random.fold_in(splits[5], 71), 0)
    return {"grads": grads, "master": master, "first_moment": first_moment, "second_moment": second_moment, "owners": owners}


learning_rate = 0.1
adam_epsilon = 1e-08
norm_epsilon = 1e-06
first_correction = 1.0 - 0.9 ** 20
second_correction = 1.0 - 0.95 ** 20

def adam_step(gradient, master, first_moment, second_moment):
    new_first = 0.9 * first_moment + 0.1 * gradient
    new_second = 0.95 * second_moment + 0.05 * gradient * gradient
    stepped = master - learning_rate * (new_first / first_correction) / (jnp.sqrt(new_second / second_correction) + adam_epsilon)
    return (new_first, new_second, stepped)

def flat_positions(owners):
    column_ids = jnp.arange(owners.shape[0], dtype=jnp.int32)
    ranked_below = owners[None, :] < owners[:, None]
    same_before = (owners[None, :] == owners[:, None]) & (column_ids[None, :] < column_ids[:, None])
    return lax.optimization_barrier(jnp.sum((ranked_below | same_before).astype(jnp.int32), axis=1))

def reference(grads, master, first_moment, second_moment, owners):

    def accumulate(step_index, running):
        return running + grads[step_index].astype(jnp.float32)
    total = lax.fori_loop(0, grads.shape[0], accumulate, jnp.zeros((grads.shape[1],), jnp.float32))
    gradient = total / grads.shape[0]
    new_first, new_second, stepped = adam_step(gradient, master, first_moment, second_moment)
    matrix = stepped.reshape(D, NC)
    squares = lax.optimization_barrier(jnp.sum(matrix * matrix, axis=0))
    factor = lax.rsqrt(squares / D + norm_epsilon)
    normed = matrix * factor[None, :]
    position = flat_positions(owners)
    model_copy = jnp.take(normed, position, axis=1).T.astype(jnp.bfloat16)
    return (normed.reshape(D * NC), new_first, new_second, model_copy)
```

```python
import jax
import jax.numpy as jnp
from jax import lax
from jax.sharding import PartitionSpec as P

D = 8192


learning_rate = 0.1
adam_epsilon = 1e-08
norm_epsilon = 1e-06
first_correction = 1.0 - 0.9**20
second_correction = 1.0 - 0.95**20
AXES = ("shard", "replica")


def adam_step(gradient, master, first_moment, second_moment):
    new_first = 0.9 * first_moment + 0.1 * gradient
    new_second = 0.95 * second_moment + 0.05 * gradient * gradient
    stepped = master - learning_rate * (new_first / first_correction) / (
        jnp.sqrt(new_second / second_correction) + adam_epsilon
    )
    return (new_first, new_second, stepped)


def flat_positions(owners):
    column_ids = jnp.arange(owners.shape[0], dtype=jnp.int32)
    ranked_below = owners[None, :] < owners[:, None]
    same_before = (owners[None, :] == owners[:, None]) & (column_ids[None, :] < column_ids[:, None])
    return jnp.sum((ranked_below | same_before).astype(jnp.int32), axis=1)


def on_device(grads, master, first_moment, second_moment, owners):
    devices = lax.axis_size("shard") * lax.axis_size("replica")
    chunk = master.shape[0]
    columns = owners.shape[0]
    pieces = lax.all_to_all(grads.reshape(devices, chunk // 128, 128), AXES, 0, 0, tiled=True)
    gradient = jnp.sum(pieces.astype(jnp.float32), axis=0).reshape(-1) / devices
    new_first, new_second, stepped = adam_step(gradient, master, first_moment, second_moment)
    matrix = stepped.reshape(-1, columns)
    position = flat_positions(owners)
    column_ids = jnp.arange(columns, dtype=jnp.int32)
    placement = (position[:, None] == column_ids[None, :]).astype(jnp.bfloat16)
    rows = jnp.einsum(
        "cj,rj->cr", placement, matrix.astype(jnp.bfloat16), preferred_element_type=jnp.float32
    ).astype(jnp.bfloat16)
    gathered = lax.all_to_all(
        jnp.broadcast_to(rows[None], (devices,) + rows.shape), AXES, 0, 0, tiled=True
    )
    wide = gathered.astype(jnp.float32)
    factor = lax.rsqrt(jnp.sum(wide * wide, axis=(0, 2)) / D + norm_epsilon)
    model_copy = jnp.transpose(wide * factor[None, :, None], (1, 0, 2)).reshape(columns, -1)
    flat_factor = jnp.sum(jnp.where(position[:, None] == column_ids[None, :], factor[:, None], 0.0), axis=0)
    new_master = (matrix * flat_factor[None, :]).reshape(-1)
    return (new_master, new_first, new_second, model_copy.astype(jnp.bfloat16))


def solution(mesh):
    placed = (P(AXES, None), P(AXES), P(AXES), P(AXES), P())
    return jax.shard_map(
        on_device,
        mesh=mesh,
        in_specs=placed,
        out_specs=(P(AXES), P(AXES), P(AXES), P()),
        check_vma=False,
    )
```

```python
import jax
import jax.numpy as jnp
from jax import lax
from jax.experimental import pallas as pl
from jax.sharding import PartitionSpec as P

D = 8192


learning_rate = 0.1
adam_epsilon = 1e-08
norm_epsilon = 1e-06
first_correction = 1.0 - 0.9**20
second_correction = 1.0 - 0.95**20
AXES = ("shard", "replica")
LANES = 128


def adam_step(gradient, master, first_moment, second_moment):
    new_first = 0.9 * first_moment + 0.1 * gradient
    new_second = 0.95 * second_moment + 0.05 * gradient * gradient
    stepped = master - learning_rate * (new_first / first_correction) / (
        jnp.sqrt(new_second / second_correction) + adam_epsilon
    )
    return (new_first, new_second, stepped)


def flat_positions(owners):
    column_ids = jnp.arange(owners.shape[0], dtype=jnp.int32)
    ranked_below = owners[None, :] < owners[:, None]
    same_before = (owners[None, :] == owners[:, None]) & (column_ids[None, :] < column_ids[:, None])
    return jnp.sum((ranked_below | same_before).astype(jnp.int32), axis=1)


def pack_kernel(grads_ref, out_ref):
    devices, lines, lanes = out_ref.shape
    for k in range(devices):
        row = grads_ref[:, k * lines * lanes : (k + 1) * lines * lanes].astype(jnp.float32)
        out_ref[k] = row.reshape(lines, lanes).astype(jnp.bfloat16)


def pack(grads, devices):
    lines = grads.shape[1] // devices // LANES
    return pl.pallas_call(
        pack_kernel, out_shape=jax.ShapeDtypeStruct((devices, lines, LANES), jnp.bfloat16)
    )(grads)


def finish_kernel(owners_ref, stepped_ref, own_ref, other_ref, master_ref, copy_ref):
    core = lax.axis_index("replica")
    chips, columns, width = own_ref.shape
    total = jnp.zeros((columns, width), jnp.float32)
    for ref in (own_ref, other_ref):
        for c in range(chips):
            value = ref[c].astype(jnp.float32)
            total = total + value * value
    factor = lax.rsqrt(jnp.sum(total, axis=1, keepdims=True) / D + norm_epsilon)
    for ref, place in ((own_ref, core), (other_ref, 1 - core)):
        for c in range(chips):
            start = pl.multiple_of((2 * c + place) * width, width)
            copy_ref[:, pl.ds(start, width)] = (ref[c].astype(jnp.float32) * factor).astype(jnp.bfloat16)
    square = (columns, columns)
    down = lax.broadcasted_iota(jnp.int32, square, 0)
    along = lax.broadcasted_iota(jnp.int32, square, 1)
    owner_row = jnp.broadcast_to(owners_ref[...].astype(jnp.float32), square)
    owner_column = jnp.sum(jnp.where(down == along, owner_row, 0.0), axis=1, keepdims=True)
    before = (owner_row < owner_column) | ((owner_row == owner_column) & (along < down))
    position = jnp.sum(before.astype(jnp.float32), axis=1, keepdims=True).astype(jnp.int32)
    period = columns // 8
    lane = lax.broadcasted_iota(jnp.int32, (1, LANES), 1)
    line = lax.broadcasted_iota(jnp.int32, stepped_ref.shape, 0) % period
    spread = jnp.zeros(stepped_ref.shape, jnp.float32)
    for p in range(period):
        flat_column = (p * LANES + lane) % columns
        picked = jnp.sum(jnp.where(position == flat_column, factor, 0.0), axis=0, keepdims=True)
        spread = jnp.where(line == p, picked, spread)
    master_ref[...] = stepped_ref[...] * spread


def finish_narrow(owners, stepped, blocks):
    columns = owners.shape[0]
    blocks = blocks.astype(jnp.float32)
    factor = lax.rsqrt(jnp.sum(blocks * blocks, axis=(0, 2)) / D + norm_epsilon)
    scaled = jnp.transpose(blocks * factor[None, :, None], (1, 0, 2))
    flat_factor = jnp.zeros((columns,), jnp.float32).at[flat_positions(owners)].set(factor)
    new_master = (stepped.reshape(-1, columns) * flat_factor).reshape(stepped.shape)
    return (new_master, scaled.reshape(columns, -1).astype(jnp.bfloat16))


def spread(value, axes, size):
    return lax.all_to_all(jnp.broadcast_to(value[None], (size,) + value.shape), axes, 0, 0, tiled=True)


def finish(owners, stepped, own, other):
    chips, columns, width = own.shape
    return pl.pallas_call(
        finish_kernel,
        out_shape=(
            jax.ShapeDtypeStruct(stepped.shape, jnp.float32),
            jax.ShapeDtypeStruct((columns, 2 * chips * width), jnp.bfloat16),
        ),
    )(owners[None, :], stepped, own, other)


def on_device(grads, master, first_moment, second_moment, owners):
    shards, replicas = lax.axis_size("shard"), lax.axis_size("replica")
    devices = shards * replicas
    columns = owners.shape[0]
    pieces = lax.all_to_all(pack(grads, devices), AXES, 0, 0, tiled=True)
    gradient = jnp.sum(pieces.astype(jnp.float32), axis=0).reshape(-1) / devices
    new_first, new_second, stepped = adam_step(gradient, master, first_moment, second_moment)
    matrix = stepped.reshape(-1, columns)
    position = flat_positions(owners)
    column_ids = jnp.arange(columns, dtype=jnp.int32)
    placement = (position[:, None] == column_ids[None, :]).astype(jnp.bfloat16)
    rows = jnp.einsum(
        "cj,rj->cr", placement, matrix.astype(jnp.bfloat16), preferred_element_type=jnp.float32
    ).astype(jnp.bfloat16)
    flat_stepped = stepped.reshape(-1, LANES)
    if replicas == 2 and rows.shape[1] % LANES == 0:
        own = spread(rows, "shard", shards)
        other = lax.ppermute(own, "replica", [(0, 1), (1, 0)])
        new_master, model_copy = finish(owners, flat_stepped, own, other)
    else:
        new_master, model_copy = finish_narrow(owners, flat_stepped, spread(rows, AXES, devices))
    return (new_master.reshape(-1), new_first, new_second, model_copy)


def solution(mesh):
    placed = (P(AXES, None), P(AXES), P(AXES), P(AXES), P())
    return jax.shard_map(
        on_device,
        mesh=mesh,
        in_specs=placed,
        out_specs=(P(AXES), P(AXES), P(AXES), P()),
        check_vma=False,
    )
```

```python
import jax
import jax.numpy as jnp
from jax import lax
from jax.experimental import pallas as pl
from jax.experimental.pallas import tpu as pltpu
from jax.sharding import PartitionSpec as P

D = 8192


learning_rate = 0.1
adam_epsilon = 1e-08
norm_epsilon = 1e-06
first_correction = 1.0 - 0.9**20
second_correction = 1.0 - 0.95**20
AXES = ("shard", "replica")
LANES = 128


def adam_step(gradient, master, first_moment, second_moment):
    new_first = 0.9 * first_moment + 0.1 * gradient
    new_second = 0.95 * second_moment + 0.05 * gradient * gradient
    stepped = master - learning_rate * (new_first / first_correction) / (
        jnp.sqrt(new_second / second_correction) + adam_epsilon
    )
    return (new_first, new_second, stepped)


def flat_positions(owners):
    column_ids = jnp.arange(owners.shape[0], dtype=jnp.int32)
    ranked_below = owners[None, :] < owners[:, None]
    same_before = (owners[None, :] == owners[:, None]) & (column_ids[None, :] < column_ids[:, None])
    return jnp.sum((ranked_below | same_before).astype(jnp.int32), axis=1)


def small(**more):
    return pltpu.CompilerParams(vmem_limit_bytes=6 * 2**20, **more)


def pack_kernel(grads_ref, out_ref, long_ref, wide_ref, packed_ref, in_sems, out_sems):
    parts, _, width = long_ref.shape
    devices, lines, lanes = out_ref.shape
    each = devices // parts
    row_ref = wide_ref.reshape(1, wide_ref.shape[0] * lanes)
    taken, given = [], []
    for p in range(parts):
        source = grads_ref.at[:, pl.ds(p * width, width)]
        taken.append(pltpu.make_async_copy(source, long_ref.at[p], in_sems.at[p]))
        place = pl.ds(p * each, each)
        given.append(pltpu.make_async_copy(packed_ref.at[place], out_ref.at[place], out_sems.at[p]))
        taken[p].start()
    for p in range(parts):
        taken[p].wait()
        row_ref[:, p * width : (p + 1) * width] = long_ref[p].astype(jnp.float32)
        for k in range(p * each, (p + 1) * each):
            packed_ref[k] = wide_ref[k * lines : (k + 1) * lines].astype(jnp.bfloat16)
        given[p].start()
    for copy in given:
        copy.wait()


def pack(grads, devices):
    lines = grads.shape[1] // devices // LANES
    if lines % 16:
        return grads.reshape(devices, lines, LANES)
    parts = 4
    packed = (devices, lines, LANES)
    return pl.pallas_call(
        pack_kernel,
        in_specs=[pl.BlockSpec(memory_space=pl.ANY)],
        out_specs=pl.BlockSpec(memory_space=pl.ANY),
        out_shape=jax.ShapeDtypeStruct(packed, jnp.bfloat16),
        scratch_shapes=[
            pltpu.VMEM((parts, 1, grads.shape[1] // parts), jnp.bfloat16),
            pltpu.VMEM((grads.shape[1] // LANES, LANES), jnp.float32),
            pltpu.VMEM(packed, jnp.bfloat16),
            pltpu.SemaphoreType.DMA((parts,)),
            pltpu.SemaphoreType.DMA((parts,)),
        ],
    )(grads)


def positions_column(owners_ref):
    columns = owners_ref.shape[1]
    square = (columns, columns)
    down = lax.broadcasted_iota(jnp.int32, square, 0)
    along = lax.broadcasted_iota(jnp.int32, square, 1)
    owner_row = jnp.broadcast_to(owners_ref[...].astype(jnp.float32), square)
    owner_column = jnp.sum(jnp.where(down == along, owner_row, 0.0), axis=1, keepdims=True)
    before = (owner_row < owner_column) | ((owner_row == owner_column) & (along < down))
    return jnp.sum(before.astype(jnp.float32), axis=1, keepdims=True).astype(jnp.int32)


def middle_kernel(
    owners_ref, pieces_ref, master_ref, first_ref, second_ref, gradient_ref, copies_ref, flat_ref
):
    devices = pieces_ref.shape[0]
    copies, columns, width = copies_ref.shape
    total = pieces_ref[0].astype(jnp.float32)
    for k in range(1, devices):
        total = total + pieces_ref[k].astype(jnp.float32)
    gradient = total / devices
    gradient_ref[...] = gradient
    flat_ref[...] = adam_step(gradient, master_ref[...], first_ref[...], second_ref[...])[2]
    period = columns // 8
    span = period * LANES
    group = span // columns
    lines = flat_ref.shape[0] // period
    wide = [flat_ref[pl.ds(b, lines, stride=period), :].astype(jnp.bfloat16) for b in range(period)]
    wide = jnp.concatenate(wide, axis=1)
    line = lax.broadcasted_iota(jnp.int32, (lines, width), 0)
    row = lax.broadcasted_iota(jnp.int32, (lines, width), 1)
    repeat = (row // group == line).astype(jnp.bfloat16)
    spread = lax.dot_general(wide, repeat, (((0,), (0,)), ((), ())), preferred_element_type=jnp.float32)
    entry = lax.broadcasted_iota(jnp.int32, (span, width), 0)
    row = lax.broadcasted_iota(jnp.int32, (span, width), 1)
    kept = jnp.where(entry // columns == row % group, spread, 0.0).astype(jnp.bfloat16)
    column = lax.broadcasted_iota(jnp.int32, (columns, span), 1) % columns
    pick = (column == positions_column(owners_ref)).astype(jnp.bfloat16)
    rows = jnp.dot(pick, kept, preferred_element_type=jnp.float32).astype(jnp.bfloat16)
    for k in range(copies):
        copies_ref[k] = rows


def middle(owners, pieces, master, first_moment, second_moment, copies):
    columns = owners.shape[0]
    flat = pieces.shape[1:]
    width = flat[0] * LANES // columns
    return pl.pallas_call(
        middle_kernel,
        out_shape=(
            jax.ShapeDtypeStruct(flat, jnp.float32),
            jax.ShapeDtypeStruct((copies, columns, width), jnp.bfloat16),
        ),
        scratch_shapes=[pltpu.VMEM(flat, jnp.float32)],
        compiler_params=small(),
    )(owners[None, :], pieces, *(x.reshape(flat) for x in (master, first_moment, second_moment)))


def squares_kernel(blocks_ref, total_ref):
    total = jnp.zeros(total_ref.shape, jnp.float32)
    for k in range(blocks_ref.shape[0]):
        value = blocks_ref[k].astype(jnp.float32)
        total = total + value * value
    total_ref[...] = total


def squares(blocks):
    return pl.pallas_call(
        squares_kernel,
        out_shape=jax.ShapeDtypeStruct(blocks.shape[1:], jnp.float32),
        compiler_params=small(),
        cost_estimate=pl.CostEstimate(
            flops=2 * blocks.size, bytes_accessed=2 * blocks.size, transcendentals=0
        ),
    )(blocks)


def finish_kernel(owners_ref, stepped_ref, part_ref, own_ref, other_ref, master_ref, copy_ref, scaled_ref, sems):
    core = lax.axis_index("replica")
    chips, columns, width = own_ref.shape
    total = part_ref[...]
    for k in range(chips):
        value = other_ref[k].astype(jnp.float32)
        total = total + value * value
    factor = lax.rsqrt(jnp.sum(total, axis=1, keepdims=True) / D + norm_epsilon)
    parts = sems.shape[0]
    each = chips // parts
    copies = []
    for p in range(parts):
        for k in range(p * each, (p + 1) * each):
            for ref, place in ((own_ref, core), (other_ref, 1 - core)):
                start = pl.multiple_of((2 * k + place) * width, width)
                scaled_ref[:, pl.ds(start, width)] = (ref[k].astype(jnp.float32) * factor).astype(jnp.bfloat16)
        part = pl.ds(p * 2 * each * width, 2 * each * width)
        copies.append(pltpu.make_async_copy(scaled_ref.at[:, part], copy_ref.at[:, part], sems.at[p]))
        copies[p].start()
    position = positions_column(owners_ref)
    period = columns // 8
    lane = lax.broadcasted_iota(jnp.int32, (1, LANES), 1)
    line = lax.broadcasted_iota(jnp.int32, stepped_ref.shape, 0) % period
    spread = jnp.zeros(stepped_ref.shape, jnp.float32)
    for p in range(period):
        flat_column = (p * LANES + lane) % columns
        picked = jnp.sum(jnp.where(position == flat_column, factor, 0.0), axis=0, keepdims=True)
        spread = jnp.where(line == p, picked, spread)
    master_ref[...] = stepped_ref[...] * spread
    for copy in copies:
        copy.wait()


def finish_narrow(owners, stepped, blocks):
    columns = owners.shape[0]
    blocks = blocks.astype(jnp.float32)
    factor = lax.rsqrt(jnp.sum(blocks * blocks, axis=(0, 2)) / D + norm_epsilon)
    scaled = jnp.transpose(blocks * factor[None, :, None], (1, 0, 2))
    flat_factor = jnp.zeros((columns,), jnp.float32).at[flat_positions(owners)].set(factor)
    new_master = (stepped.reshape(-1, columns) * flat_factor).reshape(stepped.shape)
    return (new_master, scaled.reshape(columns, -1).astype(jnp.bfloat16))


def spread(value, axes, size):
    return lax.all_to_all(jnp.broadcast_to(value[None], (size,) + value.shape), axes, 0, 0, tiled=True)


def finish(owners, stepped, part, own, other):
    chips, columns, width = own.shape
    wide = (columns, 2 * chips * width)
    parts = 4 if chips % 4 == 0 else 1
    whole = pl.BlockSpec(memory_space=pltpu.VMEM)
    return pl.pallas_call(
        finish_kernel,
        in_specs=[whole] * 5,
        out_specs=(whole, pl.BlockSpec(memory_space=pl.ANY)),
        out_shape=(
            jax.ShapeDtypeStruct(stepped.shape, jnp.float32),
            jax.ShapeDtypeStruct(wide, jnp.bfloat16),
        ),
        scratch_shapes=[pltpu.VMEM(wide, jnp.bfloat16), pltpu.SemaphoreType.DMA((parts,))],
        compiler_params=small(),
    )(owners[None, :], stepped, part, own, other)


def on_device(grads, master, first_moment, second_moment, owners):
    shards, replicas = lax.axis_size("shard"), lax.axis_size("replica")
    devices = shards * replicas
    columns = owners.shape[0]
    pieces = lax.all_to_all(pack(grads, devices), AXES, 0, 0, tiled=True)
    if replicas == 2 and master.shape[0] % (columns * LANES) == 0:
        gradient, copies = middle(owners, pieces, master, first_moment, second_moment, shards)
        new_first, new_second, stepped = adam_step(
            gradient.reshape(-1), master, first_moment, second_moment
        )
        own = lax.all_to_all(copies, "shard", 0, 0, tiled=True)
        other = lax.ppermute(own, "replica", [(0, 1), (1, 0)])
        new_master, model_copy = finish(owners, stepped.reshape(-1, LANES), squares(own), own, other)
        return (new_master.reshape(-1), new_first, new_second, model_copy)
    gradient = jnp.sum(pieces.astype(jnp.float32), axis=0).reshape(-1) / devices
    new_first, new_second, stepped = adam_step(gradient, master, first_moment, second_moment)
    rows = jnp.take(stepped.reshape(-1, columns), flat_positions(owners), axis=1).T.astype(jnp.bfloat16)
    new_master, model_copy = finish_narrow(owners, stepped, spread(rows, AXES, devices))
    return (new_master, new_first, new_second, model_copy)


def solution(mesh):
    placed = (P(AXES, None), P(AXES), P(AXES), P(AXES), P())
    return jax.shard_map(
        on_device,
        mesh=mesh,
        in_specs=placed,
        out_specs=(P(AXES), P(AXES), P(AXES), P()),
        check_vma=False,
    )
```

```python
import jax
import jax.numpy as jnp
from jax import lax
from jax.experimental import pallas as pl
from jax.experimental.pallas import tpu as pltpu
from jax.sharding import PartitionSpec as P

D = 8192


learning_rate = 0.1
adam_epsilon = 1e-08
norm_epsilon = 1e-06
first_correction = 1.0 - 0.9**20
second_correction = 1.0 - 0.95**20
AXES = ("shard", "replica")
LANES = 128


def adam_step(gradient, master, first_moment, second_moment):
    new_first = 0.9 * first_moment + 0.1 * gradient
    new_second = 0.95 * second_moment + 0.05 * gradient * gradient
    stepped = master - learning_rate * (new_first / first_correction) / (
        jnp.sqrt(new_second / second_correction) + adam_epsilon
    )
    return (new_first, new_second, stepped)


def flat_positions(owners):
    column_ids = jnp.arange(owners.shape[0], dtype=jnp.int32)
    ranked_below = owners[None, :] < owners[:, None]
    same_before = (owners[None, :] == owners[:, None]) & (column_ids[None, :] < column_ids[:, None])
    return jnp.sum((ranked_below | same_before).astype(jnp.int32), axis=1)


def small(**more):
    return pltpu.CompilerParams(vmem_limit_bytes=6 * 2**20, **more)


def pack_kernel(grads_ref, out_ref, wide_ref):
    devices, lines, lanes = out_ref.shape
    row_ref = wide_ref.reshape(1, wide_ref.shape[0] * lanes)
    width = lines * lanes
    for k in range(devices):
        row_ref[:, k * width : (k + 1) * width] = grads_ref[:, k * width : (k + 1) * width].astype(jnp.float32)
        out_ref[k] = wide_ref[k * lines : (k + 1) * lines].astype(jnp.bfloat16)


def pack(grads, devices):
    lines = grads.shape[1] // devices // LANES
    if lines % 16:
        return grads.reshape(devices, lines, LANES)
    return pl.pallas_call(
        pack_kernel,
        out_shape=jax.ShapeDtypeStruct((devices, lines, LANES), jnp.bfloat16),
        scratch_shapes=[pltpu.VMEM((grads.shape[1] // LANES, LANES), jnp.float32)],
        compiler_params=small(),
    )(grads)


def down_column(row_ref):
    columns = row_ref.shape[1]
    square = (columns, columns)
    same = lax.broadcasted_iota(jnp.int32, square, 0) == lax.broadcasted_iota(jnp.int32, square, 1)
    row = jnp.broadcast_to(row_ref[...].astype(jnp.float32), square)
    return jnp.sum(jnp.where(same, row, 0.0), axis=1, keepdims=True).astype(jnp.int32)


def middle_kernel(
    position_ref, pieces_ref, master_ref, first_ref, second_ref, gradient_ref, copies_ref, flat_ref
):
    devices = pieces_ref.shape[0]
    copies, columns, width = copies_ref.shape
    total = pieces_ref[0].astype(jnp.float32)
    for k in range(1, devices):
        total = total + pieces_ref[k].astype(jnp.float32)
    gradient = total / devices
    gradient_ref[...] = gradient
    flat_ref[...] = adam_step(gradient, master_ref[...], first_ref[...], second_ref[...])[2]
    period = columns // 8
    span = period * LANES
    group = span // columns
    lines = flat_ref.shape[0] // period
    wide = [flat_ref[pl.ds(b, lines, stride=period), :].astype(jnp.bfloat16) for b in range(period)]
    wide = jnp.concatenate(wide, axis=1)
    line = lax.broadcasted_iota(jnp.int32, (lines, width), 0)
    row = lax.broadcasted_iota(jnp.int32, (lines, width), 1)
    repeat = (row // group == line).astype(jnp.bfloat16)
    spread = lax.dot_general(wide, repeat, (((0,), (0,)), ((), ())), preferred_element_type=jnp.float32)
    entry = lax.broadcasted_iota(jnp.int32, (span, width), 0)
    row = lax.broadcasted_iota(jnp.int32, (span, width), 1)
    kept = jnp.where(entry // columns == row % group, spread, 0.0).astype(jnp.bfloat16)
    column = lax.broadcasted_iota(jnp.int32, (columns, span), 1) % columns
    pick = (column == down_column(position_ref)).astype(jnp.bfloat16)
    rows = jnp.dot(pick, kept, preferred_element_type=jnp.float32).astype(jnp.bfloat16)
    for k in range(copies):
        copies_ref[k] = rows


def middle(position, pieces, master, first_moment, second_moment, copies):
    columns = position.shape[0]
    flat = pieces.shape[1:]
    width = flat[0] * LANES // columns
    return pl.pallas_call(
        middle_kernel,
        out_shape=(
            jax.ShapeDtypeStruct(flat, jnp.float32),
            jax.ShapeDtypeStruct((copies, columns, width), jnp.bfloat16),
        ),
        scratch_shapes=[pltpu.VMEM(flat, jnp.float32)],
        compiler_params=small(),
    )(position[None, :], pieces, *(x.reshape(flat) for x in (master, first_moment, second_moment)))


def finish_kernel(position_ref, stepped_ref, own_ref, other_ref, master_ref, copy_ref, scaled_ref, sems):
    core = lax.axis_index("replica")
    chips, columns, width = own_ref.shape
    total = jnp.zeros((columns, width), jnp.float32)
    for ref in (own_ref, other_ref):
        for k in range(chips):
            value = ref[k].astype(jnp.float32)
            total = total + value * value
    factor = lax.rsqrt(jnp.sum(total, axis=1, keepdims=True) / D + norm_epsilon)
    parts = sems.shape[0]
    each = chips // parts
    copies = []
    for p in range(parts):
        for k in range(p * each, (p + 1) * each):
            for ref, place in ((own_ref, core), (other_ref, 1 - core)):
                start = pl.multiple_of((2 * k + place) * width, width)
                scaled_ref[:, pl.ds(start, width)] = (ref[k].astype(jnp.float32) * factor).astype(jnp.bfloat16)
        part = pl.ds(p * 2 * each * width, 2 * each * width)
        copies.append(pltpu.make_async_copy(scaled_ref.at[:, part], copy_ref.at[:, part], sems.at[p]))
        copies[p].start()
    position = down_column(position_ref)
    period = columns // 8
    lane = lax.broadcasted_iota(jnp.int32, (1, LANES), 1)
    line = lax.broadcasted_iota(jnp.int32, stepped_ref.shape, 0) % period
    spread = jnp.zeros(stepped_ref.shape, jnp.float32)
    for p in range(period):
        flat_column = (p * LANES + lane) % columns
        picked = jnp.sum(jnp.where(position == flat_column, factor, 0.0), axis=0, keepdims=True)
        spread = jnp.where(line == p, picked, spread)
    master_ref[...] = stepped_ref[...] * spread
    for copy in copies:
        copy.wait()


def finish_narrow(owners, stepped, blocks):
    columns = owners.shape[0]
    blocks = blocks.astype(jnp.float32)
    factor = lax.rsqrt(jnp.sum(blocks * blocks, axis=(0, 2)) / D + norm_epsilon)
    scaled = jnp.transpose(blocks * factor[None, :, None], (1, 0, 2))
    flat_factor = jnp.zeros((columns,), jnp.float32).at[flat_positions(owners)].set(factor)
    new_master = (stepped.reshape(-1, columns) * flat_factor).reshape(stepped.shape)
    return (new_master, scaled.reshape(columns, -1).astype(jnp.bfloat16))


def spread(value, axes, size):
    return lax.all_to_all(jnp.broadcast_to(value[None], (size,) + value.shape), axes, 0, 0, tiled=True)


def finish(position, stepped, own, other):
    chips, columns, width = own.shape
    wide = (columns, 2 * chips * width)
    parts = 4 if chips % 4 == 0 else 1
    whole = pl.BlockSpec(memory_space=pltpu.VMEM)
    return pl.pallas_call(
        finish_kernel,
        in_specs=[whole] * 4,
        out_specs=(whole, pl.BlockSpec(memory_space=pl.ANY)),
        out_shape=(
            jax.ShapeDtypeStruct(stepped.shape, jnp.float32),
            jax.ShapeDtypeStruct(wide, jnp.bfloat16),
        ),
        scratch_shapes=[pltpu.VMEM(wide, jnp.bfloat16), pltpu.SemaphoreType.DMA((parts,))],
        compiler_params=small(),
    )(position[None, :], stepped, own, other)


def on_device(grads, master, first_moment, second_moment, owners):
    shards, replicas = lax.axis_size("shard"), lax.axis_size("replica")
    devices = shards * replicas
    columns = owners.shape[0]
    pieces = lax.all_to_all(pack(grads, devices), AXES, 0, 0, tiled=True)
    if replicas == 2 and master.shape[0] % (columns * LANES) == 0:
        position = flat_positions(owners)
        gradient, copies = middle(position, pieces, master, first_moment, second_moment, shards)
        new_first, new_second, stepped = adam_step(
            gradient.reshape(-1), master, first_moment, second_moment
        )
        own = lax.all_to_all(copies, "shard", 0, 0, tiled=True)
        other = lax.ppermute(own, "replica", [(0, 1), (1, 0)])
        new_master, model_copy = finish(position, stepped.reshape(-1, LANES), own, other)
        return (new_master.reshape(-1), new_first, new_second, model_copy)
    gradient = jnp.sum(pieces.astype(jnp.float32), axis=0).reshape(-1) / devices
    new_first, new_second, stepped = adam_step(gradient, master, first_moment, second_moment)
    rows = jnp.take(stepped.reshape(-1, columns), flat_positions(owners), axis=1).T.astype(jnp.bfloat16)
    new_master, model_copy = finish_narrow(owners, stepped, spread(rows, AXES, devices))
    return (new_master, new_first, new_second, model_copy)


def solution(mesh):
    placed = (P(AXES, None), P(AXES), P(AXES), P(AXES), P())
    return jax.shard_map(
        on_device,
        mesh=mesh,
        in_specs=placed,
        out_specs=(P(AXES), P(AXES), P(AXES), P()),
        check_vma=False,
    )
```

```python
import functools

import jax
import jax.numpy as jnp
from jax import lax
from jax.experimental import pallas as pl
from jax.experimental.pallas import tpu as pltpu
from jax.sharding import PartitionSpec as P

D = 8192


learning_rate = 0.1
adam_epsilon = 1e-08
norm_epsilon = 1e-06
first_correction = 1.0 - 0.9**20
second_correction = 1.0 - 0.95**20
AXES = ("shard", "replica")
LANES = 128


def adam_step(gradient, master, first_moment, second_moment):
    new_first = 0.9 * first_moment + 0.1 * gradient
    new_second = 0.95 * second_moment + 0.05 * gradient * gradient
    stepped = master - learning_rate * (new_first / first_correction) / (
        jnp.sqrt(new_second / second_correction) + adam_epsilon
    )
    return (new_first, new_second, stepped)


def flat_positions(owners):
    column_ids = jnp.arange(owners.shape[0], dtype=jnp.int32)
    ranked_below = owners[None, :] < owners[:, None]
    same_before = (owners[None, :] == owners[:, None]) & (column_ids[None, :] < column_ids[:, None])
    return jnp.sum((ranked_below | same_before).astype(jnp.int32), axis=1)


def small(**more):
    return pltpu.CompilerParams(vmem_limit_bytes=6 * 2**20, **more)


def pack_kernel(grads_ref, kept_ref, sent_ref, wide_ref):
    chips, lines, lanes = kept_ref.shape
    core = lax.axis_index("replica")
    row_ref = wide_ref.reshape(1, wide_ref.shape[0] * lanes)
    width = 2 * lines * lanes
    for k in range(chips):
        row_ref[:, k * width : (k + 1) * width] = grads_ref[:, k * width : (k + 1) * width].astype(jnp.float32)
        for ref, place in ((kept_ref, core), (sent_ref, 1 - core)):
            start = pl.multiple_of((2 * k + place) * lines, lines)
            ref[k] = wide_ref[pl.ds(start, lines), :].astype(jnp.bfloat16)


def pack(grads, chips, lines):
    packed = jax.ShapeDtypeStruct((chips, lines, LANES), jnp.bfloat16)
    return pl.pallas_call(
        pack_kernel,
        out_shape=(packed, packed),
        scratch_shapes=[pltpu.VMEM((grads.shape[1] // LANES, LANES), jnp.float32)],
        compiler_params=small(),
    )(grads)


def pair_kernel(kept_ref, taken_ref, *refs):
    *held, pairs_ref = refs
    pairs = kept_ref[...].astype(jnp.float32) + taken_ref[...].astype(jnp.float32)
    pairs_ref[...] = pairs.astype(jnp.bfloat16)
    for source, target in zip(held[:4], held[4:]):
        target[...] = source[...]


def add_pairs(kept, taken, position, states):
    flat = jax.ShapeDtypeStruct(kept.shape[1:], jnp.float32)
    position = position[None, :]
    small_shapes = (jax.ShapeDtypeStruct(position.shape, position.dtype), flat, flat, flat)
    return pl.pallas_call(
        pair_kernel,
        out_shape=(*small_shapes, jax.ShapeDtypeStruct(kept.shape, jnp.bfloat16)),
        compiler_params=small(),
    )(kept, taken, position, *(x.reshape(flat.shape) for x in states))


def down_column(row_ref):
    columns = row_ref.shape[1]
    square = (columns, columns)
    same = lax.broadcasted_iota(jnp.int32, square, 0) == lax.broadcasted_iota(jnp.int32, square, 1)
    row = jnp.broadcast_to(row_ref[...].astype(jnp.float32), square)
    return jnp.sum(jnp.where(same, row, 0.0), axis=1, keepdims=True).astype(jnp.int32)


def middle_kernel(
    devices, position_ref, pieces_ref, master_ref, first_ref, second_ref,
    new_first_ref, new_second_ref, stepped_ref, copies_ref,
):
    copies, columns, width = copies_ref.shape
    total = pieces_ref[0].astype(jnp.float32)
    for k in range(1, pieces_ref.shape[0]):
        total = total + pieces_ref[k].astype(jnp.float32)
    gradient = total / devices
    new_first_ref[...], new_second_ref[...], stepped_ref[...] = adam_step(
        gradient, master_ref[...], first_ref[...], second_ref[...]
    )
    period = columns // 8
    span = period * LANES
    group = span // columns
    lines = stepped_ref.shape[0] // period
    wide = [stepped_ref[pl.ds(b, lines, stride=period), :].astype(jnp.bfloat16) for b in range(period)]
    wide = jnp.concatenate(wide, axis=1)
    line = lax.broadcasted_iota(jnp.int32, (lines, width), 0)
    row = lax.broadcasted_iota(jnp.int32, (lines, width), 1)
    repeat = (row // group == line).astype(jnp.bfloat16)
    spread = lax.dot_general(wide, repeat, (((0,), (0,)), ((), ())), preferred_element_type=jnp.float32)
    entry = lax.broadcasted_iota(jnp.int32, (span, width), 0)
    row = lax.broadcasted_iota(jnp.int32, (span, width), 1)
    kept = jnp.where(entry // columns == row % group, spread, 0.0).astype(jnp.bfloat16)
    column = lax.broadcasted_iota(jnp.int32, (columns, span), 1) % columns
    pick = (column == down_column(position_ref)).astype(jnp.bfloat16)
    rows = jnp.dot(pick, kept, preferred_element_type=jnp.float32).astype(jnp.bfloat16)
    for k in range(copies):
        copies_ref[k] = rows


def middle(position, pieces, states, devices):
    columns = position.shape[1]
    flat = jax.ShapeDtypeStruct(pieces.shape[1:], jnp.float32)
    width = flat.size // columns
    return pl.pallas_call(
        functools.partial(middle_kernel, devices),
        out_shape=(flat, flat, flat, jax.ShapeDtypeStruct((pieces.shape[0], columns, width), jnp.bfloat16)),
        compiler_params=small(),
    )(position, pieces, *states)


def finish_kernel(
    position_ref, new_first_ref, new_second_ref, stepped_ref, own_ref, other_ref,
    master_out, first_out, second_out, copy_out, master_ref, scaled_ref, sems,
):
    core = lax.axis_index("replica")
    chips, columns, width = own_ref.shape
    parts = sems.shape[0] - 3
    copies = [
        pltpu.make_async_copy(new_first_ref, first_out, sems.at[0]),
        pltpu.make_async_copy(new_second_ref, second_out, sems.at[1]),
    ]
    for copy in copies:
        copy.start()
    total = jnp.zeros((columns, width), jnp.float32)
    for ref in (own_ref, other_ref):
        for k in range(chips):
            value = ref[k].astype(jnp.float32)
            total = total + value * value
    factor = lax.rsqrt(jnp.sum(total, axis=1, keepdims=True) / D + norm_epsilon)
    position = down_column(position_ref)
    period = columns // 8
    lane = lax.broadcasted_iota(jnp.int32, (1, LANES), 1)
    line = lax.broadcasted_iota(jnp.int32, stepped_ref.shape, 0) % period
    spread = jnp.zeros(stepped_ref.shape, jnp.float32)
    for p in range(period):
        flat_column = (p * LANES + lane) % columns
        picked = jnp.sum(jnp.where(position == flat_column, factor, 0.0), axis=0, keepdims=True)
        spread = jnp.where(line == p, picked, spread)
    master_ref[...] = stepped_ref[...] * spread
    copies.append(pltpu.make_async_copy(master_ref, master_out, sems.at[2]))
    copies[2].start()
    each = chips // parts
    for p in range(parts):
        for k in range(p * each, (p + 1) * each):
            for ref, place in ((own_ref, core), (other_ref, 1 - core)):
                start = pl.multiple_of((2 * k + place) * width, width)
                scaled_ref[:, pl.ds(start, width)] = (ref[k].astype(jnp.float32) * factor).astype(jnp.bfloat16)
        part = pl.ds(p * 2 * each * width, 2 * each * width)
        copies.append(pltpu.make_async_copy(scaled_ref.at[:, part], copy_out.at[:, part], sems.at[3 + p]))
        copies[3 + p].start()
    for copy in copies:
        copy.wait()


def finish(position, new_first, new_second, stepped, own, other):
    chips, columns, width = own.shape
    wide = (columns, 2 * chips * width)
    parts = 4 if chips % 4 == 0 else 1
    flat = jax.ShapeDtypeStruct(stepped.shape, jnp.float32)
    return pl.pallas_call(
        finish_kernel,
        in_specs=[pl.BlockSpec(memory_space=pltpu.VMEM)] * 6,
        out_specs=(pl.BlockSpec(memory_space=pl.ANY),) * 4,
        out_shape=(flat, flat, flat, jax.ShapeDtypeStruct(wide, jnp.bfloat16)),
        scratch_shapes=[
            pltpu.VMEM(stepped.shape, jnp.float32),
            pltpu.VMEM(wide, jnp.bfloat16),
            pltpu.SemaphoreType.DMA((3 + parts,)),
        ],
        compiler_params=small(),
    )(position, new_first, new_second, stepped, own, other)


def finish_narrow(owners, stepped, blocks):
    columns = owners.shape[0]
    blocks = blocks.astype(jnp.float32)
    factor = lax.rsqrt(jnp.sum(blocks * blocks, axis=(0, 2)) / D + norm_epsilon)
    scaled = jnp.transpose(blocks * factor[None, :, None], (1, 0, 2))
    flat_factor = jnp.zeros((columns,), jnp.float32).at[flat_positions(owners)].set(factor)
    new_master = (stepped.reshape(-1, columns) * flat_factor).reshape(stepped.shape)
    return (new_master, scaled.reshape(columns, -1).astype(jnp.bfloat16))


def spread(value, axes, size):
    return lax.all_to_all(jnp.broadcast_to(value[None], (size,) + value.shape), axes, 0, 0, tiled=True)


def on_device(grads, master, first_moment, second_moment, owners):
    shards, replicas = lax.axis_size("shard"), lax.axis_size("replica")
    devices = shards * replicas
    columns = owners.shape[0]
    if replicas == 2 and master.shape[0] // LANES % 48 == 0:
        kept, sent = pack(grads, shards, master.shape[0] // LANES)
        taken = lax.ppermute(sent, "replica", [(0, 1), (1, 0)])
        states = (master, first_moment, second_moment)
        position, *states, pairs = add_pairs(kept, taken, flat_positions(owners), states)
        pieces = lax.all_to_all(pairs, "shard", 0, 0, tiled=True)
        *updated, copies = middle(position, pieces, states, devices)
        own = lax.all_to_all(copies, "shard", 0, 0, tiled=True)
        other = lax.ppermute(own, "replica", [(0, 1), (1, 0)])
        *flat, model_copy = finish(position, *updated, own, other)
        return (*(x.reshape(-1) for x in flat), model_copy)
    pieces = lax.all_to_all(grads.reshape(devices, -1), AXES, 0, 0, tiled=True)
    gradient = jnp.sum(pieces.astype(jnp.float32), axis=0) / devices
    new_first, new_second, stepped = adam_step(gradient, master, first_moment, second_moment)
    rows = jnp.take(stepped.reshape(-1, columns), flat_positions(owners), axis=1).T.astype(jnp.bfloat16)
    new_master, model_copy = finish_narrow(owners, stepped, spread(rows, AXES, devices))
    return (new_master, new_first, new_second, model_copy)


def solution(mesh):
    placed = (P(AXES, None), P(AXES), P(AXES), P(AXES), P())
    return jax.shard_map(
        on_device,
        mesh=mesh,
        in_specs=placed,
        out_specs=(P(AXES), P(AXES), P(AXES), P()),
        check_vma=False,
    )
```

```python
import functools

import jax
import jax.numpy as jnp
from jax import lax
from jax.experimental import pallas as pl
from jax.experimental.pallas import tpu as pltpu
from jax.sharding import PartitionSpec as P

D = 8192


learning_rate = 0.1
adam_epsilon = 1e-08
norm_epsilon = 1e-06
first_correction = 1.0 - 0.9**20
second_correction = 1.0 - 0.95**20
AXES = ("shard", "replica")
HALVES = ("half", "near", "core")
LANES = 128


def adam_step(gradient, master, first_moment, second_moment):
    new_first = 0.9 * first_moment + 0.1 * gradient
    new_second = 0.95 * second_moment + 0.05 * gradient * gradient
    stepped = master - learning_rate * (new_first / first_correction) / (
        jnp.sqrt(new_second / second_correction) + adam_epsilon
    )
    return (new_first, new_second, stepped)


def flat_positions(owners):
    column_ids = jnp.arange(owners.shape[0], dtype=jnp.int32)
    ranked_below = owners[None, :] < owners[:, None]
    same_before = (owners[None, :] == owners[:, None]) & (column_ids[None, :] < column_ids[:, None])
    return jnp.sum((ranked_below | same_before).astype(jnp.int32), axis=1)


def small(**more):
    return pltpu.CompilerParams(vmem_limit_bytes=6 * 2**20, **more)


def pack_kernel(grads_ref, kept_ref, sent_ref, wide_ref):
    near, halves, lines, lanes = kept_ref.shape
    core = lax.axis_index("core")
    row_ref = wide_ref.reshape(1, wide_ref.shape[0] * lanes)
    width = 2 * lines * lanes
    for k in range(near * halves):
        row_ref[:, k * width : (k + 1) * width] = grads_ref[:, k * width : (k + 1) * width].astype(jnp.float32)
        for ref, place in ((kept_ref, core), (sent_ref, 1 - core)):
            start = pl.multiple_of((2 * k + place) * lines, lines)
            ref[k % near, k // near] = wide_ref[pl.ds(start, lines), :].astype(jnp.bfloat16)


def pack(grads, halves, near, lines):
    packed = jax.ShapeDtypeStruct((near, halves, lines, LANES), jnp.bfloat16)
    return pl.pallas_call(
        pack_kernel,
        out_shape=(packed, packed),
        scratch_shapes=[pltpu.VMEM((grads.shape[1] // LANES, LANES), jnp.float32)],
        compiler_params=small(),
    )(grads)


def pair_kernel(kept_ref, taken_ref, position_ref, pairs_ref, position_out):
    pairs = kept_ref[...].astype(jnp.float32) + taken_ref[...].astype(jnp.float32)
    pairs_ref[...] = pairs.astype(jnp.bfloat16)
    position_out[...] = position_ref[...]


def add_pairs(kept, taken, position):
    position = position[None, :]
    return pl.pallas_call(
        pair_kernel,
        out_shape=(
            jax.ShapeDtypeStruct(kept.shape, jnp.bfloat16),
            jax.ShapeDtypeStruct(position.shape, position.dtype),
        ),
        compiler_params=small(),
    )(kept, taken, position)


def partial_kernel(pieces_ref, partial_ref):
    total = pieces_ref[0].astype(jnp.float32)
    for k in range(1, pieces_ref.shape[0]):
        total = total + pieces_ref[k].astype(jnp.float32)
    partial_ref[...] = total.astype(jnp.bfloat16)


def add_pieces(pieces):
    return pl.pallas_call(
        partial_kernel,
        out_shape=jax.ShapeDtypeStruct(pieces.shape[1:], jnp.bfloat16),
        compiler_params=small(),
    )(pieces)


def down_column(row_ref):
    columns = row_ref.shape[1]
    square = (columns, columns)
    same = lax.broadcasted_iota(jnp.int32, square, 0) == lax.broadcasted_iota(jnp.int32, square, 1)
    row = jnp.broadcast_to(row_ref[...].astype(jnp.float32), square)
    return jnp.sum(jnp.where(same, row, 0.0), axis=1, keepdims=True).astype(jnp.int32)


def middle_kernel(
    devices, position_ref, partial_ref, partner_ref, mine_ref, theirs_ref,
    new_first_ref, new_second_ref, stepped_ref, copies_ref, both_ref,
):
    half = lax.axis_index("half")
    copies, halves, columns, width = copies_ref.shape
    lines = stepped_ref.shape[0]
    total = partial_ref[...].astype(jnp.float32) + partner_ref[...].astype(jnp.float32)
    swapped = jnp.concatenate([total[1], total[0]])
    gradient = jnp.where(half == 0, total.reshape(swapped.shape), swapped) / devices
    states = [jnp.concatenate([mine_ref[k], theirs_ref[k]]) for k in range(3)]
    new_first, new_second, stepped = adam_step(gradient, *states)
    new_first_ref[...] = new_first[:lines]
    new_second_ref[...] = new_second[:lines]
    stepped_ref[...] = stepped[:lines]
    both_ref[...] = stepped
    period = columns // 8
    span = period * LANES
    group = span // columns
    groups = halves * lines // period
    wide = [both_ref[pl.ds(b, groups, stride=period), :].astype(jnp.bfloat16) for b in range(period)]
    wide = jnp.concatenate(wide, axis=1)
    line = lax.broadcasted_iota(jnp.int32, (groups, halves * width), 0)
    row = lax.broadcasted_iota(jnp.int32, (groups, halves * width), 1)
    repeat = (row // group == line).astype(jnp.bfloat16)
    spread = lax.dot_general(wide, repeat, (((0,), (0,)), ((), ())), preferred_element_type=jnp.float32)
    entry = lax.broadcasted_iota(jnp.int32, (span, halves * width), 0)
    row = lax.broadcasted_iota(jnp.int32, (span, halves * width), 1)
    kept = jnp.where(entry // columns == row % group, spread, 0.0).astype(jnp.bfloat16)
    column = lax.broadcasted_iota(jnp.int32, (columns, span), 1) % columns
    pick = (column == down_column(position_ref)).astype(jnp.bfloat16)
    rows = jnp.dot(pick, kept, preferred_element_type=jnp.float32).astype(jnp.bfloat16)
    for k in range(copies):
        copies_ref[k, half] = rows[:, :width]
        copies_ref[k, 1 - half] = rows[:, width:]


def middle(position, partial, partner, mine, theirs, near, devices):
    columns = position.shape[1]
    halves, lines, lanes = partial.shape
    flat = jax.ShapeDtypeStruct((lines, lanes), jnp.float32)
    rows = (near, halves, columns, flat.size // columns)
    return pl.pallas_call(
        functools.partial(middle_kernel, devices),
        out_shape=(flat, flat, flat, jax.ShapeDtypeStruct(rows, jnp.bfloat16)),
        scratch_shapes=[pltpu.VMEM((halves * lines, lanes), jnp.float32)],
        compiler_params=small(),
    )(position, partial, partner, mine, theirs)


def finish_kernel(
    position_ref, new_first_ref, new_second_ref, stepped_ref, own_ref, other_ref,
    master_out, first_out, second_out, copy_out, master_ref, scaled_ref, sems,
):
    core = lax.axis_index("core")
    near, halves, columns, width = own_ref.shape
    chips = near * halves
    parts = sems.shape[0] - 3
    copies = [
        pltpu.make_async_copy(new_first_ref, first_out, sems.at[0]),
        pltpu.make_async_copy(new_second_ref, second_out, sems.at[1]),
    ]
    for copy in copies:
        copy.start()
    total = jnp.zeros((columns, width), jnp.float32)
    for ref in (own_ref, other_ref):
        for k in range(chips):
            value = ref[k % near, k // near].astype(jnp.float32)
            total = total + value * value
    factor = lax.rsqrt(jnp.sum(total, axis=1, keepdims=True) / D + norm_epsilon)
    position = down_column(position_ref)
    period = columns // 8
    lane = lax.broadcasted_iota(jnp.int32, (1, LANES), 1)
    line = lax.broadcasted_iota(jnp.int32, stepped_ref.shape, 0) % period
    spread = jnp.zeros(stepped_ref.shape, jnp.float32)
    for p in range(period):
        flat_column = (p * LANES + lane) % columns
        picked = jnp.sum(jnp.where(position == flat_column, factor, 0.0), axis=0, keepdims=True)
        spread = jnp.where(line == p, picked, spread)
    master_ref[...] = stepped_ref[...] * spread
    copies.append(pltpu.make_async_copy(master_ref, master_out, sems.at[2]))
    copies[2].start()
    each = chips // parts
    for p in range(parts):
        for k in range(p * each, (p + 1) * each):
            for ref, place in ((own_ref, core), (other_ref, 1 - core)):
                start = pl.multiple_of((2 * k + place) * width, width)
                scaled = ref[k % near, k // near].astype(jnp.float32) * factor
                scaled_ref[:, pl.ds(start, width)] = scaled.astype(jnp.bfloat16)
        part = pl.ds(p * 2 * each * width, 2 * each * width)
        copies.append(pltpu.make_async_copy(scaled_ref.at[:, part], copy_out.at[:, part], sems.at[3 + p]))
        copies[3 + p].start()
    for copy in copies:
        copy.wait()


def finish(position, new_first, new_second, stepped, own, other):
    near, halves, columns, width = own.shape
    chips = near * halves
    wide = (columns, 2 * chips * width)
    parts = 4 if chips % 4 == 0 else 1
    flat = jax.ShapeDtypeStruct(stepped.shape, jnp.float32)
    return pl.pallas_call(
        finish_kernel,
        in_specs=[pl.BlockSpec(memory_space=pltpu.VMEM)] * 6,
        out_specs=(pl.BlockSpec(memory_space=pl.ANY),) * 4,
        out_shape=(flat, flat, flat, jax.ShapeDtypeStruct(wide, jnp.bfloat16)),
        scratch_shapes=[
            pltpu.VMEM(stepped.shape, jnp.float32),
            pltpu.VMEM(wide, jnp.bfloat16),
            pltpu.SemaphoreType.DMA((3 + parts,)),
        ],
        compiler_params=small(),
    )(position, new_first, new_second, stepped, own, other)


def finish_narrow(owners, stepped, blocks):
    columns = owners.shape[0]
    blocks = blocks.astype(jnp.float32)
    factor = lax.rsqrt(jnp.sum(blocks * blocks, axis=(0, 2)) / D + norm_epsilon)
    scaled = jnp.transpose(blocks * factor[None, :, None], (1, 0, 2))
    flat_factor = jnp.zeros((columns,), jnp.float32).at[flat_positions(owners)].set(factor)
    new_master = (stepped.reshape(-1, columns) * flat_factor).reshape(stepped.shape)
    return (new_master, scaled.reshape(columns, -1).astype(jnp.bfloat16))


def spread(value, axes, size):
    return lax.all_to_all(jnp.broadcast_to(value[None], (size,) + value.shape), axes, 0, 0, tiled=True)


def on_halves(grads, master, first_moment, second_moment, owners):
    halves, near, cores = (lax.axis_size(axis) for axis in HALVES)
    swap = [(0, 1), (1, 0)]
    kept, sent = pack(grads, halves, near, master.shape[0] // LANES)
    mine = jnp.stack([x.reshape(-1, LANES) for x in (master, first_moment, second_moment)])
    taken = lax.ppermute(sent, "core", swap)
    theirs = lax.ppermute(mine, "half", swap)
    pairs, position = add_pairs(kept, taken, flat_positions(owners))
    partial = add_pieces(lax.all_to_all(pairs, "near", 0, 0, tiled=True))
    partner = lax.ppermute(partial, "half", swap)
    *updated, copies = middle(position, partial, partner, mine, theirs, near, halves * near * cores)
    own = lax.all_to_all(copies, "near", 0, 0, tiled=True)
    other = lax.ppermute(own, "core", swap)
    *flat, model_copy = finish(position, *updated, own, other)
    return (*(x.reshape(-1) for x in flat), model_copy)


def on_device(grads, master, first_moment, second_moment, owners):
    devices = lax.axis_size(AXES)
    columns = owners.shape[0]
    pieces = lax.all_to_all(grads.reshape(devices, -1), AXES, 0, 0, tiled=True)
    gradient = jnp.sum(pieces.astype(jnp.float32), axis=0) / devices
    new_first, new_second, stepped = adam_step(gradient, master, first_moment, second_moment)
    rows = jnp.take(stepped.reshape(-1, columns), flat_positions(owners), axis=1).T.astype(jnp.bfloat16)
    new_master, model_copy = finish_narrow(owners, stepped, spread(rows, AXES, devices))
    return (new_master, new_first, new_second, model_copy)


def solution(mesh):
    body, axes = on_device, AXES
    if mesh.shape["replica"] == 2 and mesh.shape["shard"] % 4 == 0:
        body, axes = on_halves, HALVES
        mesh = jax.sharding.Mesh(mesh.devices.reshape(2, -1, 2), HALVES)
    placed = (P(axes, None), P(axes), P(axes), P(axes), P())
    return jax.shard_map(
        body,
        mesh=mesh,
        in_specs=placed,
        out_specs=(P(axes), P(axes), P(axes), P()),
        check_vma=False,
    )
```

```python
import functools

import jax
import jax.numpy as jnp
from jax import lax
from jax.experimental import pallas as pl
from jax.experimental.pallas import tpu as pltpu
from jax.sharding import PartitionSpec as P

D = 8192


learning_rate = 0.1
adam_epsilon = 1e-08
norm_epsilon = 1e-06
first_correction = 1.0 - 0.9**20
second_correction = 1.0 - 0.95**20
AXES = ("shard", "replica")
HALVES = ("half", "near", "core")
LANES = 128


def adam_step(gradient, master, first_moment, second_moment):
    new_first = 0.9 * first_moment + 0.1 * gradient
    new_second = 0.95 * second_moment + 0.05 * gradient * gradient
    stepped = master - learning_rate * (new_first / first_correction) / (
        jnp.sqrt(new_second / second_correction) + adam_epsilon
    )
    return (new_first, new_second, stepped)


def flat_positions(owners):
    column_ids = jnp.arange(owners.shape[0], dtype=jnp.int32)
    ranked_below = owners[None, :] < owners[:, None]
    same_before = (owners[None, :] == owners[:, None]) & (column_ids[None, :] < column_ids[:, None])
    return jnp.sum((ranked_below | same_before).astype(jnp.int32), axis=1)


def small(**more):
    return pltpu.CompilerParams(vmem_limit_bytes=6 * 2**20, **more)


def pack_kernel(grads_ref, kept_ref, sent_ref, wide_ref):
    near, halves, lines, lanes = kept_ref.shape
    core = lax.axis_index("core")
    row_ref = wide_ref.reshape(1, wide_ref.shape[0] * lanes)
    width = 2 * lines * lanes
    for k in range(near * halves):
        row_ref[:, k * width : (k + 1) * width] = grads_ref[:, k * width : (k + 1) * width].astype(jnp.float32)
        for ref, place in ((kept_ref, core), (sent_ref, 1 - core)):
            start = pl.multiple_of((2 * k + place) * lines, lines)
            ref[k % near, k // near] = wide_ref[pl.ds(start, lines), :].astype(jnp.bfloat16)


def pack(grads, halves, near, lines):
    packed = jax.ShapeDtypeStruct((near, halves, lines, LANES), jnp.bfloat16)
    return pl.pallas_call(
        pack_kernel,
        out_shape=(packed, packed),
        scratch_shapes=[pltpu.VMEM((grads.shape[1] // LANES, LANES), jnp.float32)],
        compiler_params=small(),
    )(grads)


def pair_kernel(kept_ref, taken_ref, *refs):
    *held, pairs_ref = refs
    pairs = kept_ref[...].astype(jnp.float32) + taken_ref[...].astype(jnp.float32)
    pairs_ref[...] = pairs.astype(jnp.bfloat16)
    for source, target in zip(held[:4], held[4:]):
        target[...] = source[...]


def add_pairs(kept, taken, position, states):
    flat = jax.ShapeDtypeStruct(kept.shape[2:], jnp.float32)
    position = position[None, :]
    small_shapes = (jax.ShapeDtypeStruct(position.shape, position.dtype), flat, flat, flat)
    return pl.pallas_call(
        pair_kernel,
        out_shape=(*small_shapes, jax.ShapeDtypeStruct(kept.shape, jnp.bfloat16)),
        compiler_params=small(),
    )(kept, taken, position, *(x.reshape(flat.shape) for x in states))


def partial_kernel(pieces_ref, kept_ref, sent_ref):
    half = lax.axis_index("half")
    for ref, place in ((kept_ref, half), (sent_ref, 1 - half)):
        total = pieces_ref[0, place].astype(jnp.float32)
        for k in range(1, pieces_ref.shape[0]):
            total = total + pieces_ref[k, place].astype(jnp.float32)
        ref[...] = total.astype(ref.dtype)


def add_pieces(pieces):
    shape = pieces.shape[2:]
    return pl.pallas_call(
        partial_kernel,
        out_shape=(jax.ShapeDtypeStruct(shape, jnp.float32), jax.ShapeDtypeStruct(shape, jnp.bfloat16)),
        compiler_params=small(),
    )(pieces)


def down_column(row_ref):
    columns = row_ref.shape[1]
    square = (columns, columns)
    same = lax.broadcasted_iota(jnp.int32, square, 0) == lax.broadcasted_iota(jnp.int32, square, 1)
    row = jnp.broadcast_to(row_ref[...].astype(jnp.float32), square)
    return jnp.sum(jnp.where(same, row, 0.0), axis=1, keepdims=True).astype(jnp.int32)


def middle_kernel(
    devices, position_ref, partial_ref, partner_ref, master_ref, first_ref, second_ref,
    new_first_ref, new_second_ref, stepped_ref, rows_ref,
):
    columns, width = rows_ref.shape
    gradient = (partial_ref[...] + partner_ref[...].astype(jnp.float32)) / devices
    new_first_ref[...], new_second_ref[...], stepped_ref[...] = adam_step(
        gradient, master_ref[...], first_ref[...], second_ref[...]
    )
    period = columns // 8
    span = period * LANES
    group = span // columns
    groups = stepped_ref.shape[0] // period
    wide = [stepped_ref[pl.ds(b, groups, stride=period), :].astype(jnp.bfloat16) for b in range(period)]
    wide = jnp.concatenate(wide, axis=1)
    line = lax.broadcasted_iota(jnp.int32, (groups, width), 0)
    row = lax.broadcasted_iota(jnp.int32, (groups, width), 1)
    repeat = (row // group == line).astype(jnp.bfloat16)
    spread = lax.dot_general(wide, repeat, (((0,), (0,)), ((), ())), preferred_element_type=jnp.float32)
    entry = lax.broadcasted_iota(jnp.int32, (span, width), 0)
    row = lax.broadcasted_iota(jnp.int32, (span, width), 1)
    kept = jnp.where(entry // columns == row % group, spread, 0.0).astype(jnp.bfloat16)
    column = lax.broadcasted_iota(jnp.int32, (columns, span), 1) % columns
    pick = (column == down_column(position_ref)).astype(jnp.bfloat16)
    rows_ref[...] = jnp.dot(pick, kept, preferred_element_type=jnp.float32).astype(jnp.bfloat16)


def middle(position, partial, partner, states, devices):
    columns = position.shape[1]
    flat = jax.ShapeDtypeStruct(partial.shape, jnp.float32)
    rows = jax.ShapeDtypeStruct((columns, flat.size // columns), jnp.bfloat16)
    return pl.pallas_call(
        functools.partial(middle_kernel, devices),
        out_shape=(flat, flat, flat, rows),
        compiler_params=small(),
    )(position, partial, partner, *states)


def copies_kernel(mine_ref, theirs_ref, copies_ref):
    half = lax.axis_index("half")
    for k in range(copies_ref.shape[0]):
        copies_ref[k, half] = mine_ref[...]
        copies_ref[k, 1 - half] = theirs_ref[...]


def both_halves(mine, theirs, near):
    return pl.pallas_call(
        copies_kernel,
        out_shape=jax.ShapeDtypeStruct((near, 2, *mine.shape), mine.dtype),
        compiler_params=small(),
    )(mine, theirs)


def finish_kernel(
    position_ref, new_first_ref, new_second_ref, stepped_ref, own_ref, other_ref,
    master_out, first_out, second_out, copy_out, master_ref, scaled_ref, sems,
):
    core = lax.axis_index("core")
    near, halves, columns, width = own_ref.shape
    chips = near * halves
    parts = sems.shape[0] - 3
    copies = [
        pltpu.make_async_copy(new_first_ref, first_out, sems.at[0]),
        pltpu.make_async_copy(new_second_ref, second_out, sems.at[1]),
    ]
    for copy in copies:
        copy.start()
    total = jnp.zeros((columns, width), jnp.float32)
    for ref in (own_ref, other_ref):
        for k in range(chips):
            value = ref[k % near, k // near].astype(jnp.float32)
            total = total + value * value
    factor = lax.rsqrt(jnp.sum(total, axis=1, keepdims=True) / D + norm_epsilon)
    position = down_column(position_ref)
    period = columns // 8
    lane = lax.broadcasted_iota(jnp.int32, (1, LANES), 1)
    line = lax.broadcasted_iota(jnp.int32, stepped_ref.shape, 0) % period
    spread = jnp.zeros(stepped_ref.shape, jnp.float32)
    for p in range(period):
        flat_column = (p * LANES + lane) % columns
        picked = jnp.sum(jnp.where(position == flat_column, factor, 0.0), axis=0, keepdims=True)
        spread = jnp.where(line == p, picked, spread)
    master_ref[...] = stepped_ref[...] * spread
    copies.append(pltpu.make_async_copy(master_ref, master_out, sems.at[2]))
    copies[2].start()
    each = chips // parts
    for p in range(parts):
        for k in range(p * each, (p + 1) * each):
            for ref, place in ((own_ref, core), (other_ref, 1 - core)):
                start = pl.multiple_of((2 * k + place) * width, width)
                scaled = ref[k % near, k // near].astype(jnp.float32) * factor
                scaled_ref[:, pl.ds(start, width)] = scaled.astype(jnp.bfloat16)
        part = pl.ds(p * 2 * each * width, 2 * each * width)
        copies.append(pltpu.make_async_copy(scaled_ref.at[:, part], copy_out.at[:, part], sems.at[3 + p]))
        copies[3 + p].start()
    for copy in copies:
        copy.wait()


def finish(position, new_first, new_second, stepped, own, other):
    near, halves, columns, width = own.shape
    chips = near * halves
    wide = (columns, 2 * chips * width)
    parts = 4 if chips % 4 == 0 else 1
    flat = jax.ShapeDtypeStruct(stepped.shape, jnp.float32)
    return pl.pallas_call(
        finish_kernel,
        in_specs=[pl.BlockSpec(memory_space=pltpu.VMEM)] * 6,
        out_specs=(pl.BlockSpec(memory_space=pl.ANY),) * 4,
        out_shape=(flat, flat, flat, jax.ShapeDtypeStruct(wide, jnp.bfloat16)),
        scratch_shapes=[
            pltpu.VMEM(stepped.shape, jnp.float32),
            pltpu.VMEM(wide, jnp.bfloat16),
            pltpu.SemaphoreType.DMA((3 + parts,)),
        ],
        compiler_params=small(),
    )(position, new_first, new_second, stepped, own, other)


def finish_narrow(owners, stepped, blocks):
    columns = owners.shape[0]
    blocks = blocks.astype(jnp.float32)
    factor = lax.rsqrt(jnp.sum(blocks * blocks, axis=(0, 2)) / D + norm_epsilon)
    scaled = jnp.transpose(blocks * factor[None, :, None], (1, 0, 2))
    flat_factor = jnp.zeros((columns,), jnp.float32).at[flat_positions(owners)].set(factor)
    new_master = (stepped.reshape(-1, columns) * flat_factor).reshape(stepped.shape)
    return (new_master, scaled.reshape(columns, -1).astype(jnp.bfloat16))


def spread(value, axes, size):
    return lax.all_to_all(jnp.broadcast_to(value[None], (size,) + value.shape), axes, 0, 0, tiled=True)


def on_halves(grads, master, first_moment, second_moment, owners):
    halves, near, cores = (lax.axis_size(axis) for axis in HALVES)
    swap = [(0, 1), (1, 0)]
    kept, sent = pack(grads, halves, near, master.shape[0] // LANES)
    taken = lax.ppermute(sent, "core", swap)
    states = (master, first_moment, second_moment)
    position, *states, pairs = add_pairs(kept, taken, flat_positions(owners), states)
    kept, sent = add_pieces(lax.all_to_all(pairs, "near", 0, 0, tiled=True))
    taken = lax.ppermute(sent, "half", swap)
    *updated, rows = middle(position, kept, taken, states, halves * near * cores)
    copies = both_halves(rows, lax.ppermute(rows, "half", swap), near)
    own = lax.all_to_all(copies, "near", 0, 0, tiled=True)
    other = lax.ppermute(own, "core", swap)
    *flat, model_copy = finish(position, *updated, own, other)
    return (*(x.reshape(-1) for x in flat), model_copy)


def on_device(grads, master, first_moment, second_moment, owners):
    devices = lax.axis_size(AXES)
    columns = owners.shape[0]
    pieces = lax.all_to_all(grads.reshape(devices, -1), AXES, 0, 0, tiled=True)
    gradient = jnp.sum(pieces.astype(jnp.float32), axis=0) / devices
    new_first, new_second, stepped = adam_step(gradient, master, first_moment, second_moment)
    rows = jnp.take(stepped.reshape(-1, columns), flat_positions(owners), axis=1).T.astype(jnp.bfloat16)
    new_master, model_copy = finish_narrow(owners, stepped, spread(rows, AXES, devices))
    return (new_master, new_first, new_second, model_copy)


def solution(mesh):
    body, axes = on_device, AXES
    if mesh.shape["replica"] == 2 and mesh.shape["shard"] % 4 == 0:
        body, axes = on_halves, HALVES
        mesh = jax.sharding.Mesh(mesh.devices.reshape(2, -1, 2), HALVES)
    placed = (P(axes, None), P(axes), P(axes), P(axes), P())
    return jax.shard_map(
        body,
        mesh=mesh,
        in_specs=placed,
        out_specs=(P(axes), P(axes), P(axes), P()),
        check_vma=False,
    )
```

```python
import functools

import jax
import jax.numpy as jnp
from jax import lax
from jax.experimental import pallas as pl
from jax.experimental.pallas import tpu as pltpu
from jax.sharding import PartitionSpec as P

D = 8192


learning_rate = 0.1
adam_epsilon = 1e-08
norm_epsilon = 1e-06
first_correction = 1.0 - 0.9**20
second_correction = 1.0 - 0.95**20
AXES = ("shard", "replica")
LANES = 128


def adam_step(gradient, master, first_moment, second_moment):
    new_first = 0.9 * first_moment + 0.1 * gradient
    new_second = 0.95 * second_moment + 0.05 * gradient * gradient
    stepped = master - learning_rate * (new_first / first_correction) / (
        jnp.sqrt(new_second / second_correction) + adam_epsilon
    )
    return (new_first, new_second, stepped)


def flat_positions(owners):
    column_ids = jnp.arange(owners.shape[0], dtype=jnp.int32)
    ranked_below = owners[None, :] < owners[:, None]
    same_before = (owners[None, :] == owners[:, None]) & (column_ids[None, :] < column_ids[:, None])
    return jnp.sum((ranked_below | same_before).astype(jnp.int32), axis=1)


def small(**more):
    return pltpu.CompilerParams(vmem_limit_bytes=6 * 2**20, **more)


def pack_kernel(kept, grads_ref, packed_ref, long_ref, wide_ref, sems):
    chips, lines, lanes = packed_ref.shape
    core = lax.axis_index("replica")
    place = core if kept else 1 - core
    width = lines * lanes
    copies = []
    for k in range(chips):
        start = pl.multiple_of((2 * k + place) * width, width)
        source = grads_ref.at[:, pl.ds(start, width)]
        copies.append(pltpu.make_async_copy(source, long_ref.at[k], sems.at[k]))
        copies[k].start()
    row_ref = wide_ref.reshape(1, chips * width)
    for k in range(chips):
        copies[k].wait()
        row_ref[:, k * width : (k + 1) * width] = long_ref[k].astype(jnp.float32)
        packed_ref[k] = wide_ref[k * lines : (k + 1) * lines].astype(jnp.bfloat16)


def pack(kept, grads, chips, lines):
    return pl.pallas_call(
        functools.partial(pack_kernel, kept),
        in_specs=[pl.BlockSpec(memory_space=pl.ANY)],
        out_shape=jax.ShapeDtypeStruct((chips, lines, LANES), jnp.bfloat16),
        scratch_shapes=[
            pltpu.VMEM((chips, 1, lines * LANES), jnp.bfloat16),
            pltpu.VMEM((chips * lines, LANES), jnp.float32),
            pltpu.SemaphoreType.DMA((chips,)),
        ],
        compiler_params=pltpu.CompilerParams(vmem_limit_bytes=54736 * 2**10),
        cost_estimate=pl.CostEstimate(flops=0, bytes_accessed=2 * grads.size, transcendentals=0),
    )(grads)


def pair_kernel(kept_ref, taken_ref, *refs):
    *held, pairs_ref = refs
    pairs = kept_ref[...].astype(jnp.float32) + taken_ref[...].astype(jnp.float32)
    pairs_ref[...] = pairs.astype(jnp.bfloat16)
    for source, target in zip(held[:4], held[4:]):
        target[...] = source[...]


def add_pairs(kept, taken, position, states):
    flat = jax.ShapeDtypeStruct(kept.shape[1:], jnp.float32)
    position = position[None, :]
    small_shapes = (jax.ShapeDtypeStruct(position.shape, position.dtype), flat, flat, flat)
    return pl.pallas_call(
        pair_kernel,
        out_shape=(*small_shapes, jax.ShapeDtypeStruct(kept.shape, jnp.bfloat16)),
        compiler_params=small(),
    )(kept, taken, position, *(x.reshape(flat.shape) for x in states))


def down_column(row_ref):
    columns = row_ref.shape[1]
    square = (columns, columns)
    same = lax.broadcasted_iota(jnp.int32, square, 0) == lax.broadcasted_iota(jnp.int32, square, 1)
    row = jnp.broadcast_to(row_ref[...].astype(jnp.float32), square)
    return jnp.sum(jnp.where(same, row, 0.0), axis=1, keepdims=True).astype(jnp.int32)


def middle_kernel(
    devices, position_ref, pieces_ref, master_ref, first_ref, second_ref,
    new_first_ref, new_second_ref, stepped_ref, copies_ref,
):
    copies, columns, width = copies_ref.shape
    total = pieces_ref[0].astype(jnp.float32)
    for k in range(1, pieces_ref.shape[0]):
        total = total + pieces_ref[k].astype(jnp.float32)
    gradient = total / devices
    new_first_ref[...], new_second_ref[...], stepped_ref[...] = adam_step(
        gradient, master_ref[...], first_ref[...], second_ref[...]
    )
    period = columns // 8
    span = period * LANES
    group = span // columns
    lines = stepped_ref.shape[0] // period
    wide = [stepped_ref[pl.ds(b, lines, stride=period), :].astype(jnp.bfloat16) for b in range(period)]
    wide = jnp.concatenate(wide, axis=1)
    line = lax.broadcasted_iota(jnp.int32, (lines, width), 0)
    row = lax.broadcasted_iota(jnp.int32, (lines, width), 1)
    repeat = (row // group == line).astype(jnp.bfloat16)
    spread = lax.dot_general(wide, repeat, (((0,), (0,)), ((), ())), preferred_element_type=jnp.float32)
    entry = lax.broadcasted_iota(jnp.int32, (span, width), 0)
    row = lax.broadcasted_iota(jnp.int32, (span, width), 1)
    kept = jnp.where(entry // columns == row % group, spread, 0.0).astype(jnp.bfloat16)
    column = lax.broadcasted_iota(jnp.int32, (columns, span), 1) % columns
    pick = (column == down_column(position_ref)).astype(jnp.bfloat16)
    rows = jnp.dot(pick, kept, preferred_element_type=jnp.float32).astype(jnp.bfloat16)
    for k in range(copies):
        copies_ref[k] = rows


def middle(position, pieces, states, devices):
    columns = position.shape[1]
    flat = jax.ShapeDtypeStruct(pieces.shape[1:], jnp.float32)
    width = flat.size // columns
    return pl.pallas_call(
        functools.partial(middle_kernel, devices),
        out_shape=(flat, flat, flat, jax.ShapeDtypeStruct((pieces.shape[0], columns, width), jnp.bfloat16)),
        compiler_params=small(),
    )(position, pieces, *states)


def finish_kernel(
    position_ref, new_first_ref, new_second_ref, stepped_ref, own_ref, other_ref,
    master_out, first_out, second_out, copy_out, master_ref, scaled_ref, sems,
):
    core = lax.axis_index("replica")
    chips, columns, width = own_ref.shape
    parts = sems.shape[0] - 3
    copies = [
        pltpu.make_async_copy(new_first_ref, first_out, sems.at[0]),
        pltpu.make_async_copy(new_second_ref, second_out, sems.at[1]),
    ]
    for copy in copies:
        copy.start()
    total = jnp.zeros((columns, width), jnp.float32)
    for ref in (own_ref, other_ref):
        for k in range(chips):
            value = ref[k].astype(jnp.float32)
            total = total + value * value
    factor = lax.rsqrt(jnp.sum(total, axis=1, keepdims=True) / D + norm_epsilon)
    position = down_column(position_ref)
    period = columns // 8
    lane = lax.broadcasted_iota(jnp.int32, (1, LANES), 1)
    line = lax.broadcasted_iota(jnp.int32, stepped_ref.shape, 0) % period
    spread = jnp.zeros(stepped_ref.shape, jnp.float32)
    for p in range(period):
        flat_column = (p * LANES + lane) % columns
        picked = jnp.sum(jnp.where(position == flat_column, factor, 0.0), axis=0, keepdims=True)
        spread = jnp.where(line == p, picked, spread)
    master_ref[...] = stepped_ref[...] * spread
    copies.append(pltpu.make_async_copy(master_ref, master_out, sems.at[2]))
    copies[2].start()
    each = chips // parts
    for p in range(parts):
        for k in range(p * each, (p + 1) * each):
            for ref, place in ((own_ref, core), (other_ref, 1 - core)):
                start = pl.multiple_of((2 * k + place) * width, width)
                scaled_ref[:, pl.ds(start, width)] = (ref[k].astype(jnp.float32) * factor).astype(jnp.bfloat16)
        part = pl.ds(p * 2 * each * width, 2 * each * width)
        copies.append(pltpu.make_async_copy(scaled_ref.at[:, part], copy_out.at[:, part], sems.at[3 + p]))
        copies[3 + p].start()
    for copy in copies:
        copy.wait()


def finish(position, new_first, new_second, stepped, own, other):
    chips, columns, width = own.shape
    wide = (columns, 2 * chips * width)
    parts = 4 if chips % 4 == 0 else 1
    flat = jax.ShapeDtypeStruct(stepped.shape, jnp.float32)
    return pl.pallas_call(
        finish_kernel,
        in_specs=[pl.BlockSpec(memory_space=pltpu.VMEM)] * 6,
        out_specs=(pl.BlockSpec(memory_space=pl.ANY),) * 4,
        out_shape=(flat, flat, flat, jax.ShapeDtypeStruct(wide, jnp.bfloat16)),
        scratch_shapes=[
            pltpu.VMEM(stepped.shape, jnp.float32),
            pltpu.VMEM(wide, jnp.bfloat16),
            pltpu.SemaphoreType.DMA((3 + parts,)),
        ],
        compiler_params=small(),
    )(position, new_first, new_second, stepped, own, other)


def finish_narrow(owners, stepped, blocks):
    columns = owners.shape[0]
    blocks = blocks.astype(jnp.float32)
    factor = lax.rsqrt(jnp.sum(blocks * blocks, axis=(0, 2)) / D + norm_epsilon)
    scaled = jnp.transpose(blocks * factor[None, :, None], (1, 0, 2))
    flat_factor = jnp.zeros((columns,), jnp.float32).at[flat_positions(owners)].set(factor)
    new_master = (stepped.reshape(-1, columns) * flat_factor).reshape(stepped.shape)
    return (new_master, scaled.reshape(columns, -1).astype(jnp.bfloat16))


def spread(value, axes, size):
    return lax.all_to_all(jnp.broadcast_to(value[None], (size,) + value.shape), axes, 0, 0, tiled=True)


def on_device(grads, master, first_moment, second_moment, owners):
    shards, replicas = lax.axis_size("shard"), lax.axis_size("replica")
    devices = shards * replicas
    columns = owners.shape[0]
    if replicas == 2 and master.shape[0] // LANES % 48 == 0:
        lines = master.shape[0] // LANES
        taken = lax.ppermute(pack(False, grads, shards, lines), "replica", [(0, 1), (1, 0)])
        kept = pack(True, grads, shards, lines)
        states = (master, first_moment, second_moment)
        position, *states, pairs = add_pairs(kept, taken, flat_positions(owners), states)
        pieces = lax.all_to_all(pairs, "shard", 0, 0, tiled=True)
        *updated, copies = middle(position, pieces, states, devices)
        own = lax.all_to_all(copies, "shard", 0, 0, tiled=True)
        other = lax.ppermute(own, "replica", [(0, 1), (1, 0)])
        *flat, model_copy = finish(position, *updated, own, other)
        return (*(x.reshape(-1) for x in flat), model_copy)
    pieces = lax.all_to_all(grads.reshape(devices, -1), AXES, 0, 0, tiled=True)
    gradient = jnp.sum(pieces.astype(jnp.float32), axis=0) / devices
    new_first, new_second, stepped = adam_step(gradient, master, first_moment, second_moment)
    rows = jnp.take(stepped.reshape(-1, columns), flat_positions(owners), axis=1).T.astype(jnp.bfloat16)
    new_master, model_copy = finish_narrow(owners, stepped, spread(rows, AXES, devices))
    return (new_master, new_first, new_second, model_copy)


def solution(mesh):
    placed = (P(AXES, None), P(AXES), P(AXES), P(AXES), P())
    return jax.shard_map(
        on_device,
        mesh=mesh,
        in_specs=placed,
        out_specs=(P(AXES), P(AXES), P(AXES), P()),
        check_vma=False,
    )
```

```python
import functools

import jax
import jax.numpy as jnp
from jax import lax
from jax.experimental import pallas as pl
from jax.experimental.pallas import tpu as pltpu
from jax.sharding import PartitionSpec as P

D = 8192


learning_rate = 0.1
adam_epsilon = 1e-08
norm_epsilon = 1e-06
first_correction = 1.0 - 0.9**20
second_correction = 1.0 - 0.95**20
AXES = ("shard", "replica")
LAYERS = ("layer", "plane", "core")
PLANE = 4
LANES = 128


def adam_step(gradient, master, first_moment, second_moment):
    new_first = 0.9 * first_moment + 0.1 * gradient
    new_second = 0.95 * second_moment + 0.05 * gradient * gradient
    stepped = master - learning_rate * (new_first / first_correction) / (
        jnp.sqrt(new_second / second_correction) + adam_epsilon
    )
    return (new_first, new_second, stepped)


def flat_positions(owners):
    column_ids = jnp.arange(owners.shape[0], dtype=jnp.int32)
    ranked_below = owners[None, :] < owners[:, None]
    same_before = (owners[None, :] == owners[:, None]) & (column_ids[None, :] < column_ids[:, None])
    return jnp.sum((ranked_below | same_before).astype(jnp.int32), axis=1)


def small(**more):
    return pltpu.CompilerParams(vmem_limit_bytes=6 * 2**20, **more)


def slot(chip, chips):
    return chip % PLANE * (chips // PLANE) + chip // PLANE


def pack_kernel(grads_ref, kept_ref, sent_ref, wide_ref):
    chips, lines, lanes = kept_ref.shape
    core = lax.axis_index("core")
    row_ref = wide_ref.reshape(1, wide_ref.shape[0] * lanes)
    width = 2 * lines * lanes
    for k in range(chips):
        row_ref[:, k * width : (k + 1) * width] = grads_ref[:, k * width : (k + 1) * width].astype(jnp.float32)
        for ref, place in ((kept_ref, core), (sent_ref, 1 - core)):
            start = pl.multiple_of((2 * k + place) * lines, lines)
            ref[slot(k, chips)] = wide_ref[pl.ds(start, lines), :].astype(jnp.bfloat16)


def pack(grads, chips, lines):
    packed = jax.ShapeDtypeStruct((chips, lines, LANES), jnp.bfloat16)
    return pl.pallas_call(
        pack_kernel,
        out_shape=(packed, packed),
        scratch_shapes=[pltpu.VMEM((grads.shape[1] // LANES, LANES), jnp.float32)],
        compiler_params=small(),
    )(grads)


def pair_kernel(kept_ref, taken_ref, *refs):
    *held, pairs_ref = refs
    pairs = kept_ref[...].astype(jnp.float32) + taken_ref[...].astype(jnp.float32)
    pairs_ref[...] = pairs.astype(jnp.bfloat16)
    for source, target in zip(held[:4], held[4:]):
        target[...] = source[...]


def add_pairs(kept, taken, position, states):
    flat = jax.ShapeDtypeStruct(kept.shape[1:], jnp.float32)
    position = position[None, :]
    small_shapes = (jax.ShapeDtypeStruct(position.shape, position.dtype), flat, flat, flat)
    return pl.pallas_call(
        pair_kernel,
        out_shape=(*small_shapes, jax.ShapeDtypeStruct(kept.shape, jnp.bfloat16)),
        compiler_params=small(),
    )(kept, taken, position, *(x.reshape(flat.shape) for x in states))


def down_column(row_ref):
    columns = row_ref.shape[1]
    square = (columns, columns)
    same = lax.broadcasted_iota(jnp.int32, square, 0) == lax.broadcasted_iota(jnp.int32, square, 1)
    row = jnp.broadcast_to(row_ref[...].astype(jnp.float32), square)
    return jnp.sum(jnp.where(same, row, 0.0), axis=1, keepdims=True).astype(jnp.int32)


def middle_kernel(
    devices, position_ref, pieces_ref, master_ref, first_ref, second_ref,
    new_first_ref, new_second_ref, stepped_ref, copies_ref,
):
    copies, columns, width = copies_ref.shape
    total = pieces_ref[0].astype(jnp.float32)
    for k in range(1, pieces_ref.shape[0]):
        total = total + pieces_ref[k].astype(jnp.float32)
    gradient = total / devices
    new_first_ref[...], new_second_ref[...], stepped_ref[...] = adam_step(
        gradient, master_ref[...], first_ref[...], second_ref[...]
    )
    period = columns // 8
    span = period * LANES
    group = span // columns
    lines = stepped_ref.shape[0] // period
    wide = [stepped_ref[pl.ds(b, lines, stride=period), :].astype(jnp.bfloat16) for b in range(period)]
    wide = jnp.concatenate(wide, axis=1)
    line = lax.broadcasted_iota(jnp.int32, (lines, width), 0)
    row = lax.broadcasted_iota(jnp.int32, (lines, width), 1)
    repeat = (row // group == line).astype(jnp.bfloat16)
    spread = lax.dot_general(wide, repeat, (((0,), (0,)), ((), ())), preferred_element_type=jnp.float32)
    entry = lax.broadcasted_iota(jnp.int32, (span, width), 0)
    row = lax.broadcasted_iota(jnp.int32, (span, width), 1)
    kept = jnp.where(entry // columns == row % group, spread, 0.0).astype(jnp.bfloat16)
    column = lax.broadcasted_iota(jnp.int32, (columns, span), 1) % columns
    pick = (column == down_column(position_ref)).astype(jnp.bfloat16)
    rows = jnp.dot(pick, kept, preferred_element_type=jnp.float32).astype(jnp.bfloat16)
    for k in range(copies):
        copies_ref[k] = rows


def middle(position, pieces, states, devices):
    columns = position.shape[1]
    flat = jax.ShapeDtypeStruct(pieces.shape[1:], jnp.float32)
    width = flat.size // columns
    return pl.pallas_call(
        functools.partial(middle_kernel, devices),
        out_shape=(flat, flat, flat, jax.ShapeDtypeStruct((pieces.shape[0], columns, width), jnp.bfloat16)),
        compiler_params=small(),
    )(position, pieces, *states)


def finish_kernel(
    position_ref, new_first_ref, new_second_ref, stepped_ref, own_ref, other_ref,
    master_out, first_out, second_out, copy_out, master_ref, scaled_ref, sems,
):
    core = lax.axis_index("core")
    chips, columns, width = own_ref.shape
    parts = sems.shape[0] - 3
    copies = [
        pltpu.make_async_copy(new_first_ref, first_out, sems.at[0]),
        pltpu.make_async_copy(new_second_ref, second_out, sems.at[1]),
    ]
    for copy in copies:
        copy.start()
    total = jnp.zeros((columns, width), jnp.float32)
    for ref in (own_ref, other_ref):
        for k in range(chips):
            value = ref[k].astype(jnp.float32)
            total = total + value * value
    factor = lax.rsqrt(jnp.sum(total, axis=1, keepdims=True) / D + norm_epsilon)
    position = down_column(position_ref)
    period = columns // 8
    lane = lax.broadcasted_iota(jnp.int32, (1, LANES), 1)
    line = lax.broadcasted_iota(jnp.int32, stepped_ref.shape, 0) % period
    spread = jnp.zeros(stepped_ref.shape, jnp.float32)
    for p in range(period):
        flat_column = (p * LANES + lane) % columns
        picked = jnp.sum(jnp.where(position == flat_column, factor, 0.0), axis=0, keepdims=True)
        spread = jnp.where(line == p, picked, spread)
    master_ref[...] = stepped_ref[...] * spread
    copies.append(pltpu.make_async_copy(master_ref, master_out, sems.at[2]))
    copies[2].start()
    each = chips // parts
    for p in range(parts):
        for k in range(p * each, (p + 1) * each):
            for ref, place in ((own_ref, core), (other_ref, 1 - core)):
                start = pl.multiple_of((2 * k + place) * width, width)
                scaled_ref[:, pl.ds(start, width)] = (ref[slot(k, chips)].astype(jnp.float32) * factor).astype(jnp.bfloat16)
        part = pl.ds(p * 2 * each * width, 2 * each * width)
        copies.append(pltpu.make_async_copy(scaled_ref.at[:, part], copy_out.at[:, part], sems.at[3 + p]))
        copies[3 + p].start()
    for copy in copies:
        copy.wait()


def finish(position, new_first, new_second, stepped, own, other):
    chips, columns, width = own.shape
    wide = (columns, 2 * chips * width)
    parts = 4 if chips % 4 == 0 else 1
    flat = jax.ShapeDtypeStruct(stepped.shape, jnp.float32)
    return pl.pallas_call(
        finish_kernel,
        in_specs=[pl.BlockSpec(memory_space=pltpu.VMEM)] * 6,
        out_specs=(pl.BlockSpec(memory_space=pl.ANY),) * 4,
        out_shape=(flat, flat, flat, jax.ShapeDtypeStruct(wide, jnp.bfloat16)),
        scratch_shapes=[
            pltpu.VMEM(stepped.shape, jnp.float32),
            pltpu.VMEM(wide, jnp.bfloat16),
            pltpu.SemaphoreType.DMA((3 + parts,)),
        ],
        compiler_params=small(),
    )(position, new_first, new_second, stepped, own, other)


def finish_narrow(owners, stepped, blocks):
    columns = owners.shape[0]
    blocks = blocks.astype(jnp.float32)
    factor = lax.rsqrt(jnp.sum(blocks * blocks, axis=(0, 2)) / D + norm_epsilon)
    scaled = jnp.transpose(blocks * factor[None, :, None], (1, 0, 2))
    flat_factor = jnp.zeros((columns,), jnp.float32).at[flat_positions(owners)].set(factor)
    new_master = (stepped.reshape(-1, columns) * flat_factor).reshape(stepped.shape)
    return (new_master, scaled.reshape(columns, -1).astype(jnp.bfloat16))


def spread(value, axes, size):
    return lax.all_to_all(jnp.broadcast_to(value[None], (size,) + value.shape), axes, 0, 0, tiled=True)


def on_layers(grads, master, first_moment, second_moment, owners):
    chips = lax.axis_size(("layer", "plane"))
    swap = [(0, 1), (1, 0)]
    kept, sent = pack(grads, chips, master.shape[0] // LANES)
    taken = lax.ppermute(sent, "core", swap)
    states = (master, first_moment, second_moment)
    position, *states, pairs = add_pairs(kept, taken, flat_positions(owners), states)
    pieces = lax.all_to_all(pairs, ("plane", "layer"), 0, 0, tiled=True)
    *updated, copies = middle(position, pieces, states, 2 * chips)
    own = lax.all_to_all(copies, ("plane", "layer"), 0, 0, tiled=True)
    other = lax.ppermute(own, "core", swap)
    *flat, model_copy = finish(position, *updated, own, other)
    return (*(x.reshape(-1) for x in flat), model_copy)


def on_device(grads, master, first_moment, second_moment, owners):
    devices = lax.axis_size(AXES)
    columns = owners.shape[0]
    pieces = lax.all_to_all(grads.reshape(devices, -1), AXES, 0, 0, tiled=True)
    gradient = jnp.sum(pieces.astype(jnp.float32), axis=0) / devices
    new_first, new_second, stepped = adam_step(gradient, master, first_moment, second_moment)
    rows = jnp.take(stepped.reshape(-1, columns), flat_positions(owners), axis=1).T.astype(jnp.bfloat16)
    new_master, model_copy = finish_narrow(owners, stepped, spread(rows, AXES, devices))
    return (new_master, new_first, new_second, model_copy)


def solution(mesh):
    body, axes = on_device, AXES
    if mesh.shape["replica"] == 2 and mesh.shape["shard"] % PLANE == 0:
        body, axes = on_layers, LAYERS
        mesh = jax.sharding.Mesh(mesh.devices.reshape(-1, PLANE, 2), LAYERS)
    placed = (P(axes, None), P(axes), P(axes), P(axes), P())
    return jax.shard_map(
        body,
        mesh=mesh,
        in_specs=placed,
        out_specs=(P(axes), P(axes), P(axes), P()),
        check_vma=False,
    )
```

```python
import functools

import jax
import jax.numpy as jnp
from jax import lax
from jax.experimental import pallas as pl
from jax.experimental.pallas import tpu as pltpu
from jax.sharding import PartitionSpec as P

D = 8192


learning_rate = 0.1
adam_epsilon = 1e-08
norm_epsilon = 1e-06
first_correction = 1.0 - 0.9**20
second_correction = 1.0 - 0.95**20
AXES = ("shard", "replica")
LANES = 128


def adam_step(gradient, master, first_moment, second_moment):
    new_first = 0.9 * first_moment + 0.1 * gradient
    new_second = 0.95 * second_moment + 0.05 * gradient * gradient
    stepped = master - learning_rate * (new_first / first_correction) / (
        jnp.sqrt(new_second / second_correction) + adam_epsilon
    )
    return (new_first, new_second, stepped)


def flat_positions(owners):
    column_ids = jnp.arange(owners.shape[0], dtype=jnp.int32)
    ranked_below = owners[None, :] < owners[:, None]
    same_before = (owners[None, :] == owners[:, None]) & (column_ids[None, :] < column_ids[:, None])
    return jnp.sum((ranked_below | same_before).astype(jnp.int32), axis=1)


def small(**more):
    return pltpu.CompilerParams(vmem_limit_bytes=6 * 2**20, **more)


def pack_kernel(grads_ref, kept_ref, sent_ref):
    chips, lines, lanes = kept_ref.shape
    core = lax.axis_index("replica")
    width = lines * lanes
    for k in range(chips):
        for ref, place in ((kept_ref, core), (sent_ref, 1 - core)):
            start = pl.multiple_of((2 * k + place) * width, width)
            row = grads_ref[:, pl.ds(start, width)].astype(jnp.float32)
            ref[k] = row.reshape(lines, lanes).astype(jnp.bfloat16)


def pack(grads, chips, lines):
    packed = jax.ShapeDtypeStruct((chips, lines, LANES), jnp.bfloat16)
    return pl.pallas_call(pack_kernel, out_shape=(packed, packed), compiler_params=small())(grads)


def pair_kernel(kept_ref, taken_ref, *refs):
    *held, pairs_ref = refs
    pairs = kept_ref[...].astype(jnp.float32) + taken_ref[...].astype(jnp.float32)
    pairs_ref[...] = pairs.astype(jnp.bfloat16)
    for source, target in zip(held[:4], held[4:]):
        target[...] = source[...]


def add_pairs(kept, taken, position, states):
    flat = jax.ShapeDtypeStruct(kept.shape[1:], jnp.float32)
    position = position[None, :]
    small_shapes = (jax.ShapeDtypeStruct(position.shape, position.dtype), flat, flat, flat)
    return pl.pallas_call(
        pair_kernel,
        out_shape=(*small_shapes, jax.ShapeDtypeStruct(kept.shape, jnp.bfloat16)),
        compiler_params=small(),
    )(kept, taken, position, *(x.reshape(flat.shape) for x in states))


def down_column(row_ref):
    columns = row_ref.shape[1]
    square = (columns, columns)
    same = lax.broadcasted_iota(jnp.int32, square, 0) == lax.broadcasted_iota(jnp.int32, square, 1)
    row = jnp.broadcast_to(row_ref[...].astype(jnp.float32), square)
    return jnp.sum(jnp.where(same, row, 0.0), axis=1, keepdims=True).astype(jnp.int32)


def middle_kernel(
    devices, position_ref, pieces_ref, master_ref, first_ref, second_ref,
    new_first_ref, new_second_ref, stepped_ref, copies_ref,
):
    copies, columns, width = copies_ref.shape
    total = pieces_ref[0].astype(jnp.float32)
    for k in range(1, pieces_ref.shape[0]):
        total = total + pieces_ref[k].astype(jnp.float32)
    gradient = total / devices
    new_first_ref[...], new_second_ref[...], stepped_ref[...] = adam_step(
        gradient, master_ref[...], first_ref[...], second_ref[...]
    )
    period = columns // 8
    span = period * LANES
    group = span // columns
    lines = stepped_ref.shape[0] // period
    wide = [stepped_ref[pl.ds(b, lines, stride=period), :].astype(jnp.bfloat16) for b in range(period)]
    wide = jnp.concatenate(wide, axis=1)
    line = lax.broadcasted_iota(jnp.int32, (lines, width), 0)
    row = lax.broadcasted_iota(jnp.int32, (lines, width), 1)
    repeat = (row // group == line).astype(jnp.bfloat16)
    spread = lax.dot_general(wide, repeat, (((0,), (0,)), ((), ())), preferred_element_type=jnp.float32)
    entry = lax.broadcasted_iota(jnp.int32, (span, width), 0)
    row = lax.broadcasted_iota(jnp.int32, (span, width), 1)
    kept = jnp.where(entry // columns == row % group, spread, 0.0).astype(jnp.bfloat16)
    column = lax.broadcasted_iota(jnp.int32, (columns, span), 1) % columns
    pick = (column == down_column(position_ref)).astype(jnp.bfloat16)
    rows = jnp.dot(pick, kept, preferred_element_type=jnp.float32).astype(jnp.bfloat16)
    for k in range(copies):
        copies_ref[k] = rows


def middle(position, pieces, states, devices):
    columns = position.shape[1]
    flat = jax.ShapeDtypeStruct(pieces.shape[1:], jnp.float32)
    width = flat.size // columns
    return pl.pallas_call(
        functools.partial(middle_kernel, devices),
        out_shape=(flat, flat, flat, jax.ShapeDtypeStruct((pieces.shape[0], columns, width), jnp.bfloat16)),
        compiler_params=small(),
    )(position, pieces, *states)


def finish_kernel(
    position_ref, new_first_ref, new_second_ref, stepped_ref, own_ref, other_ref,
    master_out, first_out, second_out, copy_out, master_ref, scaled_ref, sems,
):
    core = lax.axis_index("replica")
    chips, columns, width = own_ref.shape
    parts = sems.shape[0] - 3
    copies = [
        pltpu.make_async_copy(new_first_ref, first_out, sems.at[0]),
        pltpu.make_async_copy(new_second_ref, second_out, sems.at[1]),
    ]
    for copy in copies:
        copy.start()
    total = jnp.zeros((columns, width), jnp.float32)
    for ref in (own_ref, other_ref):
        for k in range(chips):
            value = ref[k].astype(jnp.float32)
            total = total + value * value
    factor = lax.rsqrt(jnp.sum(total, axis=1, keepdims=True) / D + norm_epsilon)
    each = chips // parts
    for p in range(parts):
        for k in range(p * each, (p + 1) * each):
            for ref, place in ((own_ref, core), (other_ref, 1 - core)):
                start = pl.multiple_of((2 * k + place) * width, width)
                scaled_ref[:, pl.ds(start, width)] = (ref[k].astype(jnp.float32) * factor).astype(jnp.bfloat16)
        part = pl.ds(p * 2 * each * width, 2 * each * width)
        copies.append(pltpu.make_async_copy(scaled_ref.at[:, part], copy_out.at[:, part], sems.at[3 + p]))
        copies[-1].start()
    position = down_column(position_ref)
    period = columns // 8
    lane = lax.broadcasted_iota(jnp.int32, (1, LANES), 1)
    line = lax.broadcasted_iota(jnp.int32, stepped_ref.shape, 0) % period
    spread = jnp.zeros(stepped_ref.shape, jnp.float32)
    for p in range(period):
        flat_column = (p * LANES + lane) % columns
        picked = jnp.sum(jnp.where(position == flat_column, factor, 0.0), axis=0, keepdims=True)
        spread = jnp.where(line == p, picked, spread)
    master_ref[...] = stepped_ref[...] * spread
    copies.append(pltpu.make_async_copy(master_ref, master_out, sems.at[2]))
    copies[-1].start()
    for copy in copies:
        copy.wait()


def finish(position, new_first, new_second, stepped, own, other):
    chips, columns, width = own.shape
    wide = (columns, 2 * chips * width)
    parts = 4 if chips % 4 == 0 else 1
    flat = jax.ShapeDtypeStruct(stepped.shape, jnp.float32)
    return pl.pallas_call(
        finish_kernel,
        in_specs=[pl.BlockSpec(memory_space=pltpu.VMEM)] * 6,
        out_specs=(pl.BlockSpec(memory_space=pl.ANY),) * 4,
        out_shape=(flat, flat, flat, jax.ShapeDtypeStruct(wide, jnp.bfloat16)),
        scratch_shapes=[
            pltpu.VMEM(stepped.shape, jnp.float32),
            pltpu.VMEM(wide, jnp.bfloat16),
            pltpu.SemaphoreType.DMA((3 + parts,)),
        ],
        compiler_params=small(),
    )(position, new_first, new_second, stepped, own, other)


def finish_narrow(owners, stepped, blocks):
    columns = owners.shape[0]
    blocks = blocks.astype(jnp.float32)
    factor = lax.rsqrt(jnp.sum(blocks * blocks, axis=(0, 2)) / D + norm_epsilon)
    scaled = jnp.transpose(blocks * factor[None, :, None], (1, 0, 2))
    flat_factor = jnp.zeros((columns,), jnp.float32).at[flat_positions(owners)].set(factor)
    new_master = (stepped.reshape(-1, columns) * flat_factor).reshape(stepped.shape)
    return (new_master, scaled.reshape(columns, -1).astype(jnp.bfloat16))


def spread(value, axes, size):
    return lax.all_to_all(jnp.broadcast_to(value[None], (size,) + value.shape), axes, 0, 0, tiled=True)


def on_device(grads, master, first_moment, second_moment, owners):
    shards, replicas = lax.axis_size("shard"), lax.axis_size("replica")
    devices = shards * replicas
    columns = owners.shape[0]
    if replicas == 2 and master.shape[0] // LANES % 48 == 0:
        kept, sent = pack(grads, shards, master.shape[0] // LANES)
        taken = lax.ppermute(sent, "replica", [(0, 1), (1, 0)])
        states = (master, first_moment, second_moment)
        position, *states, pairs = add_pairs(kept, taken, flat_positions(owners), states)
        pieces = lax.all_to_all(pairs, "shard", 0, 0, tiled=True)
        *updated, copies = middle(position, pieces, states, devices)
        own = lax.all_to_all(copies, "shard", 0, 0, tiled=True)
        other = lax.ppermute(own, "replica", [(0, 1), (1, 0)])
        *flat, model_copy = finish(position, *updated, own, other)
        return (*(x.reshape(-1) for x in flat), model_copy)
    pieces = lax.all_to_all(grads.reshape(devices, -1), AXES, 0, 0, tiled=True)
    gradient = jnp.sum(pieces.astype(jnp.float32), axis=0) / devices
    new_first, new_second, stepped = adam_step(gradient, master, first_moment, second_moment)
    rows = jnp.take(stepped.reshape(-1, columns), flat_positions(owners), axis=1).T.astype(jnp.bfloat16)
    new_master, model_copy = finish_narrow(owners, stepped, spread(rows, AXES, devices))
    return (new_master, new_first, new_second, model_copy)


def solution(mesh):
    placed = (P(AXES, None), P(AXES), P(AXES), P(AXES), P())
    return jax.shard_map(
        on_device,
        mesh=mesh,
        in_specs=placed,
        out_specs=(P(AXES), P(AXES), P(AXES), P()),
        check_vma=False,
    )
```

```python
import functools

import jax
import jax.numpy as jnp
from jax import lax
from jax.experimental import pallas as pl
from jax.experimental.pallas import tpu as pltpu
from jax.sharding import PartitionSpec as P

D = 8192


learning_rate = 0.1
adam_epsilon = 1e-08
norm_epsilon = 1e-06
first_correction = 1.0 - 0.9**20
second_correction = 1.0 - 0.95**20
AXES = ("shard", "replica")
LANES = 128


def adam_step(gradient, master, first_moment, second_moment):
    new_first = 0.9 * first_moment + 0.1 * gradient
    new_second = 0.95 * second_moment + 0.05 * gradient * gradient
    stepped = master - learning_rate * (new_first / first_correction) / (
        jnp.sqrt(new_second / second_correction) + adam_epsilon
    )
    return (new_first, new_second, stepped)


def flat_positions(owners):
    column_ids = jnp.arange(owners.shape[0], dtype=jnp.int32)
    ranked_below = owners[None, :] < owners[:, None]
    same_before = (owners[None, :] == owners[:, None]) & (column_ids[None, :] < column_ids[:, None])
    return jnp.sum((ranked_below | same_before).astype(jnp.int32), axis=1)


def small(**more):
    return pltpu.CompilerParams(vmem_limit_bytes=6 * 2**20, **more)


def far_first(chips):
    return list(range(chips))[::-1]


def middle_first(chips):
    return [(k + chips // 2) % chips for k in range(chips)]


def pack_kernel(grads_ref, kept_ref, sent_ref):
    chips, lines, lanes = kept_ref.shape
    core = lax.axis_index("replica")
    width = lines * lanes
    order = far_first(chips)
    slots = [order.index(k) for k in range(chips)]
    for k in range(chips):
        for ref, place in ((kept_ref, core), (sent_ref, 1 - core)):
            start = pl.multiple_of((2 * k + place) * width, width)
            row = grads_ref[:, pl.ds(start, width)].astype(jnp.float32)
            ref[slots[k]] = row.reshape(lines, lanes).astype(jnp.bfloat16)


def pack(grads, chips, lines):
    packed = jax.ShapeDtypeStruct((chips, lines, LANES), jnp.bfloat16)
    return pl.pallas_call(pack_kernel, out_shape=(packed, packed), compiler_params=small())(grads)


def pair_kernel(kept_ref, taken_ref, *refs):
    *held, pairs_ref = refs
    pairs = kept_ref[...].astype(jnp.float32) + taken_ref[...].astype(jnp.float32)
    pairs_ref[...] = pairs.astype(jnp.bfloat16)
    for source, target in zip(held[:4], held[4:]):
        target[...] = source[...]


def add_pairs(kept, taken, position, states):
    flat = jax.ShapeDtypeStruct(kept.shape[1:], jnp.float32)
    position = position[None, :]
    small_shapes = (jax.ShapeDtypeStruct(position.shape, position.dtype), flat, flat, flat)
    return pl.pallas_call(
        pair_kernel,
        out_shape=(*small_shapes, jax.ShapeDtypeStruct(kept.shape, jnp.bfloat16)),
        compiler_params=small(),
    )(kept, taken, position, *(x.reshape(flat.shape) for x in states))


def down_column(row_ref):
    columns = row_ref.shape[1]
    square = (columns, columns)
    same = lax.broadcasted_iota(jnp.int32, square, 0) == lax.broadcasted_iota(jnp.int32, square, 1)
    row = jnp.broadcast_to(row_ref[...].astype(jnp.float32), square)
    return jnp.sum(jnp.where(same, row, 0.0), axis=1, keepdims=True).astype(jnp.int32)


def middle_kernel(
    devices, position_ref, pieces_ref, master_ref, first_ref, second_ref,
    new_first_ref, new_second_ref, stepped_ref, copies_ref,
):
    copies, columns, width = copies_ref.shape
    total = pieces_ref[0].astype(jnp.float32)
    for k in range(1, pieces_ref.shape[0]):
        total = total + pieces_ref[k].astype(jnp.float32)
    gradient = total / devices
    new_first_ref[...], new_second_ref[...], stepped_ref[...] = adam_step(
        gradient, master_ref[...], first_ref[...], second_ref[...]
    )
    period = columns // 8
    span = period * LANES
    group = span // columns
    lines = stepped_ref.shape[0] // period
    wide = [stepped_ref[pl.ds(b, lines, stride=period), :].astype(jnp.bfloat16) for b in range(period)]
    wide = jnp.concatenate(wide, axis=1)
    line = lax.broadcasted_iota(jnp.int32, (lines, width), 0)
    row = lax.broadcasted_iota(jnp.int32, (lines, width), 1)
    repeat = (row // group == line).astype(jnp.bfloat16)
    spread = lax.dot_general(wide, repeat, (((0,), (0,)), ((), ())), preferred_element_type=jnp.float32)
    entry = lax.broadcasted_iota(jnp.int32, (span, width), 0)
    row = lax.broadcasted_iota(jnp.int32, (span, width), 1)
    kept = jnp.where(entry // columns == row % group, spread, 0.0).astype(jnp.bfloat16)
    column = lax.broadcasted_iota(jnp.int32, (columns, span), 1) % columns
    pick = (column == down_column(position_ref)).astype(jnp.bfloat16)
    rows = jnp.dot(pick, kept, preferred_element_type=jnp.float32).astype(jnp.bfloat16)
    for k in range(copies):
        copies_ref[k] = rows


def middle(position, pieces, states, devices):
    columns = position.shape[1]
    flat = jax.ShapeDtypeStruct(pieces.shape[1:], jnp.float32)
    width = flat.size // columns
    return pl.pallas_call(
        functools.partial(middle_kernel, devices),
        out_shape=(flat, flat, flat, jax.ShapeDtypeStruct((pieces.shape[0], columns, width), jnp.bfloat16)),
        compiler_params=small(),
    )(position, pieces, *states)


def finish_kernel(
    position_ref, new_first_ref, new_second_ref, stepped_ref, own_ref, other_ref,
    master_out, first_out, second_out, copy_out, master_ref, scaled_ref, sems,
):
    core = lax.axis_index("replica")
    chips, columns, width = own_ref.shape
    parts = sems.shape[0] - 3
    copies = [
        pltpu.make_async_copy(new_first_ref, first_out, sems.at[0]),
        pltpu.make_async_copy(new_second_ref, second_out, sems.at[1]),
    ]
    for copy in copies:
        copy.start()
    total = jnp.zeros((columns, width), jnp.float32)
    for ref in (own_ref, other_ref):
        for k in range(chips):
            value = ref[k].astype(jnp.float32)
            total = total + value * value
    factor = lax.rsqrt(jnp.sum(total, axis=1, keepdims=True) / D + norm_epsilon)
    order = middle_first(chips)
    slots = [order.index(k) for k in range(chips)]
    each = chips // parts
    for p in range(parts):
        for k in range(p * each, (p + 1) * each):
            for ref, place in ((own_ref, core), (other_ref, 1 - core)):
                start = pl.multiple_of((2 * k + place) * width, width)
                scaled_ref[:, pl.ds(start, width)] = (ref[slots[k]].astype(jnp.float32) * factor).astype(jnp.bfloat16)
        part = pl.ds(p * 2 * each * width, 2 * each * width)
        copies.append(pltpu.make_async_copy(scaled_ref.at[:, part], copy_out.at[:, part], sems.at[3 + p]))
        copies[-1].start()
    position = down_column(position_ref)
    period = columns // 8
    lane = lax.broadcasted_iota(jnp.int32, (1, LANES), 1)
    line = lax.broadcasted_iota(jnp.int32, stepped_ref.shape, 0) % period
    spread = jnp.zeros(stepped_ref.shape, jnp.float32)
    for p in range(period):
        flat_column = (p * LANES + lane) % columns
        picked = jnp.sum(jnp.where(position == flat_column, factor, 0.0), axis=0, keepdims=True)
        spread = jnp.where(line == p, picked, spread)
    master_ref[...] = stepped_ref[...] * spread
    copies.append(pltpu.make_async_copy(master_ref, master_out, sems.at[2]))
    copies[-1].start()
    for copy in copies:
        copy.wait()


def finish(position, new_first, new_second, stepped, own, other):
    chips, columns, width = own.shape
    wide = (columns, 2 * chips * width)
    parts = 4 if chips % 4 == 0 else 1
    flat = jax.ShapeDtypeStruct(stepped.shape, jnp.float32)
    return pl.pallas_call(
        finish_kernel,
        in_specs=[pl.BlockSpec(memory_space=pltpu.VMEM)] * 6,
        out_specs=(pl.BlockSpec(memory_space=pl.ANY),) * 4,
        out_shape=(flat, flat, flat, jax.ShapeDtypeStruct(wide, jnp.bfloat16)),
        scratch_shapes=[
            pltpu.VMEM(stepped.shape, jnp.float32),
            pltpu.VMEM(wide, jnp.bfloat16),
            pltpu.SemaphoreType.DMA((3 + parts,)),
        ],
        compiler_params=small(),
    )(position, new_first, new_second, stepped, own, other)


def finish_narrow(owners, stepped, blocks):
    columns = owners.shape[0]
    blocks = blocks.astype(jnp.float32)
    factor = lax.rsqrt(jnp.sum(blocks * blocks, axis=(0, 2)) / D + norm_epsilon)
    scaled = jnp.transpose(blocks * factor[None, :, None], (1, 0, 2))
    flat_factor = jnp.zeros((columns,), jnp.float32).at[flat_positions(owners)].set(factor)
    new_master = (stepped.reshape(-1, columns) * flat_factor).reshape(stepped.shape)
    return (new_master, scaled.reshape(columns, -1).astype(jnp.bfloat16))


def spread(value, axes, size):
    return lax.all_to_all(jnp.broadcast_to(value[None], (size,) + value.shape), axes, 0, 0, tiled=True)


def on_device(grads, master, first_moment, second_moment, owners):
    shards, replicas = lax.axis_size("shard"), lax.axis_size("replica")
    devices = shards * replicas
    columns = owners.shape[0]
    if replicas == 2 and master.shape[0] // LANES % 48 == 0:
        kept, sent = pack(grads, shards, master.shape[0] // LANES)
        taken = lax.ppermute(sent, "replica", [(0, 1), (1, 0)])
        states = (master, first_moment, second_moment)
        position, *states, pairs = add_pairs(kept, taken, flat_positions(owners), states)
        groups = [far_first(shards)]
        pieces = lax.all_to_all(pairs, "shard", 0, 0, tiled=True, axis_index_groups=groups)
        *updated, copies = middle(position, pieces, states, devices)
        groups = [middle_first(shards)]
        own = lax.all_to_all(copies, "shard", 0, 0, tiled=True, axis_index_groups=groups)
        other = lax.ppermute(own, "replica", [(0, 1), (1, 0)])
        *flat, model_copy = finish(position, *updated, own, other)
        return (*(x.reshape(-1) for x in flat), model_copy)
    pieces = lax.all_to_all(grads.reshape(devices, -1), AXES, 0, 0, tiled=True)
    gradient = jnp.sum(pieces.astype(jnp.float32), axis=0) / devices
    new_first, new_second, stepped = adam_step(gradient, master, first_moment, second_moment)
    rows = jnp.take(stepped.reshape(-1, columns), flat_positions(owners), axis=1).T.astype(jnp.bfloat16)
    new_master, model_copy = finish_narrow(owners, stepped, spread(rows, AXES, devices))
    return (new_master, new_first, new_second, model_copy)


def solution(mesh):
    placed = (P(AXES, None), P(AXES), P(AXES), P(AXES), P())
    return jax.shard_map(
        on_device,
        mesh=mesh,
        in_specs=placed,
        out_specs=(P(AXES), P(AXES), P(AXES), P()),
        check_vma=False,
    )
```

```python
import functools

import jax
import jax.numpy as jnp
from jax import lax
from jax.experimental import pallas as pl
from jax.experimental.pallas import tpu as pltpu
from jax.sharding import PartitionSpec as P

D = 8192


learning_rate = 0.1
adam_epsilon = 1e-08
norm_epsilon = 1e-06
first_correction = 1.0 - 0.9**20
second_correction = 1.0 - 0.95**20
AXES = ("shard", "replica")
LANES = 128


def adam_step(gradient, master, first_moment, second_moment):
    new_first = 0.9 * first_moment + 0.1 * gradient
    new_second = 0.95 * second_moment + 0.05 * gradient * gradient
    stepped = master - learning_rate * (new_first / first_correction) / (
        jnp.sqrt(new_second / second_correction) + adam_epsilon
    )
    return (new_first, new_second, stepped)


def flat_positions(owners):
    column_ids = jnp.arange(owners.shape[0], dtype=jnp.int32)
    ranked_below = owners[None, :] < owners[:, None]
    same_before = (owners[None, :] == owners[:, None]) & (column_ids[None, :] < column_ids[:, None])
    return jnp.sum((ranked_below | same_before).astype(jnp.int32), axis=1)


def small(**more):
    return pltpu.CompilerParams(vmem_limit_bytes=6 * 2**20, **more)


def far_first(chips):
    return list(range(chips))[::-1]


def pack_kernel(grads_ref, kept_ref, sent_ref):
    chips, lines, lanes = kept_ref.shape
    core = lax.axis_index("replica")
    width = lines * lanes
    order = far_first(chips)
    slots = [order.index(k) for k in range(chips)]
    for k in range(chips):
        for ref, place in ((kept_ref, core), (sent_ref, 1 - core)):
            start = pl.multiple_of((2 * k + place) * width, width)
            row = grads_ref[:, pl.ds(start, width)].astype(jnp.float32)
            ref[slots[k]] = row.reshape(lines, lanes).astype(jnp.bfloat16)


def pack(grads, chips, lines):
    packed = jax.ShapeDtypeStruct((chips, lines, LANES), jnp.bfloat16)
    return pl.pallas_call(pack_kernel, out_shape=(packed, packed), compiler_params=small())(grads)


def pair_kernel(kept_ref, taken_ref, *refs):
    *held, pairs_ref = refs
    pairs = kept_ref[...].astype(jnp.float32) + taken_ref[...].astype(jnp.float32)
    pairs_ref[...] = pairs.astype(jnp.bfloat16)
    for source, target in zip(held[:4], held[4:]):
        target[...] = source[...]


def add_pairs(kept, taken, position, states):
    flat = jax.ShapeDtypeStruct(kept.shape[1:], jnp.float32)
    position = position[None, :]
    small_shapes = (jax.ShapeDtypeStruct(position.shape, position.dtype), flat, flat, flat)
    return pl.pallas_call(
        pair_kernel,
        out_shape=(*small_shapes, jax.ShapeDtypeStruct(kept.shape, jnp.bfloat16)),
        compiler_params=small(),
    )(kept, taken, position, *(x.reshape(flat.shape) for x in states))


def down_column(row_ref):
    columns = row_ref.shape[1]
    square = (columns, columns)
    same = lax.broadcasted_iota(jnp.int32, square, 0) == lax.broadcasted_iota(jnp.int32, square, 1)
    row = jnp.broadcast_to(row_ref[...].astype(jnp.float32), square)
    return jnp.sum(jnp.where(same, row, 0.0), axis=1, keepdims=True).astype(jnp.int32)


def middle_kernel(
    devices, position_ref, pieces_ref, master_ref, first_ref, second_ref,
    new_first_ref, new_second_ref, stepped_ref, copies_ref,
):
    copies, columns, width = copies_ref.shape
    total = pieces_ref[0].astype(jnp.float32)
    for k in range(1, pieces_ref.shape[0]):
        total = total + pieces_ref[k].astype(jnp.float32)
    gradient = total / devices
    new_first_ref[...], new_second_ref[...], stepped_ref[...] = adam_step(
        gradient, master_ref[...], first_ref[...], second_ref[...]
    )
    period = columns // 8
    span = period * LANES
    group = span // columns
    lines = stepped_ref.shape[0] // period
    wide = [stepped_ref[pl.ds(b, lines, stride=period), :].astype(jnp.bfloat16) for b in range(period)]
    wide = jnp.concatenate(wide, axis=1)
    line = lax.broadcasted_iota(jnp.int32, (lines, width), 0)
    row = lax.broadcasted_iota(jnp.int32, (lines, width), 1)
    repeat = (row // group == line).astype(jnp.bfloat16)
    spread = lax.dot_general(wide, repeat, (((0,), (0,)), ((), ())), preferred_element_type=jnp.float32)
    entry = lax.broadcasted_iota(jnp.int32, (span, width), 0)
    row = lax.broadcasted_iota(jnp.int32, (span, width), 1)
    kept = jnp.where(entry // columns == row % group, spread, 0.0).astype(jnp.bfloat16)
    column = lax.broadcasted_iota(jnp.int32, (columns, span), 1) % columns
    pick = (column == down_column(position_ref)).astype(jnp.bfloat16)
    rows = jnp.dot(pick, kept, preferred_element_type=jnp.float32).astype(jnp.bfloat16)
    for k in range(copies):
        copies_ref[k] = rows


def middle(position, pieces, states, devices):
    columns = position.shape[1]
    flat = jax.ShapeDtypeStruct(pieces.shape[1:], jnp.float32)
    width = flat.size // columns
    return pl.pallas_call(
        functools.partial(middle_kernel, devices),
        out_shape=(flat, flat, flat, jax.ShapeDtypeStruct((pieces.shape[0], columns, width), jnp.bfloat16)),
        compiler_params=small(),
    )(position, pieces, *states)


def finish_kernel(
    position_ref, new_first_ref, new_second_ref, stepped_ref, own_ref, other_ref,
    master_out, first_out, second_out, copy_out, master_ref, scaled_ref, sems,
):
    core = lax.axis_index("replica")
    chips, columns, width = own_ref.shape
    parts = sems.shape[0] - 3
    copies = [
        pltpu.make_async_copy(new_first_ref, first_out, sems.at[0]),
        pltpu.make_async_copy(new_second_ref, second_out, sems.at[1]),
    ]
    for copy in copies:
        copy.start()
    total = jnp.zeros((columns, width), jnp.float32)
    for ref in (own_ref, other_ref):
        for k in range(chips):
            value = ref[k].astype(jnp.float32)
            total = total + value * value
    factor = lax.rsqrt(jnp.sum(total, axis=1, keepdims=True) / D + norm_epsilon)
    order = far_first(chips)
    slots = [order.index(k) for k in range(chips)]
    each = chips // parts
    for p in range(parts):
        for k in range(p * each, (p + 1) * each):
            for ref, place in ((own_ref, core), (other_ref, 1 - core)):
                start = pl.multiple_of((2 * k + place) * width, width)
                scaled_ref[:, pl.ds(start, width)] = (ref[slots[k]].astype(jnp.float32) * factor).astype(jnp.bfloat16)
        part = pl.ds(p * 2 * each * width, 2 * each * width)
        copies.append(pltpu.make_async_copy(scaled_ref.at[:, part], copy_out.at[:, part], sems.at[3 + p]))
        copies[-1].start()
    position = down_column(position_ref)
    period = columns // 8
    lane = lax.broadcasted_iota(jnp.int32, (1, LANES), 1)
    line = lax.broadcasted_iota(jnp.int32, stepped_ref.shape, 0) % period
    spread = jnp.zeros(stepped_ref.shape, jnp.float32)
    for p in range(period):
        flat_column = (p * LANES + lane) % columns
        picked = jnp.sum(jnp.where(position == flat_column, factor, 0.0), axis=0, keepdims=True)
        spread = jnp.where(line == p, picked, spread)
    master_ref[...] = stepped_ref[...] * spread
    copies.append(pltpu.make_async_copy(master_ref, master_out, sems.at[2]))
    copies[-1].start()
    for copy in copies:
        copy.wait()


def finish(position, new_first, new_second, stepped, own, other):
    chips, columns, width = own.shape
    wide = (columns, 2 * chips * width)
    parts = 4 if chips % 4 == 0 else 1
    flat = jax.ShapeDtypeStruct(stepped.shape, jnp.float32)
    return pl.pallas_call(
        finish_kernel,
        in_specs=[pl.BlockSpec(memory_space=pltpu.VMEM)] * 6,
        out_specs=(pl.BlockSpec(memory_space=pl.ANY),) * 4,
        out_shape=(flat, flat, flat, jax.ShapeDtypeStruct(wide, jnp.bfloat16)),
        scratch_shapes=[
            pltpu.VMEM(stepped.shape, jnp.float32),
            pltpu.VMEM(wide, jnp.bfloat16),
            pltpu.SemaphoreType.DMA((3 + parts,)),
        ],
        compiler_params=small(),
    )(position, new_first, new_second, stepped, own, other)


def finish_narrow(owners, stepped, blocks):
    columns = owners.shape[0]
    blocks = blocks.astype(jnp.float32)
    factor = lax.rsqrt(jnp.sum(blocks * blocks, axis=(0, 2)) / D + norm_epsilon)
    scaled = jnp.transpose(blocks * factor[None, :, None], (1, 0, 2))
    flat_factor = jnp.zeros((columns,), jnp.float32).at[flat_positions(owners)].set(factor)
    new_master = (stepped.reshape(-1, columns) * flat_factor).reshape(stepped.shape)
    return (new_master, scaled.reshape(columns, -1).astype(jnp.bfloat16))


def spread(value, axes, size):
    return lax.all_to_all(jnp.broadcast_to(value[None], (size,) + value.shape), axes, 0, 0, tiled=True)


def on_device(grads, master, first_moment, second_moment, owners):
    shards, replicas = lax.axis_size("shard"), lax.axis_size("replica")
    devices = shards * replicas
    columns = owners.shape[0]
    if replicas == 2 and master.shape[0] // LANES % 48 == 0:
        kept, sent = pack(grads, shards, master.shape[0] // LANES)
        taken = lax.ppermute(sent, "replica", [(0, 1), (1, 0)])
        states = (master, first_moment, second_moment)
        position, *states, pairs = add_pairs(kept, taken, flat_positions(owners), states)
        groups = [far_first(shards)]
        pieces = lax.all_to_all(pairs, "shard", 0, 0, tiled=True, axis_index_groups=groups)
        *updated, copies = middle(position, pieces, states, devices)
        own = lax.all_to_all(copies, "shard", 0, 0, tiled=True, axis_index_groups=groups)
        other = lax.ppermute(own, "replica", [(0, 1), (1, 0)])
        *flat, model_copy = finish(position, *updated, own, other)
        return (*(x.reshape(-1) for x in flat), model_copy)
    pieces = lax.all_to_all(grads.reshape(devices, -1), AXES, 0, 0, tiled=True)
    gradient = jnp.sum(pieces.astype(jnp.float32), axis=0) / devices
    new_first, new_second, stepped = adam_step(gradient, master, first_moment, second_moment)
    rows = jnp.take(stepped.reshape(-1, columns), flat_positions(owners), axis=1).T.astype(jnp.bfloat16)
    new_master, model_copy = finish_narrow(owners, stepped, spread(rows, AXES, devices))
    return (new_master, new_first, new_second, model_copy)


def solution(mesh):
    placed = (P(AXES, None), P(AXES), P(AXES), P(AXES), P())
    return jax.shard_map(
        on_device,
        mesh=mesh,
        in_specs=placed,
        out_specs=(P(AXES), P(AXES), P(AXES), P()),
        check_vma=False,
    )
```

```python
import functools

import jax
import jax.numpy as jnp
from jax import lax
from jax.experimental import pallas as pl
from jax.experimental.pallas import tpu as pltpu
from jax.sharding import PartitionSpec as P

D = 8192


learning_rate = 0.1
adam_epsilon = 1e-08
norm_epsilon = 1e-06
first_correction = 1.0 - 0.9**20
second_correction = 1.0 - 0.95**20
AXES = ("shard", "replica")
LANES = 128
FIRST = (11, 8)


def adam_step(gradient, master, first_moment, second_moment):
    new_first = 0.9 * first_moment + 0.1 * gradient
    new_second = 0.95 * second_moment + 0.05 * gradient * gradient
    stepped = master - learning_rate * (new_first / first_correction) / (
        jnp.sqrt(new_second / second_correction) + adam_epsilon
    )
    return (new_first, new_second, stepped)


def flat_positions(owners):
    column_ids = jnp.arange(owners.shape[0], dtype=jnp.int32)
    ranked_below = owners[None, :] < owners[:, None]
    same_before = (owners[None, :] == owners[:, None]) & (column_ids[None, :] < column_ids[:, None])
    return jnp.sum((ranked_below | same_before).astype(jnp.int32), axis=1)


def small(**more):
    return pltpu.CompilerParams(vmem_limit_bytes=6 * 2**20, **more)


def listed(chips, first):
    first = first % chips
    return [k ^ first for k in range(chips)]


def pack_kernel(grads_ref, kept_ref, sent_ref):
    chips, lines, lanes = kept_ref.shape
    core = lax.axis_index("replica")
    width = lines * lanes
    order = listed(chips, FIRST[0])
    slots = [order.index(k) for k in range(chips)]
    for k in range(chips):
        for ref, place in ((kept_ref, core), (sent_ref, 1 - core)):
            start = pl.multiple_of((2 * k + place) * width, width)
            row = grads_ref[:, pl.ds(start, width)].astype(jnp.float32)
            ref[slots[k]] = row.reshape(lines, lanes).astype(jnp.bfloat16)


def pack(grads, chips, lines):
    packed = jax.ShapeDtypeStruct((chips, lines, LANES), jnp.bfloat16)
    return pl.pallas_call(pack_kernel, out_shape=(packed, packed), compiler_params=small())(grads)


def pair_kernel(kept_ref, taken_ref, *refs):
    *held, pairs_ref = refs
    pairs = kept_ref[...].astype(jnp.float32) + taken_ref[...].astype(jnp.float32)
    pairs_ref[...] = pairs.astype(jnp.bfloat16)
    for source, target in zip(held[:4], held[4:]):
        target[...] = source[...]


def add_pairs(kept, taken, position, states):
    flat = jax.ShapeDtypeStruct(kept.shape[1:], jnp.float32)
    position = position[None, :]
    small_shapes = (jax.ShapeDtypeStruct(position.shape, position.dtype), flat, flat, flat)
    return pl.pallas_call(
        pair_kernel,
        out_shape=(*small_shapes, jax.ShapeDtypeStruct(kept.shape, jnp.bfloat16)),
        compiler_params=small(),
    )(kept, taken, position, *(x.reshape(flat.shape) for x in states))


def down_column(row_ref):
    columns = row_ref.shape[1]
    square = (columns, columns)
    same = lax.broadcasted_iota(jnp.int32, square, 0) == lax.broadcasted_iota(jnp.int32, square, 1)
    row = jnp.broadcast_to(row_ref[...].astype(jnp.float32), square)
    return jnp.sum(jnp.where(same, row, 0.0), axis=1, keepdims=True).astype(jnp.int32)


def middle_kernel(
    devices, position_ref, pieces_ref, master_ref, first_ref, second_ref,
    new_first_ref, new_second_ref, stepped_ref, copies_ref,
):
    copies, columns, width = copies_ref.shape
    total = pieces_ref[0].astype(jnp.float32)
    for k in range(1, pieces_ref.shape[0]):
        total = total + pieces_ref[k].astype(jnp.float32)
    gradient = total / devices
    new_first_ref[...], new_second_ref[...], stepped_ref[...] = adam_step(
        gradient, master_ref[...], first_ref[...], second_ref[...]
    )
    period = columns // 8
    span = period * LANES
    group = span // columns
    lines = stepped_ref.shape[0] // period
    wide = [stepped_ref[pl.ds(b, lines, stride=period), :].astype(jnp.bfloat16) for b in range(period)]
    wide = jnp.concatenate(wide, axis=1)
    line = lax.broadcasted_iota(jnp.int32, (lines, width), 0)
    row = lax.broadcasted_iota(jnp.int32, (lines, width), 1)
    repeat = (row // group == line).astype(jnp.bfloat16)
    spread = lax.dot_general(wide, repeat, (((0,), (0,)), ((), ())), preferred_element_type=jnp.float32)
    entry = lax.broadcasted_iota(jnp.int32, (span, width), 0)
    row = lax.broadcasted_iota(jnp.int32, (span, width), 1)
    kept = jnp.where(entry // columns == row % group, spread, 0.0).astype(jnp.bfloat16)
    column = lax.broadcasted_iota(jnp.int32, (columns, span), 1) % columns
    pick = (column == down_column(position_ref)).astype(jnp.bfloat16)
    rows = jnp.dot(pick, kept, preferred_element_type=jnp.float32).astype(jnp.bfloat16)
    for k in range(copies):
        copies_ref[k] = rows


def middle(position, pieces, states, devices):
    columns = position.shape[1]
    flat = jax.ShapeDtypeStruct(pieces.shape[1:], jnp.float32)
    width = flat.size // columns
    return pl.pallas_call(
        functools.partial(middle_kernel, devices),
        out_shape=(flat, flat, flat, jax.ShapeDtypeStruct((pieces.shape[0], columns, width), jnp.bfloat16)),
        compiler_params=small(),
    )(position, pieces, *states)


def finish_kernel(
    position_ref, new_first_ref, new_second_ref, stepped_ref, own_ref, other_ref,
    master_out, first_out, second_out, copy_out, master_ref, scaled_ref, sems,
):
    core = lax.axis_index("replica")
    chips, columns, width = own_ref.shape
    parts = sems.shape[0] - 3
    copies = [
        pltpu.make_async_copy(new_first_ref, first_out, sems.at[0]),
        pltpu.make_async_copy(new_second_ref, second_out, sems.at[1]),
    ]
    for copy in copies:
        copy.start()
    total = jnp.zeros((columns, width), jnp.float32)
    for ref in (own_ref, other_ref):
        for k in range(chips):
            value = ref[k].astype(jnp.float32)
            total = total + value * value
    factor = lax.rsqrt(jnp.sum(total, axis=1, keepdims=True) / D + norm_epsilon)
    order = listed(chips, FIRST[1])
    slots = [order.index(k) for k in range(chips)]
    each = chips // parts
    for p in range(parts):
        for k in range(p * each, (p + 1) * each):
            for ref, place in ((own_ref, core), (other_ref, 1 - core)):
                start = pl.multiple_of((2 * k + place) * width, width)
                scaled_ref[:, pl.ds(start, width)] = (ref[slots[k]].astype(jnp.float32) * factor).astype(jnp.bfloat16)
        part = pl.ds(p * 2 * each * width, 2 * each * width)
        copies.append(pltpu.make_async_copy(scaled_ref.at[:, part], copy_out.at[:, part], sems.at[3 + p]))
        copies[-1].start()
    position = down_column(position_ref)
    period = columns // 8
    lane = lax.broadcasted_iota(jnp.int32, (1, LANES), 1)
    line = lax.broadcasted_iota(jnp.int32, stepped_ref.shape, 0) % period
    spread = jnp.zeros(stepped_ref.shape, jnp.float32)
    for p in range(period):
        flat_column = (p * LANES + lane) % columns
        picked = jnp.sum(jnp.where(position == flat_column, factor, 0.0), axis=0, keepdims=True)
        spread = jnp.where(line == p, picked, spread)
    master_ref[...] = stepped_ref[...] * spread
    copies.append(pltpu.make_async_copy(master_ref, master_out, sems.at[2]))
    copies[-1].start()
    for copy in copies:
        copy.wait()


def finish(position, new_first, new_second, stepped, own, other):
    chips, columns, width = own.shape
    wide = (columns, 2 * chips * width)
    parts = 4 if chips % 4 == 0 else 1
    flat = jax.ShapeDtypeStruct(stepped.shape, jnp.float32)
    return pl.pallas_call(
        finish_kernel,
        in_specs=[pl.BlockSpec(memory_space=pltpu.VMEM)] * 6,
        out_specs=(pl.BlockSpec(memory_space=pl.ANY),) * 4,
        out_shape=(flat, flat, flat, jax.ShapeDtypeStruct(wide, jnp.bfloat16)),
        scratch_shapes=[
            pltpu.VMEM(stepped.shape, jnp.float32),
            pltpu.VMEM(wide, jnp.bfloat16),
            pltpu.SemaphoreType.DMA((3 + parts,)),
        ],
        compiler_params=small(),
    )(position, new_first, new_second, stepped, own, other)


def finish_narrow(owners, stepped, blocks):
    columns = owners.shape[0]
    blocks = blocks.astype(jnp.float32)
    factor = lax.rsqrt(jnp.sum(blocks * blocks, axis=(0, 2)) / D + norm_epsilon)
    scaled = jnp.transpose(blocks * factor[None, :, None], (1, 0, 2))
    flat_factor = jnp.zeros((columns,), jnp.float32).at[flat_positions(owners)].set(factor)
    new_master = (stepped.reshape(-1, columns) * flat_factor).reshape(stepped.shape)
    return (new_master, scaled.reshape(columns, -1).astype(jnp.bfloat16))


def spread(value, axes, size):
    return lax.all_to_all(jnp.broadcast_to(value[None], (size,) + value.shape), axes, 0, 0, tiled=True)


def on_device(grads, master, first_moment, second_moment, owners):
    shards, replicas = lax.axis_size("shard"), lax.axis_size("replica")
    devices = shards * replicas
    columns = owners.shape[0]
    if replicas == 2 and shards == 16 and master.shape[0] // LANES % 48 == 0:
        kept, sent = pack(grads, shards, master.shape[0] // LANES)
        taken = lax.ppermute(sent, "replica", [(0, 1), (1, 0)])
        states = (master, first_moment, second_moment)
        position, *states, pairs = add_pairs(kept, taken, flat_positions(owners), states)
        groups = [listed(shards, FIRST[0])]
        pieces = lax.all_to_all(pairs, "shard", 0, 0, tiled=True, axis_index_groups=groups)
        *updated, copies = middle(position, pieces, states, devices)
        groups = [listed(shards, FIRST[1])]
        own = lax.all_to_all(copies, "shard", 0, 0, tiled=True, axis_index_groups=groups)
        other = lax.ppermute(own, "replica", [(0, 1), (1, 0)])
        *flat, model_copy = finish(position, *updated, own, other)
        return (*(x.reshape(-1) for x in flat), model_copy)
    pieces = lax.all_to_all(grads.reshape(devices, -1), AXES, 0, 0, tiled=True)
    gradient = jnp.sum(pieces.astype(jnp.float32), axis=0) / devices
    new_first, new_second, stepped = adam_step(gradient, master, first_moment, second_moment)
    rows = jnp.take(stepped.reshape(-1, columns), flat_positions(owners), axis=1).T.astype(jnp.bfloat16)
    new_master, model_copy = finish_narrow(owners, stepped, spread(rows, AXES, devices))
    return (new_master, new_first, new_second, model_copy)


def solution(mesh):
    placed = (P(AXES, None), P(AXES), P(AXES), P(AXES), P())
    return jax.shard_map(
        on_device,
        mesh=mesh,
        in_specs=placed,
        out_specs=(P(AXES), P(AXES), P(AXES), P()),
        check_vma=False,
    )
```

```python
import functools

import jax
import jax.numpy as jnp
from jax import lax
from jax.experimental import pallas as pl
from jax.experimental.pallas import tpu as pltpu
from jax.sharding import PartitionSpec as P

D = 8192


learning_rate = 0.1
adam_epsilon = 1e-08
norm_epsilon = 1e-06
first_correction = 1.0 - 0.9**20
second_correction = 1.0 - 0.95**20
AXES = ("shard", "replica")
LANES = 128
FIRST = (11, 11)


def adam_step(gradient, master, first_moment, second_moment):
    new_first = 0.9 * first_moment + 0.1 * gradient
    new_second = 0.95 * second_moment + 0.05 * gradient * gradient
    stepped = master - learning_rate * (new_first / first_correction) / (
        jnp.sqrt(new_second / second_correction) + adam_epsilon
    )
    return (new_first, new_second, stepped)


def flat_positions(owners):
    column_ids = jnp.arange(owners.shape[0], dtype=jnp.int32)
    ranked_below = owners[None, :] < owners[:, None]
    same_before = (owners[None, :] == owners[:, None]) & (column_ids[None, :] < column_ids[:, None])
    return jnp.sum((ranked_below | same_before).astype(jnp.int32), axis=1)


def small(**more):
    return pltpu.CompilerParams(vmem_limit_bytes=6 * 2**20, **more)


def listed(chips, first):
    first = first % chips
    return [k ^ first for k in range(chips)]


def pack_kernel(grads_ref, kept_ref, sent_ref):
    chips, lines, lanes = kept_ref.shape
    core = lax.axis_index("replica")
    width = lines * lanes
    order = listed(chips, FIRST[0])
    slots = [order.index(k) for k in range(chips)]
    for k in range(chips):
        for ref, place in ((kept_ref, core), (sent_ref, 1 - core)):
            start = pl.multiple_of((2 * k + place) * width, width)
            row = grads_ref[:, pl.ds(start, width)].astype(jnp.float32)
            ref[slots[k]] = row.reshape(lines, lanes).astype(jnp.bfloat16)


def pack(grads, chips, lines):
    packed = jax.ShapeDtypeStruct((chips, lines, LANES), jnp.bfloat16)
    return pl.pallas_call(pack_kernel, out_shape=(packed, packed), compiler_params=small())(grads)


def pair_kernel(kept_ref, taken_ref, *refs):
    *held, pairs_ref = refs
    pairs = kept_ref[...].astype(jnp.float32) + taken_ref[...].astype(jnp.float32)
    pairs_ref[...] = pairs.astype(jnp.bfloat16)
    for source, target in zip(held[:4], held[4:]):
        target[...] = source[...]


def add_pairs(kept, taken, position, states):
    flat = jax.ShapeDtypeStruct(kept.shape[1:], jnp.float32)
    position = position[None, :]
    small_shapes = (jax.ShapeDtypeStruct(position.shape, position.dtype), flat, flat, flat)
    return pl.pallas_call(
        pair_kernel,
        out_shape=(*small_shapes, jax.ShapeDtypeStruct(kept.shape, jnp.bfloat16)),
        compiler_params=small(),
    )(kept, taken, position, *(x.reshape(flat.shape) for x in states))


def down_column(row_ref):
    columns = row_ref.shape[1]
    square = (columns, columns)
    same = lax.broadcasted_iota(jnp.int32, square, 0) == lax.broadcasted_iota(jnp.int32, square, 1)
    row = jnp.broadcast_to(row_ref[...].astype(jnp.float32), square)
    return jnp.sum(jnp.where(same, row, 0.0), axis=1, keepdims=True).astype(jnp.int32)


def middle_kernel(
    devices, position_ref, pieces_ref, master_ref, first_ref, second_ref,
    new_first_ref, new_second_ref, stepped_ref, copies_ref,
):
    copies, columns, width = copies_ref.shape
    total = pieces_ref[0].astype(jnp.float32)
    for k in range(1, pieces_ref.shape[0]):
        total = total + pieces_ref[k].astype(jnp.float32)
    gradient = total / devices
    new_first_ref[...], new_second_ref[...], stepped_ref[...] = adam_step(
        gradient, master_ref[...], first_ref[...], second_ref[...]
    )
    period = columns // 8
    span = period * LANES
    group = span // columns
    lines = stepped_ref.shape[0] // period
    wide = [stepped_ref[pl.ds(b, lines, stride=period), :].astype(jnp.bfloat16) for b in range(period)]
    wide = jnp.concatenate(wide, axis=1)
    line = lax.broadcasted_iota(jnp.int32, (lines, width), 0)
    row = lax.broadcasted_iota(jnp.int32, (lines, width), 1)
    repeat = (row // group == line).astype(jnp.bfloat16)
    spread = lax.dot_general(wide, repeat, (((0,), (0,)), ((), ())), preferred_element_type=jnp.float32)
    entry = lax.broadcasted_iota(jnp.int32, (span, width), 0)
    row = lax.broadcasted_iota(jnp.int32, (span, width), 1)
    kept = jnp.where(entry // columns == row % group, spread, 0.0).astype(jnp.bfloat16)
    column = lax.broadcasted_iota(jnp.int32, (columns, span), 1) % columns
    pick = (column == down_column(position_ref)).astype(jnp.bfloat16)
    rows = jnp.dot(pick, kept, preferred_element_type=jnp.float32).astype(jnp.bfloat16)
    for k in range(copies):
        copies_ref[k] = rows


def middle(position, pieces, states, devices):
    columns = position.shape[1]
    flat = jax.ShapeDtypeStruct(pieces.shape[1:], jnp.float32)
    width = flat.size // columns
    return pl.pallas_call(
        functools.partial(middle_kernel, devices),
        out_shape=(flat, flat, flat, jax.ShapeDtypeStruct((pieces.shape[0], columns, width), jnp.bfloat16)),
        compiler_params=small(),
    )(position, pieces, *states)


def finish_kernel(
    position_ref, new_first_ref, new_second_ref, stepped_ref, own_ref, other_ref,
    master_out, first_out, second_out, copy_out, master_ref, scaled_ref, sems,
):
    core = lax.axis_index("replica")
    chips, columns, width = own_ref.shape
    parts = sems.shape[0] - 3
    copies = [
        pltpu.make_async_copy(new_first_ref, first_out, sems.at[0]),
        pltpu.make_async_copy(new_second_ref, second_out, sems.at[1]),
    ]
    for copy in copies:
        copy.start()
    total = jnp.zeros((columns, width), jnp.float32)
    for ref in (own_ref, other_ref):
        for k in range(chips):
            value = ref[k].astype(jnp.float32)
            total = total + value * value
    factor = lax.rsqrt(jnp.sum(total, axis=1, keepdims=True) / D + norm_epsilon)
    order = listed(chips, FIRST[1])
    slots = [order.index(k) for k in range(chips)]
    each = chips // parts
    for p in range(parts):
        for k in range(p * each, (p + 1) * each):
            for ref, place in ((own_ref, core), (other_ref, 1 - core)):
                start = pl.multiple_of((2 * k + place) * width, width)
                scaled_ref[:, pl.ds(start, width)] = (ref[slots[k]].astype(jnp.float32) * factor).astype(jnp.bfloat16)
        part = pl.ds(p * 2 * each * width, 2 * each * width)
        copies.append(pltpu.make_async_copy(scaled_ref.at[:, part], copy_out.at[:, part], sems.at[3 + p]))
        copies[-1].start()
    position = down_column(position_ref)
    period = columns // 8
    lane = lax.broadcasted_iota(jnp.int32, (1, LANES), 1)
    line = lax.broadcasted_iota(jnp.int32, stepped_ref.shape, 0) % period
    spread = jnp.zeros(stepped_ref.shape, jnp.float32)
    for p in range(period):
        flat_column = (p * LANES + lane) % columns
        picked = jnp.sum(jnp.where(position == flat_column, factor, 0.0), axis=0, keepdims=True)
        spread = jnp.where(line == p, picked, spread)
    master_ref[...] = stepped_ref[...] * spread
    copies.append(pltpu.make_async_copy(master_ref, master_out, sems.at[2]))
    copies[-1].start()
    for copy in copies:
        copy.wait()


def finish(position, new_first, new_second, stepped, own, other):
    chips, columns, width = own.shape
    wide = (columns, 2 * chips * width)
    parts = 4 if chips % 4 == 0 else 1
    flat = jax.ShapeDtypeStruct(stepped.shape, jnp.float32)
    return pl.pallas_call(
        finish_kernel,
        in_specs=[pl.BlockSpec(memory_space=pltpu.VMEM)] * 6,
        out_specs=(pl.BlockSpec(memory_space=pl.ANY),) * 4,
        out_shape=(flat, flat, flat, jax.ShapeDtypeStruct(wide, jnp.bfloat16)),
        scratch_shapes=[
            pltpu.VMEM(stepped.shape, jnp.float32),
            pltpu.VMEM(wide, jnp.bfloat16),
            pltpu.SemaphoreType.DMA((3 + parts,)),
        ],
        compiler_params=small(),
    )(position, new_first, new_second, stepped, own, other)


def finish_narrow(owners, stepped, blocks):
    columns = owners.shape[0]
    blocks = blocks.astype(jnp.float32)
    factor = lax.rsqrt(jnp.sum(blocks * blocks, axis=(0, 2)) / D + norm_epsilon)
    scaled = jnp.transpose(blocks * factor[None, :, None], (1, 0, 2))
    flat_factor = jnp.zeros((columns,), jnp.float32).at[flat_positions(owners)].set(factor)
    new_master = (stepped.reshape(-1, columns) * flat_factor).reshape(stepped.shape)
    return (new_master, scaled.reshape(columns, -1).astype(jnp.bfloat16))


def spread(value, axes, size):
    return lax.all_to_all(jnp.broadcast_to(value[None], (size,) + value.shape), axes, 0, 0, tiled=True)


def on_device(grads, master, first_moment, second_moment, owners):
    shards, replicas = lax.axis_size("shard"), lax.axis_size("replica")
    devices = shards * replicas
    columns = owners.shape[0]
    if replicas == 2 and shards == 16 and master.shape[0] // LANES % 48 == 0:
        kept, sent = pack(grads, shards, master.shape[0] // LANES)
        taken = lax.ppermute(sent, "replica", [(0, 1), (1, 0)])
        states = (master, first_moment, second_moment)
        position, *states, pairs = add_pairs(kept, taken, flat_positions(owners), states)
        groups = [listed(shards, FIRST[0])]
        pieces = lax.all_to_all(pairs, "shard", 0, 0, tiled=True, axis_index_groups=groups)
        *updated, copies = middle(position, pieces, states, devices)
        groups = [listed(shards, FIRST[1])]
        own = lax.all_to_all(copies, "shard", 0, 0, tiled=True, axis_index_groups=groups)
        other = lax.ppermute(own, "replica", [(0, 1), (1, 0)])
        *flat, model_copy = finish(position, *updated, own, other)
        return (*(x.reshape(-1) for x in flat), model_copy)
    pieces = lax.all_to_all(grads.reshape(devices, -1), AXES, 0, 0, tiled=True)
    gradient = jnp.sum(pieces.astype(jnp.float32), axis=0) / devices
    new_first, new_second, stepped = adam_step(gradient, master, first_moment, second_moment)
    rows = jnp.take(stepped.reshape(-1, columns), flat_positions(owners), axis=1).T.astype(jnp.bfloat16)
    new_master, model_copy = finish_narrow(owners, stepped, spread(rows, AXES, devices))
    return (new_master, new_first, new_second, model_copy)


def solution(mesh):
    placed = (P(AXES, None), P(AXES), P(AXES), P(AXES), P())
    return jax.shard_map(
        on_device,
        mesh=mesh,
        in_specs=placed,
        out_specs=(P(AXES), P(AXES), P(AXES), P()),
        check_vma=False,
    )
```

```python
import functools

import jax
import jax.numpy as jnp
from jax import lax
from jax.experimental import pallas as pl
from jax.experimental.pallas import tpu as pltpu
from jax.sharding import PartitionSpec as P

D = 8192


learning_rate = 0.1
adam_epsilon = 1e-08
norm_epsilon = 1e-06
first_correction = 1.0 - 0.9**20
second_correction = 1.0 - 0.95**20
AXES = ("shard", "replica")
LANES = 128
FIRST = ((11, 15), (11, 15))


def adam_step(gradient, master, first_moment, second_moment):
    new_first = 0.9 * first_moment + 0.1 * gradient
    new_second = 0.95 * second_moment + 0.05 * gradient * gradient
    stepped = master - learning_rate * (new_first / first_correction) / (
        jnp.sqrt(new_second / second_correction) + adam_epsilon
    )
    return (new_first, new_second, stepped)


def flat_positions(owners):
    column_ids = jnp.arange(owners.shape[0], dtype=jnp.int32)
    ranked_below = owners[None, :] < owners[:, None]
    same_before = (owners[None, :] == owners[:, None]) & (column_ids[None, :] < column_ids[:, None])
    return jnp.sum((ranked_below | same_before).astype(jnp.int32), axis=1)


def small(**more):
    return pltpu.CompilerParams(vmem_limit_bytes=6 * 2**20, **more)


def groups(chips, firsts):
    return [[2 * (k ^ first) + core for k in range(chips)] for core, first in enumerate(firsts)]


def slot(chip, core, firsts):
    return jnp.bitwise_xor(chip, jnp.where(core == 0, firsts[0], firsts[1]))


def pack_kernel(grads_ref, kept_ref, sent_ref):
    chips, lines, lanes = kept_ref.shape
    core = lax.axis_index("replica")
    width = lines * lanes
    for k in range(chips):
        for ref, place in ((kept_ref, core), (sent_ref, 1 - core)):
            start = pl.multiple_of((2 * k + place) * width, width)
            row = grads_ref[:, pl.ds(start, width)].astype(jnp.float32)
            ref[slot(k, place, FIRST[0])] = row.reshape(lines, lanes).astype(jnp.bfloat16)


def pack(grads, chips, lines):
    packed = jax.ShapeDtypeStruct((chips, lines, LANES), jnp.bfloat16)
    return pl.pallas_call(pack_kernel, out_shape=(packed, packed), compiler_params=small())(grads)


def pair_kernel(kept_ref, taken_ref, *refs):
    *held, pairs_ref = refs
    pairs = kept_ref[...].astype(jnp.float32) + taken_ref[...].astype(jnp.float32)
    pairs_ref[...] = pairs.astype(jnp.bfloat16)
    for source, target in zip(held[:4], held[4:]):
        target[...] = source[...]


def add_pairs(kept, taken, position, states):
    flat = jax.ShapeDtypeStruct(kept.shape[1:], jnp.float32)
    position = position[None, :]
    small_shapes = (jax.ShapeDtypeStruct(position.shape, position.dtype), flat, flat, flat)
    return pl.pallas_call(
        pair_kernel,
        out_shape=(*small_shapes, jax.ShapeDtypeStruct(kept.shape, jnp.bfloat16)),
        compiler_params=small(),
    )(kept, taken, position, *(x.reshape(flat.shape) for x in states))


def down_column(row_ref):
    columns = row_ref.shape[1]
    square = (columns, columns)
    same = lax.broadcasted_iota(jnp.int32, square, 0) == lax.broadcasted_iota(jnp.int32, square, 1)
    row = jnp.broadcast_to(row_ref[...].astype(jnp.float32), square)
    return jnp.sum(jnp.where(same, row, 0.0), axis=1, keepdims=True).astype(jnp.int32)


def middle_kernel(
    devices, position_ref, pieces_ref, master_ref, first_ref, second_ref,
    new_first_ref, new_second_ref, stepped_ref, copies_ref,
):
    copies, columns, width = copies_ref.shape
    total = pieces_ref[0].astype(jnp.float32)
    for k in range(1, pieces_ref.shape[0]):
        total = total + pieces_ref[k].astype(jnp.float32)
    gradient = total / devices
    new_first_ref[...], new_second_ref[...], stepped_ref[...] = adam_step(
        gradient, master_ref[...], first_ref[...], second_ref[...]
    )
    period = columns // 8
    span = period * LANES
    group = span // columns
    lines = stepped_ref.shape[0] // period
    wide = [stepped_ref[pl.ds(b, lines, stride=period), :].astype(jnp.bfloat16) for b in range(period)]
    wide = jnp.concatenate(wide, axis=1)
    line = lax.broadcasted_iota(jnp.int32, (lines, width), 0)
    row = lax.broadcasted_iota(jnp.int32, (lines, width), 1)
    repeat = (row // group == line).astype(jnp.bfloat16)
    spread = lax.dot_general(wide, repeat, (((0,), (0,)), ((), ())), preferred_element_type=jnp.float32)
    entry = lax.broadcasted_iota(jnp.int32, (span, width), 0)
    row = lax.broadcasted_iota(jnp.int32, (span, width), 1)
    kept = jnp.where(entry // columns == row % group, spread, 0.0).astype(jnp.bfloat16)
    column = lax.broadcasted_iota(jnp.int32, (columns, span), 1) % columns
    pick = (column == down_column(position_ref)).astype(jnp.bfloat16)
    rows = jnp.dot(pick, kept, preferred_element_type=jnp.float32).astype(jnp.bfloat16)
    for k in range(copies):
        copies_ref[k] = rows


def middle(position, pieces, states, devices):
    columns = position.shape[1]
    flat = jax.ShapeDtypeStruct(pieces.shape[1:], jnp.float32)
    width = flat.size // columns
    return pl.pallas_call(
        functools.partial(middle_kernel, devices),
        out_shape=(flat, flat, flat, jax.ShapeDtypeStruct((pieces.shape[0], columns, width), jnp.bfloat16)),
        compiler_params=small(),
    )(position, pieces, *states)


def finish_kernel(
    position_ref, new_first_ref, new_second_ref, stepped_ref, own_ref, other_ref,
    master_out, first_out, second_out, copy_out, master_ref, scaled_ref, sems,
):
    core = lax.axis_index("replica")
    chips, columns, width = own_ref.shape
    parts = sems.shape[0] - 3
    copies = [
        pltpu.make_async_copy(new_first_ref, first_out, sems.at[0]),
        pltpu.make_async_copy(new_second_ref, second_out, sems.at[1]),
    ]
    for copy in copies:
        copy.start()
    total = jnp.zeros((columns, width), jnp.float32)
    for ref in (own_ref, other_ref):
        for k in range(chips):
            value = ref[k].astype(jnp.float32)
            total = total + value * value
    factor = lax.rsqrt(jnp.sum(total, axis=1, keepdims=True) / D + norm_epsilon)
    each = chips // parts
    for p in range(parts):
        for k in range(p * each, (p + 1) * each):
            for ref, place in ((own_ref, core), (other_ref, 1 - core)):
                start = pl.multiple_of((2 * k + place) * width, width)
                scaled = ref[slot(k, place, FIRST[1])].astype(jnp.float32) * factor
                scaled_ref[:, pl.ds(start, width)] = scaled.astype(jnp.bfloat16)
        part = pl.ds(p * 2 * each * width, 2 * each * width)
        copies.append(pltpu.make_async_copy(scaled_ref.at[:, part], copy_out.at[:, part], sems.at[3 + p]))
        copies[-1].start()
    position = down_column(position_ref)
    period = columns // 8
    lane = lax.broadcasted_iota(jnp.int32, (1, LANES), 1)
    line = lax.broadcasted_iota(jnp.int32, stepped_ref.shape, 0) % period
    spread = jnp.zeros(stepped_ref.shape, jnp.float32)
    for p in range(period):
        flat_column = (p * LANES + lane) % columns
        picked = jnp.sum(jnp.where(position == flat_column, factor, 0.0), axis=0, keepdims=True)
        spread = jnp.where(line == p, picked, spread)
    master_ref[...] = stepped_ref[...] * spread
    copies.append(pltpu.make_async_copy(master_ref, master_out, sems.at[2]))
    copies[-1].start()
    for copy in copies:
        copy.wait()


def finish(position, new_first, new_second, stepped, own, other):
    chips, columns, width = own.shape
    wide = (columns, 2 * chips * width)
    parts = 4 if chips % 4 == 0 else 1
    flat = jax.ShapeDtypeStruct(stepped.shape, jnp.float32)
    return pl.pallas_call(
        finish_kernel,
        in_specs=[pl.BlockSpec(memory_space=pltpu.VMEM)] * 6,
        out_specs=(pl.BlockSpec(memory_space=pl.ANY),) * 4,
        out_shape=(flat, flat, flat, jax.ShapeDtypeStruct(wide, jnp.bfloat16)),
        scratch_shapes=[
            pltpu.VMEM(stepped.shape, jnp.float32),
            pltpu.VMEM(wide, jnp.bfloat16),
            pltpu.SemaphoreType.DMA((3 + parts,)),
        ],
        compiler_params=small(),
    )(position, new_first, new_second, stepped, own, other)


def finish_narrow(owners, stepped, blocks):
    columns = owners.shape[0]
    blocks = blocks.astype(jnp.float32)
    factor = lax.rsqrt(jnp.sum(blocks * blocks, axis=(0, 2)) / D + norm_epsilon)
    scaled = jnp.transpose(blocks * factor[None, :, None], (1, 0, 2))
    flat_factor = jnp.zeros((columns,), jnp.float32).at[flat_positions(owners)].set(factor)
    new_master = (stepped.reshape(-1, columns) * flat_factor).reshape(stepped.shape)
    return (new_master, scaled.reshape(columns, -1).astype(jnp.bfloat16))


def spread(value, axes, size):
    return lax.all_to_all(jnp.broadcast_to(value[None], (size,) + value.shape), axes, 0, 0, tiled=True)


def on_device(grads, master, first_moment, second_moment, owners):
    shards, replicas = lax.axis_size("shard"), lax.axis_size("replica")
    devices = shards * replicas
    columns = owners.shape[0]
    if replicas == 2 and shards == 16 and master.shape[0] // LANES % 48 == 0:
        kept, sent = pack(grads, shards, master.shape[0] // LANES)
        taken = lax.ppermute(sent, "replica", [(0, 1), (1, 0)])
        states = (master, first_moment, second_moment)
        position, *states, pairs = add_pairs(kept, taken, flat_positions(owners), states)
        pieces = lax.all_to_all(
            pairs, AXES, 0, 0, tiled=True, axis_index_groups=groups(shards, FIRST[0])
        )
        *updated, copies = middle(position, pieces, states, devices)
        own = lax.all_to_all(
            copies, AXES, 0, 0, tiled=True, axis_index_groups=groups(shards, FIRST[1])
        )
        other = lax.ppermute(own, "replica", [(0, 1), (1, 0)])
        *flat, model_copy = finish(position, *updated, own, other)
        return (*(x.reshape(-1) for x in flat), model_copy)
    pieces = lax.all_to_all(grads.reshape(devices, -1), AXES, 0, 0, tiled=True)
    gradient = jnp.sum(pieces.astype(jnp.float32), axis=0) / devices
    new_first, new_second, stepped = adam_step(gradient, master, first_moment, second_moment)
    rows = jnp.take(stepped.reshape(-1, columns), flat_positions(owners), axis=1).T.astype(jnp.bfloat16)
    new_master, model_copy = finish_narrow(owners, stepped, spread(rows, AXES, devices))
    return (new_master, new_first, new_second, model_copy)


def solution(mesh):
    placed = (P(AXES, None), P(AXES), P(AXES), P(AXES), P())
    return jax.shard_map(
        on_device,
        mesh=mesh,
        in_specs=placed,
        out_specs=(P(AXES), P(AXES), P(AXES), P()),
        check_vma=False,
    )
```

```python
import functools

import jax
import jax.numpy as jnp
from jax import lax
from jax.experimental import pallas as pl
from jax.experimental.pallas import tpu as pltpu
from jax.sharding import PartitionSpec as P

D = 8192


learning_rate = 0.1
adam_epsilon = 1e-08
norm_epsilon = 1e-06
first_correction = 1.0 - 0.9**20
second_correction = 1.0 - 0.95**20
AXES = ("shard", "replica")
LANES = 128
FIRST = 11
PLANE = 4


def adam_step(gradient, master, first_moment, second_moment):
    new_first = 0.9 * first_moment + 0.1 * gradient
    new_second = 0.95 * second_moment + 0.05 * gradient * gradient
    stepped = master - learning_rate * (new_first / first_correction) / (
        jnp.sqrt(new_second / second_correction) + adam_epsilon
    )
    return (new_first, new_second, stepped)


def flat_positions(owners):
    column_ids = jnp.arange(owners.shape[0], dtype=jnp.int32)
    ranked_below = owners[None, :] < owners[:, None]
    same_before = (owners[None, :] == owners[:, None]) & (column_ids[None, :] < column_ids[:, None])
    return jnp.sum((ranked_below | same_before).astype(jnp.int32), axis=1)


def small(**more):
    return pltpu.CompilerParams(vmem_limit_bytes=6 * 2**20, **more)


def place_of(chip):
    by_layer = chip ^ FIRST
    return by_layer, by_layer % PLANE * PLANE + by_layer // PLANE


def groups(chips):
    lists = [[0] * chips, [0] * chips]
    for chip in range(chips):
        for core, place in enumerate(place_of(chip)):
            lists[core][place] = 2 * chip + core
    return lists


def slot(chip, core):
    places = place_of(chip)
    return jnp.where(core == 0, places[0], places[1])


def pack_kernel(grads_ref, kept_ref, sent_ref):
    chips, lines, lanes = kept_ref.shape
    core = lax.axis_index("replica")
    width = lines * lanes
    for k in range(chips):
        for ref, place in ((kept_ref, core), (sent_ref, 1 - core)):
            start = pl.multiple_of((2 * k + place) * width, width)
            row = grads_ref[:, pl.ds(start, width)].astype(jnp.float32)
            ref[slot(k, place)] = row.reshape(lines, lanes).astype(jnp.bfloat16)


def pack(grads, chips, lines):
    packed = jax.ShapeDtypeStruct((chips, lines, LANES), jnp.bfloat16)
    return pl.pallas_call(pack_kernel, out_shape=(packed, packed), compiler_params=small())(grads)


def pair_kernel(kept_ref, taken_ref, *refs):
    *held, pairs_ref = refs
    pairs = kept_ref[...].astype(jnp.float32) + taken_ref[...].astype(jnp.float32)
    pairs_ref[...] = pairs.astype(jnp.bfloat16)
    for source, target in zip(held[:4], held[4:]):
        target[...] = source[...]


def add_pairs(kept, taken, position, states):
    flat = jax.ShapeDtypeStruct(kept.shape[1:], jnp.float32)
    position = position[None, :]
    small_shapes = (jax.ShapeDtypeStruct(position.shape, position.dtype), flat, flat, flat)
    return pl.pallas_call(
        pair_kernel,
        out_shape=(*small_shapes, jax.ShapeDtypeStruct(kept.shape, jnp.bfloat16)),
        compiler_params=small(),
    )(kept, taken, position, *(x.reshape(flat.shape) for x in states))


def down_column(row_ref):
    columns = row_ref.shape[1]
    square = (columns, columns)
    same = lax.broadcasted_iota(jnp.int32, square, 0) == lax.broadcasted_iota(jnp.int32, square, 1)
    row = jnp.broadcast_to(row_ref[...].astype(jnp.float32), square)
    return jnp.sum(jnp.where(same, row, 0.0), axis=1, keepdims=True).astype(jnp.int32)


def middle_kernel(
    devices, position_ref, pieces_ref, master_ref, first_ref, second_ref,
    new_first_ref, new_second_ref, stepped_ref, copies_ref,
):
    copies, columns, width = copies_ref.shape
    total = pieces_ref[0].astype(jnp.float32)
    for k in range(1, pieces_ref.shape[0]):
        total = total + pieces_ref[k].astype(jnp.float32)
    gradient = total / devices
    new_first_ref[...], new_second_ref[...], stepped_ref[...] = adam_step(
        gradient, master_ref[...], first_ref[...], second_ref[...]
    )
    period = columns // 8
    span = period * LANES
    group = span // columns
    lines = stepped_ref.shape[0] // period
    wide = [stepped_ref[pl.ds(b, lines, stride=period), :].astype(jnp.bfloat16) for b in range(period)]
    wide = jnp.concatenate(wide, axis=1)
    line = lax.broadcasted_iota(jnp.int32, (lines, width), 0)
    row = lax.broadcasted_iota(jnp.int32, (lines, width), 1)
    repeat = (row // group == line).astype(jnp.bfloat16)
    spread = lax.dot_general(wide, repeat, (((0,), (0,)), ((), ())), preferred_element_type=jnp.float32)
    entry = lax.broadcasted_iota(jnp.int32, (span, width), 0)
    row = lax.broadcasted_iota(jnp.int32, (span, width), 1)
    kept = jnp.where(entry // columns == row % group, spread, 0.0).astype(jnp.bfloat16)
    column = lax.broadcasted_iota(jnp.int32, (columns, span), 1) % columns
    pick = (column == down_column(position_ref)).astype(jnp.bfloat16)
    rows = jnp.dot(pick, kept, preferred_element_type=jnp.float32).astype(jnp.bfloat16)
    for k in range(copies):
        copies_ref[k] = rows


def middle(position, pieces, states, devices):
    columns = position.shape[1]
    flat = jax.ShapeDtypeStruct(pieces.shape[1:], jnp.float32)
    width = flat.size // columns
    return pl.pallas_call(
        functools.partial(middle_kernel, devices),
        out_shape=(flat, flat, flat, jax.ShapeDtypeStruct((pieces.shape[0], columns, width), jnp.bfloat16)),
        compiler_params=small(),
    )(position, pieces, *states)


def finish_kernel(
    position_ref, new_first_ref, new_second_ref, stepped_ref, own_ref, other_ref,
    master_out, first_out, second_out, copy_out, master_ref, scaled_ref, sems,
):
    core = lax.axis_index("replica")
    chips, columns, width = own_ref.shape
    parts = sems.shape[0] - 3
    copies = [
        pltpu.make_async_copy(new_first_ref, first_out, sems.at[0]),
        pltpu.make_async_copy(new_second_ref, second_out, sems.at[1]),
    ]
    for copy in copies:
        copy.start()
    total = jnp.zeros((columns, width), jnp.float32)
    for ref in (own_ref, other_ref):
        for k in range(chips):
            value = ref[k].astype(jnp.float32)
            total = total + value * value
    factor = lax.rsqrt(jnp.sum(total, axis=1, keepdims=True) / D + norm_epsilon)
    each = chips // parts
    for p in range(parts):
        for k in range(p * each, (p + 1) * each):
            for ref, place in ((own_ref, core), (other_ref, 1 - core)):
                start = pl.multiple_of((2 * k + place) * width, width)
                scaled = ref[slot(k, place)].astype(jnp.float32) * factor
                scaled_ref[:, pl.ds(start, width)] = scaled.astype(jnp.bfloat16)
        part = pl.ds(p * 2 * each * width, 2 * each * width)
        copies.append(pltpu.make_async_copy(scaled_ref.at[:, part], copy_out.at[:, part], sems.at[3 + p]))
        copies[-1].start()
    position = down_column(position_ref)
    period = columns // 8
    lane = lax.broadcasted_iota(jnp.int32, (1, LANES), 1)
    line = lax.broadcasted_iota(jnp.int32, stepped_ref.shape, 0) % period
    spread = jnp.zeros(stepped_ref.shape, jnp.float32)
    for p in range(period):
        flat_column = (p * LANES + lane) % columns
        picked = jnp.sum(jnp.where(position == flat_column, factor, 0.0), axis=0, keepdims=True)
        spread = jnp.where(line == p, picked, spread)
    master_ref[...] = stepped_ref[...] * spread
    copies.append(pltpu.make_async_copy(master_ref, master_out, sems.at[2]))
    copies[-1].start()
    for copy in copies:
        copy.wait()


def finish(position, new_first, new_second, stepped, own, other):
    chips, columns, width = own.shape
    wide = (columns, 2 * chips * width)
    parts = 4 if chips % 4 == 0 else 1
    flat = jax.ShapeDtypeStruct(stepped.shape, jnp.float32)
    return pl.pallas_call(
        finish_kernel,
        in_specs=[pl.BlockSpec(memory_space=pltpu.VMEM)] * 6,
        out_specs=(pl.BlockSpec(memory_space=pl.ANY),) * 4,
        out_shape=(flat, flat, flat, jax.ShapeDtypeStruct(wide, jnp.bfloat16)),
        scratch_shapes=[
            pltpu.VMEM(stepped.shape, jnp.float32),
            pltpu.VMEM(wide, jnp.bfloat16),
            pltpu.SemaphoreType.DMA((3 + parts,)),
        ],
        compiler_params=small(),
    )(position, new_first, new_second, stepped, own, other)


def finish_narrow(owners, stepped, blocks):
    columns = owners.shape[0]
    blocks = blocks.astype(jnp.float32)
    factor = lax.rsqrt(jnp.sum(blocks * blocks, axis=(0, 2)) / D + norm_epsilon)
    scaled = jnp.transpose(blocks * factor[None, :, None], (1, 0, 2))
    flat_factor = jnp.zeros((columns,), jnp.float32).at[flat_positions(owners)].set(factor)
    new_master = (stepped.reshape(-1, columns) * flat_factor).reshape(stepped.shape)
    return (new_master, scaled.reshape(columns, -1).astype(jnp.bfloat16))


def spread(value, axes, size):
    return lax.all_to_all(jnp.broadcast_to(value[None], (size,) + value.shape), axes, 0, 0, tiled=True)


def on_device(grads, master, first_moment, second_moment, owners):
    shards, replicas = lax.axis_size("shard"), lax.axis_size("replica")
    devices = shards * replicas
    columns = owners.shape[0]
    if replicas == 2 and shards == 16 and master.shape[0] // LANES % 48 == 0:
        kept, sent = pack(grads, shards, master.shape[0] // LANES)
        taken = lax.ppermute(sent, "replica", [(0, 1), (1, 0)])
        states = (master, first_moment, second_moment)
        position, *states, pairs = add_pairs(kept, taken, flat_positions(owners), states)
        pieces = lax.all_to_all(pairs, AXES, 0, 0, tiled=True, axis_index_groups=groups(shards))
        *updated, copies = middle(position, pieces, states, devices)
        own = lax.all_to_all(copies, AXES, 0, 0, tiled=True, axis_index_groups=groups(shards))
        other = lax.ppermute(own, "replica", [(0, 1), (1, 0)])
        *flat, model_copy = finish(position, *updated, own, other)
        return (*(x.reshape(-1) for x in flat), model_copy)
    pieces = lax.all_to_all(grads.reshape(devices, -1), AXES, 0, 0, tiled=True)
    gradient = jnp.sum(pieces.astype(jnp.float32), axis=0) / devices
    new_first, new_second, stepped = adam_step(gradient, master, first_moment, second_moment)
    rows = jnp.take(stepped.reshape(-1, columns), flat_positions(owners), axis=1).T.astype(jnp.bfloat16)
    new_master, model_copy = finish_narrow(owners, stepped, spread(rows, AXES, devices))
    return (new_master, new_first, new_second, model_copy)


def solution(mesh):
    placed = (P(AXES, None), P(AXES), P(AXES), P(AXES), P())
    return jax.shard_map(
        on_device,
        mesh=mesh,
        in_specs=placed,
        out_specs=(P(AXES), P(AXES), P(AXES), P()),
        check_vma=False,
    )
```

```python
import functools

import jax
import jax.numpy as jnp
from jax import lax
from jax.experimental import pallas as pl
from jax.experimental.pallas import tpu as pltpu
from jax.sharding import PartitionSpec as P

D = 8192


learning_rate = 0.1
adam_epsilon = 1e-08
norm_epsilon = 1e-06
first_correction = 1.0 - 0.9**20
second_correction = 1.0 - 0.95**20
AXES = ("shard", "replica")
LANES = 128
FIRST = 11
PLANE = 4


def adam_step(gradient, master, first_moment, second_moment):
    new_first = 0.9 * first_moment + 0.1 * gradient
    new_second = 0.95 * second_moment + 0.05 * gradient * gradient
    stepped = master - learning_rate * (new_first / first_correction) / (
        jnp.sqrt(new_second / second_correction) + adam_epsilon
    )
    return (new_first, new_second, stepped)


def flat_positions(owners):
    column_ids = jnp.arange(owners.shape[0], dtype=jnp.int32)
    ranked_below = owners[None, :] < owners[:, None]
    same_before = (owners[None, :] == owners[:, None]) & (column_ids[None, :] < column_ids[:, None])
    return jnp.sum((ranked_below | same_before).astype(jnp.int32), axis=1)


def small(**more):
    return pltpu.CompilerParams(vmem_limit_bytes=6 * 2**20, **more)


def place_of(chip):
    by_layer = chip ^ FIRST
    by_column = by_layer % PLANE * PLANE + by_layer // PLANE
    return by_column, by_column


def groups(chips):
    lists = [[0] * chips, [0] * chips]
    for chip in range(chips):
        for core, place in enumerate(place_of(chip)):
            lists[core][place] = 2 * chip + core
    return lists


def slot(chip, core):
    places = place_of(chip)
    return jnp.where(core == 0, places[0], places[1])


def pack_kernel(grads_ref, kept_ref, sent_ref):
    chips, lines, lanes = kept_ref.shape
    core = lax.axis_index("replica")
    width = lines * lanes
    for k in range(chips):
        for ref, place in ((kept_ref, core), (sent_ref, 1 - core)):
            start = pl.multiple_of((2 * k + place) * width, width)
            row = grads_ref[:, pl.ds(start, width)].astype(jnp.float32)
            ref[slot(k, place)] = row.reshape(lines, lanes).astype(jnp.bfloat16)


def pack(grads, chips, lines):
    packed = jax.ShapeDtypeStruct((chips, lines, LANES), jnp.bfloat16)
    return pl.pallas_call(pack_kernel, out_shape=(packed, packed), compiler_params=small())(grads)


def pair_kernel(kept_ref, taken_ref, *refs):
    *held, pairs_ref = refs
    pairs = kept_ref[...].astype(jnp.float32) + taken_ref[...].astype(jnp.float32)
    pairs_ref[...] = pairs.astype(jnp.bfloat16)
    for source, target in zip(held[:4], held[4:]):
        target[...] = source[...]


def add_pairs(kept, taken, position, states):
    flat = jax.ShapeDtypeStruct(kept.shape[1:], jnp.float32)
    position = position[None, :]
    small_shapes = (jax.ShapeDtypeStruct(position.shape, position.dtype), flat, flat, flat)
    return pl.pallas_call(
        pair_kernel,
        out_shape=(*small_shapes, jax.ShapeDtypeStruct(kept.shape, jnp.bfloat16)),
        compiler_params=small(),
    )(kept, taken, position, *(x.reshape(flat.shape) for x in states))


def down_column(row_ref):
    columns = row_ref.shape[1]
    square = (columns, columns)
    same = lax.broadcasted_iota(jnp.int32, square, 0) == lax.broadcasted_iota(jnp.int32, square, 1)
    row = jnp.broadcast_to(row_ref[...].astype(jnp.float32), square)
    return jnp.sum(jnp.where(same, row, 0.0), axis=1, keepdims=True).astype(jnp.int32)


def middle_kernel(
    devices, position_ref, pieces_ref, master_ref, first_ref, second_ref,
    new_first_ref, new_second_ref, stepped_ref, copies_ref,
):
    copies, columns, width = copies_ref.shape
    total = pieces_ref[0].astype(jnp.float32)
    for k in range(1, pieces_ref.shape[0]):
        total = total + pieces_ref[k].astype(jnp.float32)
    gradient = total / devices
    new_first_ref[...], new_second_ref[...], stepped_ref[...] = adam_step(
        gradient, master_ref[...], first_ref[...], second_ref[...]
    )
    period = columns // 8
    span = period * LANES
    group = span // columns
    lines = stepped_ref.shape[0] // period
    wide = [stepped_ref[pl.ds(b, lines, stride=period), :].astype(jnp.bfloat16) for b in range(period)]
    wide = jnp.concatenate(wide, axis=1)
    line = lax.broadcasted_iota(jnp.int32, (lines, width), 0)
    row = lax.broadcasted_iota(jnp.int32, (lines, width), 1)
    repeat = (row // group == line).astype(jnp.bfloat16)
    spread = lax.dot_general(wide, repeat, (((0,), (0,)), ((), ())), preferred_element_type=jnp.float32)
    entry = lax.broadcasted_iota(jnp.int32, (span, width), 0)
    row = lax.broadcasted_iota(jnp.int32, (span, width), 1)
    kept = jnp.where(entry // columns == row % group, spread, 0.0).astype(jnp.bfloat16)
    column = lax.broadcasted_iota(jnp.int32, (columns, span), 1) % columns
    pick = (column == down_column(position_ref)).astype(jnp.bfloat16)
    rows = jnp.dot(pick, kept, preferred_element_type=jnp.float32).astype(jnp.bfloat16)
    for k in range(copies):
        copies_ref[k] = rows


def middle(position, pieces, states, devices):
    columns = position.shape[1]
    flat = jax.ShapeDtypeStruct(pieces.shape[1:], jnp.float32)
    width = flat.size // columns
    return pl.pallas_call(
        functools.partial(middle_kernel, devices),
        out_shape=(flat, flat, flat, jax.ShapeDtypeStruct((pieces.shape[0], columns, width), jnp.bfloat16)),
        compiler_params=small(),
    )(position, pieces, *states)


def finish_kernel(
    position_ref, new_first_ref, new_second_ref, stepped_ref, own_ref, other_ref,
    master_out, first_out, second_out, copy_out, master_ref, scaled_ref, sems,
):
    core = lax.axis_index("replica")
    chips, columns, width = own_ref.shape
    parts = sems.shape[0] - 3
    copies = [
        pltpu.make_async_copy(new_first_ref, first_out, sems.at[0]),
        pltpu.make_async_copy(new_second_ref, second_out, sems.at[1]),
    ]
    for copy in copies:
        copy.start()
    total = jnp.zeros((columns, width), jnp.float32)
    for ref in (own_ref, other_ref):
        for k in range(chips):
            value = ref[k].astype(jnp.float32)
            total = total + value * value
    factor = lax.rsqrt(jnp.sum(total, axis=1, keepdims=True) / D + norm_epsilon)
    each = chips // parts
    for p in range(parts):
        for k in range(p * each, (p + 1) * each):
            for ref, place in ((own_ref, core), (other_ref, 1 - core)):
                start = pl.multiple_of((2 * k + place) * width, width)
                scaled = ref[slot(k, place)].astype(jnp.float32) * factor
                scaled_ref[:, pl.ds(start, width)] = scaled.astype(jnp.bfloat16)
        part = pl.ds(p * 2 * each * width, 2 * each * width)
        copies.append(pltpu.make_async_copy(scaled_ref.at[:, part], copy_out.at[:, part], sems.at[3 + p]))
        copies[-1].start()
    position = down_column(position_ref)
    period = columns // 8
    lane = lax.broadcasted_iota(jnp.int32, (1, LANES), 1)
    line = lax.broadcasted_iota(jnp.int32, stepped_ref.shape, 0) % period
    spread = jnp.zeros(stepped_ref.shape, jnp.float32)
    for p in range(period):
        flat_column = (p * LANES + lane) % columns
        picked = jnp.sum(jnp.where(position == flat_column, factor, 0.0), axis=0, keepdims=True)
        spread = jnp.where(line == p, picked, spread)
    master_ref[...] = stepped_ref[...] * spread
    copies.append(pltpu.make_async_copy(master_ref, master_out, sems.at[2]))
    copies[-1].start()
    for copy in copies:
        copy.wait()


def finish(position, new_first, new_second, stepped, own, other):
    chips, columns, width = own.shape
    wide = (columns, 2 * chips * width)
    parts = 4 if chips % 4 == 0 else 1
    flat = jax.ShapeDtypeStruct(stepped.shape, jnp.float32)
    return pl.pallas_call(
        finish_kernel,
        in_specs=[pl.BlockSpec(memory_space=pltpu.VMEM)] * 6,
        out_specs=(pl.BlockSpec(memory_space=pl.ANY),) * 4,
        out_shape=(flat, flat, flat, jax.ShapeDtypeStruct(wide, jnp.bfloat16)),
        scratch_shapes=[
            pltpu.VMEM(stepped.shape, jnp.float32),
            pltpu.VMEM(wide, jnp.bfloat16),
            pltpu.SemaphoreType.DMA((3 + parts,)),
        ],
        compiler_params=small(),
    )(position, new_first, new_second, stepped, own, other)


def finish_narrow(owners, stepped, blocks):
    columns = owners.shape[0]
    blocks = blocks.astype(jnp.float32)
    factor = lax.rsqrt(jnp.sum(blocks * blocks, axis=(0, 2)) / D + norm_epsilon)
    scaled = jnp.transpose(blocks * factor[None, :, None], (1, 0, 2))
    flat_factor = jnp.zeros((columns,), jnp.float32).at[flat_positions(owners)].set(factor)
    new_master = (stepped.reshape(-1, columns) * flat_factor).reshape(stepped.shape)
    return (new_master, scaled.reshape(columns, -1).astype(jnp.bfloat16))


def spread(value, axes, size):
    return lax.all_to_all(jnp.broadcast_to(value[None], (size,) + value.shape), axes, 0, 0, tiled=True)


def on_device(grads, master, first_moment, second_moment, owners):
    shards, replicas = lax.axis_size("shard"), lax.axis_size("replica")
    devices = shards * replicas
    columns = owners.shape[0]
    if replicas == 2 and shards == 16 and master.shape[0] // LANES % 48 == 0:
        kept, sent = pack(grads, shards, master.shape[0] // LANES)
        taken = lax.ppermute(sent, "replica", [(0, 1), (1, 0)])
        states = (master, first_moment, second_moment)
        position, *states, pairs = add_pairs(kept, taken, flat_positions(owners), states)
        pieces = lax.all_to_all(pairs, AXES, 0, 0, tiled=True, axis_index_groups=groups(shards))
        *updated, copies = middle(position, pieces, states, devices)
        own = lax.all_to_all(copies, AXES, 0, 0, tiled=True, axis_index_groups=groups(shards))
        other = lax.ppermute(own, "replica", [(0, 1), (1, 0)])
        *flat, model_copy = finish(position, *updated, own, other)
        return (*(x.reshape(-1) for x in flat), model_copy)
    pieces = lax.all_to_all(grads.reshape(devices, -1), AXES, 0, 0, tiled=True)
    gradient = jnp.sum(pieces.astype(jnp.float32), axis=0) / devices
    new_first, new_second, stepped = adam_step(gradient, master, first_moment, second_moment)
    rows = jnp.take(stepped.reshape(-1, columns), flat_positions(owners), axis=1).T.astype(jnp.bfloat16)
    new_master, model_copy = finish_narrow(owners, stepped, spread(rows, AXES, devices))
    return (new_master, new_first, new_second, model_copy)


def solution(mesh):
    placed = (P(AXES, None), P(AXES), P(AXES), P(AXES), P())
    return jax.shard_map(
        on_device,
        mesh=mesh,
        in_specs=placed,
        out_specs=(P(AXES), P(AXES), P(AXES), P()),
        check_vma=False,
    )
```

```python
import functools

import jax
import jax.numpy as jnp
from jax import lax
from jax.experimental import pallas as pl
from jax.experimental.pallas import tpu as pltpu
from jax.sharding import PartitionSpec as P

D = 8192


learning_rate = 0.1
adam_epsilon = 1e-08
norm_epsilon = 1e-06
first_correction = 1.0 - 0.9**20
second_correction = 1.0 - 0.95**20
AXES = ("shard", "replica")
LANES = 128
FIRST = (11, 7)
PLANE = 4


def adam_step(gradient, master, first_moment, second_moment):
    new_first = 0.9 * first_moment + 0.1 * gradient
    new_second = 0.95 * second_moment + 0.05 * gradient * gradient
    stepped = master - learning_rate * (new_first / first_correction) / (
        jnp.sqrt(new_second / second_correction) + adam_epsilon
    )
    return (new_first, new_second, stepped)


def flat_positions(owners):
    column_ids = jnp.arange(owners.shape[0], dtype=jnp.int32)
    ranked_below = owners[None, :] < owners[:, None]
    same_before = (owners[None, :] == owners[:, None]) & (column_ids[None, :] < column_ids[:, None])
    return jnp.sum((ranked_below | same_before).astype(jnp.int32), axis=1)


def small(**more):
    return pltpu.CompilerParams(vmem_limit_bytes=6 * 2**20, **more)


def place_of(chip, first):
    by_layer = chip ^ first
    return by_layer, by_layer % PLANE * PLANE + by_layer // PLANE


def groups(chips, first):
    lists = [[0] * chips, [0] * chips]
    for chip in range(chips):
        for core, place in enumerate(place_of(chip, first)):
            lists[core][place] = 2 * chip + core
    return lists


def slot(chip, core, first):
    places = place_of(chip, first)
    return jnp.where(core == 0, places[0], places[1])


def pack_kernel(grads_ref, kept_ref, sent_ref):
    chips, lines, lanes = kept_ref.shape
    core = lax.axis_index("replica")
    width = lines * lanes
    for k in range(chips):
        for ref, place in ((kept_ref, core), (sent_ref, 1 - core)):
            start = pl.multiple_of((2 * k + place) * width, width)
            row = grads_ref[:, pl.ds(start, width)].astype(jnp.float32)
            ref[slot(k, place, FIRST[0])] = row.reshape(lines, lanes).astype(jnp.bfloat16)


def pack(grads, chips, lines):
    packed = jax.ShapeDtypeStruct((chips, lines, LANES), jnp.bfloat16)
    return pl.pallas_call(pack_kernel, out_shape=(packed, packed), compiler_params=small())(grads)


def pair_kernel(kept_ref, taken_ref, *refs):
    *held, pairs_ref = refs
    pairs = kept_ref[...].astype(jnp.float32) + taken_ref[...].astype(jnp.float32)
    pairs_ref[...] = pairs.astype(jnp.bfloat16)
    for source, target in zip(held[:4], held[4:]):
        target[...] = source[...]


def add_pairs(kept, taken, position, states):
    flat = jax.ShapeDtypeStruct(kept.shape[1:], jnp.float32)
    position = position[None, :]
    small_shapes = (jax.ShapeDtypeStruct(position.shape, position.dtype), flat, flat, flat)
    return pl.pallas_call(
        pair_kernel,
        out_shape=(*small_shapes, jax.ShapeDtypeStruct(kept.shape, jnp.bfloat16)),
        compiler_params=small(),
    )(kept, taken, position, *(x.reshape(flat.shape) for x in states))


def down_column(row_ref):
    columns = row_ref.shape[1]
    square = (columns, columns)
    same = lax.broadcasted_iota(jnp.int32, square, 0) == lax.broadcasted_iota(jnp.int32, square, 1)
    row = jnp.broadcast_to(row_ref[...].astype(jnp.float32), square)
    return jnp.sum(jnp.where(same, row, 0.0), axis=1, keepdims=True).astype(jnp.int32)


def middle_kernel(
    devices, position_ref, pieces_ref, master_ref, first_ref, second_ref,
    new_first_ref, new_second_ref, stepped_ref, copies_ref,
):
    copies, columns, width = copies_ref.shape
    total = pieces_ref[0].astype(jnp.float32)
    for k in range(1, pieces_ref.shape[0]):
        total = total + pieces_ref[k].astype(jnp.float32)
    gradient = total / devices
    new_first_ref[...], new_second_ref[...], stepped_ref[...] = adam_step(
        gradient, master_ref[...], first_ref[...], second_ref[...]
    )
    period = columns // 8
    span = period * LANES
    group = span // columns
    lines = stepped_ref.shape[0] // period
    wide = [stepped_ref[pl.ds(b, lines, stride=period), :].astype(jnp.bfloat16) for b in range(period)]
    wide = jnp.concatenate(wide, axis=1)
    line = lax.broadcasted_iota(jnp.int32, (lines, width), 0)
    row = lax.broadcasted_iota(jnp.int32, (lines, width), 1)
    repeat = (row // group == line).astype(jnp.bfloat16)
    spread = lax.dot_general(wide, repeat, (((0,), (0,)), ((), ())), preferred_element_type=jnp.float32)
    entry = lax.broadcasted_iota(jnp.int32, (span, width), 0)
    row = lax.broadcasted_iota(jnp.int32, (span, width), 1)
    kept = jnp.where(entry // columns == row % group, spread, 0.0).astype(jnp.bfloat16)
    column = lax.broadcasted_iota(jnp.int32, (columns, span), 1) % columns
    pick = (column == down_column(position_ref)).astype(jnp.bfloat16)
    rows = jnp.dot(pick, kept, preferred_element_type=jnp.float32).astype(jnp.bfloat16)
    for k in range(copies):
        copies_ref[k] = rows


def middle(position, pieces, states, devices):
    columns = position.shape[1]
    flat = jax.ShapeDtypeStruct(pieces.shape[1:], jnp.float32)
    width = flat.size // columns
    return pl.pallas_call(
        functools.partial(middle_kernel, devices),
        out_shape=(flat, flat, flat, jax.ShapeDtypeStruct((pieces.shape[0], columns, width), jnp.bfloat16)),
        compiler_params=small(),
    )(position, pieces, *states)


def finish_kernel(
    position_ref, new_first_ref, new_second_ref, stepped_ref, own_ref, other_ref,
    master_out, first_out, second_out, copy_out, master_ref, scaled_ref, sems,
):
    core = lax.axis_index("replica")
    chips, columns, width = own_ref.shape
    parts = sems.shape[0] - 3
    copies = [
        pltpu.make_async_copy(new_first_ref, first_out, sems.at[0]),
        pltpu.make_async_copy(new_second_ref, second_out, sems.at[1]),
    ]
    for copy in copies:
        copy.start()
    total = jnp.zeros((columns, width), jnp.float32)
    for ref in (own_ref, other_ref):
        for k in range(chips):
            value = ref[k].astype(jnp.float32)
            total = total + value * value
    factor = lax.rsqrt(jnp.sum(total, axis=1, keepdims=True) / D + norm_epsilon)
    each = chips // parts
    for p in range(parts):
        for k in range(p * each, (p + 1) * each):
            for ref, place in ((own_ref, core), (other_ref, 1 - core)):
                start = pl.multiple_of((2 * k + place) * width, width)
                scaled = ref[slot(k, place, FIRST[1])].astype(jnp.float32) * factor
                scaled_ref[:, pl.ds(start, width)] = scaled.astype(jnp.bfloat16)
        part = pl.ds(p * 2 * each * width, 2 * each * width)
        copies.append(pltpu.make_async_copy(scaled_ref.at[:, part], copy_out.at[:, part], sems.at[3 + p]))
        copies[-1].start()
    position = down_column(position_ref)
    period = columns // 8
    lane = lax.broadcasted_iota(jnp.int32, (1, LANES), 1)
    line = lax.broadcasted_iota(jnp.int32, stepped_ref.shape, 0) % period
    spread = jnp.zeros(stepped_ref.shape, jnp.float32)
    for p in range(period):
        flat_column = (p * LANES + lane) % columns
        picked = jnp.sum(jnp.where(position == flat_column, factor, 0.0), axis=0, keepdims=True)
        spread = jnp.where(line == p, picked, spread)
    master_ref[...] = stepped_ref[...] * spread
    copies.append(pltpu.make_async_copy(master_ref, master_out, sems.at[2]))
    copies[-1].start()
    for copy in copies:
        copy.wait()


def finish(position, new_first, new_second, stepped, own, other):
    chips, columns, width = own.shape
    wide = (columns, 2 * chips * width)
    parts = 4 if chips % 4 == 0 else 1
    flat = jax.ShapeDtypeStruct(stepped.shape, jnp.float32)
    return pl.pallas_call(
        finish_kernel,
        in_specs=[pl.BlockSpec(memory_space=pltpu.VMEM)] * 6,
        out_specs=(pl.BlockSpec(memory_space=pl.ANY),) * 4,
        out_shape=(flat, flat, flat, jax.ShapeDtypeStruct(wide, jnp.bfloat16)),
        scratch_shapes=[
            pltpu.VMEM(stepped.shape, jnp.float32),
            pltpu.VMEM(wide, jnp.bfloat16),
            pltpu.SemaphoreType.DMA((3 + parts,)),
        ],
        compiler_params=small(),
    )(position, new_first, new_second, stepped, own, other)


def finish_narrow(owners, stepped, blocks):
    columns = owners.shape[0]
    blocks = blocks.astype(jnp.float32)
    factor = lax.rsqrt(jnp.sum(blocks * blocks, axis=(0, 2)) / D + norm_epsilon)
    scaled = jnp.transpose(blocks * factor[None, :, None], (1, 0, 2))
    flat_factor = jnp.zeros((columns,), jnp.float32).at[flat_positions(owners)].set(factor)
    new_master = (stepped.reshape(-1, columns) * flat_factor).reshape(stepped.shape)
    return (new_master, scaled.reshape(columns, -1).astype(jnp.bfloat16))


def spread(value, axes, size):
    return lax.all_to_all(jnp.broadcast_to(value[None], (size,) + value.shape), axes, 0, 0, tiled=True)


def on_device(grads, master, first_moment, second_moment, owners):
    shards, replicas = lax.axis_size("shard"), lax.axis_size("replica")
    devices = shards * replicas
    columns = owners.shape[0]
    if replicas == 2 and shards == 16 and master.shape[0] // LANES % 48 == 0:
        kept, sent = pack(grads, shards, master.shape[0] // LANES)
        taken = lax.ppermute(sent, "replica", [(0, 1), (1, 0)])
        states = (master, first_moment, second_moment)
        position, *states, pairs = add_pairs(kept, taken, flat_positions(owners), states)
        lists = groups(shards, FIRST[0])
        pieces = lax.all_to_all(pairs, AXES, 0, 0, tiled=True, axis_index_groups=lists)
        *updated, copies = middle(position, pieces, states, devices)
        lists = groups(shards, FIRST[1])
        own = lax.all_to_all(copies, AXES, 0, 0, tiled=True, axis_index_groups=lists)
        other = lax.ppermute(own, "replica", [(0, 1), (1, 0)])
        *flat, model_copy = finish(position, *updated, own, other)
        return (*(x.reshape(-1) for x in flat), model_copy)
    pieces = lax.all_to_all(grads.reshape(devices, -1), AXES, 0, 0, tiled=True)
    gradient = jnp.sum(pieces.astype(jnp.float32), axis=0) / devices
    new_first, new_second, stepped = adam_step(gradient, master, first_moment, second_moment)
    rows = jnp.take(stepped.reshape(-1, columns), flat_positions(owners), axis=1).T.astype(jnp.bfloat16)
    new_master, model_copy = finish_narrow(owners, stepped, spread(rows, AXES, devices))
    return (new_master, new_first, new_second, model_copy)


def solution(mesh):
    placed = (P(AXES, None), P(AXES), P(AXES), P(AXES), P())
    return jax.shard_map(
        on_device,
        mesh=mesh,
        in_specs=placed,
        out_specs=(P(AXES), P(AXES), P(AXES), P()),
        check_vma=False,
    )
```

```python
import functools

import jax
import jax.numpy as jnp
from jax import lax
from jax.experimental import pallas as pl
from jax.experimental.pallas import tpu as pltpu
from jax.sharding import PartitionSpec as P

D = 8192


learning_rate = 0.1
adam_epsilon = 1e-08
norm_epsilon = 1e-06
first_correction = 1.0 - 0.9**20
second_correction = 1.0 - 0.95**20
AXES = ("shard", "replica")
LANES = 128
FIRST = 11
BY_LAYER = (True, False)
PLANE = 4


def adam_step(gradient, master, first_moment, second_moment):
    new_first = 0.9 * first_moment + 0.1 * gradient
    new_second = 0.95 * second_moment + 0.05 * gradient * gradient
    stepped = master - learning_rate * (new_first / first_correction) / (
        jnp.sqrt(new_second / second_correction) + adam_epsilon
    )
    return (new_first, new_second, stepped)


def flat_positions(owners):
    column_ids = jnp.arange(owners.shape[0], dtype=jnp.int32)
    ranked_below = owners[None, :] < owners[:, None]
    same_before = (owners[None, :] == owners[:, None]) & (column_ids[None, :] < column_ids[:, None])
    return jnp.sum((ranked_below | same_before).astype(jnp.int32), axis=1)


def small(**more):
    return pltpu.CompilerParams(vmem_limit_bytes=6 * 2**20, **more)


def place_of(chip, step):
    by_layer = chip ^ FIRST
    by_column = by_layer % PLANE * PLANE + by_layer // PLANE
    return by_layer if BY_LAYER[step] else by_column, by_column


def groups(chips, step):
    lists = [[0] * chips, [0] * chips]
    for chip in range(chips):
        for core, place in enumerate(place_of(chip, step)):
            lists[core][place] = 2 * chip + core
    return lists


def slot(chip, core, step):
    places = place_of(chip, step)
    return jnp.where(core == 0, places[0], places[1])


def pack_kernel(grads_ref, kept_ref, sent_ref):
    chips, lines, lanes = kept_ref.shape
    core = lax.axis_index("replica")
    width = lines * lanes
    for k in range(chips):
        for ref, place in ((kept_ref, core), (sent_ref, 1 - core)):
            start = pl.multiple_of((2 * k + place) * width, width)
            row = grads_ref[:, pl.ds(start, width)].astype(jnp.float32)
            ref[slot(k, place, 0)] = row.reshape(lines, lanes).astype(jnp.bfloat16)


def pack(grads, chips, lines):
    packed = jax.ShapeDtypeStruct((chips, lines, LANES), jnp.bfloat16)
    return pl.pallas_call(pack_kernel, out_shape=(packed, packed), compiler_params=small())(grads)


def pair_kernel(kept_ref, taken_ref, *refs):
    *held, pairs_ref = refs
    pairs = kept_ref[...].astype(jnp.float32) + taken_ref[...].astype(jnp.float32)
    pairs_ref[...] = pairs.astype(jnp.bfloat16)
    for source, target in zip(held[:4], held[4:]):
        target[...] = source[...]


def add_pairs(kept, taken, position, states):
    flat = jax.ShapeDtypeStruct(kept.shape[1:], jnp.float32)
    position = position[None, :]
    small_shapes = (jax.ShapeDtypeStruct(position.shape, position.dtype), flat, flat, flat)
    return pl.pallas_call(
        pair_kernel,
        out_shape=(*small_shapes, jax.ShapeDtypeStruct(kept.shape, jnp.bfloat16)),
        compiler_params=small(),
    )(kept, taken, position, *(x.reshape(flat.shape) for x in states))


def down_column(row_ref):
    columns = row_ref.shape[1]
    square = (columns, columns)
    same = lax.broadcasted_iota(jnp.int32, square, 0) == lax.broadcasted_iota(jnp.int32, square, 1)
    row = jnp.broadcast_to(row_ref[...].astype(jnp.float32), square)
    return jnp.sum(jnp.where(same, row, 0.0), axis=1, keepdims=True).astype(jnp.int32)


def middle_kernel(
    devices, position_ref, pieces_ref, master_ref, first_ref, second_ref,
    new_first_ref, new_second_ref, stepped_ref, copies_ref,
):
    copies, columns, width = copies_ref.shape
    total = pieces_ref[0].astype(jnp.float32)
    for k in range(1, pieces_ref.shape[0]):
        total = total + pieces_ref[k].astype(jnp.float32)
    gradient = total / devices
    new_first_ref[...], new_second_ref[...], stepped_ref[...] = adam_step(
        gradient, master_ref[...], first_ref[...], second_ref[...]
    )
    period = columns // 8
    span = period * LANES
    group = span // columns
    lines = stepped_ref.shape[0] // period
    wide = [stepped_ref[pl.ds(b, lines, stride=period), :].astype(jnp.bfloat16) for b in range(period)]
    wide = jnp.concatenate(wide, axis=1)
    line = lax.broadcasted_iota(jnp.int32, (lines, width), 0)
    row = lax.broadcasted_iota(jnp.int32, (lines, width), 1)
    repeat = (row // group == line).astype(jnp.bfloat16)
    spread = lax.dot_general(wide, repeat, (((0,), (0,)), ((), ())), preferred_element_type=jnp.float32)
    entry = lax.broadcasted_iota(jnp.int32, (span, width), 0)
    row = lax.broadcasted_iota(jnp.int32, (span, width), 1)
    kept = jnp.where(entry // columns == row % group, spread, 0.0).astype(jnp.bfloat16)
    column = lax.broadcasted_iota(jnp.int32, (columns, span), 1) % columns
    pick = (column == down_column(position_ref)).astype(jnp.bfloat16)
    rows = jnp.dot(pick, kept, preferred_element_type=jnp.float32).astype(jnp.bfloat16)
    for k in range(copies):
        copies_ref[k] = rows


def middle(position, pieces, states, devices):
    columns = position.shape[1]
    flat = jax.ShapeDtypeStruct(pieces.shape[1:], jnp.float32)
    width = flat.size // columns
    return pl.pallas_call(
        functools.partial(middle_kernel, devices),
        out_shape=(flat, flat, flat, jax.ShapeDtypeStruct((pieces.shape[0], columns, width), jnp.bfloat16)),
        compiler_params=small(),
    )(position, pieces, *states)


def finish_kernel(
    position_ref, new_first_ref, new_second_ref, stepped_ref, own_ref, other_ref,
    master_out, first_out, second_out, copy_out, master_ref, scaled_ref, sems,
):
    core = lax.axis_index("replica")
    chips, columns, width = own_ref.shape
    parts = sems.shape[0] - 3
    copies = [
        pltpu.make_async_copy(new_first_ref, first_out, sems.at[0]),
        pltpu.make_async_copy(new_second_ref, second_out, sems.at[1]),
    ]
    for copy in copies:
        copy.start()
    total = jnp.zeros((columns, width), jnp.float32)
    for ref in (own_ref, other_ref):
        for k in range(chips):
            value = ref[k].astype(jnp.float32)
            total = total + value * value
    factor = lax.rsqrt(jnp.sum(total, axis=1, keepdims=True) / D + norm_epsilon)
    each = chips // parts
    for p in range(parts):
        for k in range(p * each, (p + 1) * each):
            for ref, place in ((own_ref, core), (other_ref, 1 - core)):
                start = pl.multiple_of((2 * k + place) * width, width)
                scaled = ref[slot(k, place, 1)].astype(jnp.float32) * factor
                scaled_ref[:, pl.ds(start, width)] = scaled.astype(jnp.bfloat16)
        part = pl.ds(p * 2 * each * width, 2 * each * width)
        copies.append(pltpu.make_async_copy(scaled_ref.at[:, part], copy_out.at[:, part], sems.at[3 + p]))
        copies[-1].start()
    position = down_column(position_ref)
    period = columns // 8
    lane = lax.broadcasted_iota(jnp.int32, (1, LANES), 1)
    line = lax.broadcasted_iota(jnp.int32, stepped_ref.shape, 0) % period
    spread = jnp.zeros(stepped_ref.shape, jnp.float32)
    for p in range(period):
        flat_column = (p * LANES + lane) % columns
        picked = jnp.sum(jnp.where(position == flat_column, factor, 0.0), axis=0, keepdims=True)
        spread = jnp.where(line == p, picked, spread)
    master_ref[...] = stepped_ref[...] * spread
    copies.append(pltpu.make_async_copy(master_ref, master_out, sems.at[2]))
    copies[-1].start()
    for copy in copies:
        copy.wait()


def finish(position, new_first, new_second, stepped, own, other):
    chips, columns, width = own.shape
    wide = (columns, 2 * chips * width)
    parts = 4 if chips % 4 == 0 else 1
    flat = jax.ShapeDtypeStruct(stepped.shape, jnp.float32)
    return pl.pallas_call(
        finish_kernel,
        in_specs=[pl.BlockSpec(memory_space=pltpu.VMEM)] * 6,
        out_specs=(pl.BlockSpec(memory_space=pl.ANY),) * 4,
        out_shape=(flat, flat, flat, jax.ShapeDtypeStruct(wide, jnp.bfloat16)),
        scratch_shapes=[
            pltpu.VMEM(stepped.shape, jnp.float32),
            pltpu.VMEM(wide, jnp.bfloat16),
            pltpu.SemaphoreType.DMA((3 + parts,)),
        ],
        compiler_params=small(),
    )(position, new_first, new_second, stepped, own, other)


def finish_narrow(owners, stepped, blocks):
    columns = owners.shape[0]
    blocks = blocks.astype(jnp.float32)
    factor = lax.rsqrt(jnp.sum(blocks * blocks, axis=(0, 2)) / D + norm_epsilon)
    scaled = jnp.transpose(blocks * factor[None, :, None], (1, 0, 2))
    flat_factor = jnp.zeros((columns,), jnp.float32).at[flat_positions(owners)].set(factor)
    new_master = (stepped.reshape(-1, columns) * flat_factor).reshape(stepped.shape)
    return (new_master, scaled.reshape(columns, -1).astype(jnp.bfloat16))


def spread(value, axes, size):
    return lax.all_to_all(jnp.broadcast_to(value[None], (size,) + value.shape), axes, 0, 0, tiled=True)


def on_device(grads, master, first_moment, second_moment, owners):
    shards, replicas = lax.axis_size("shard"), lax.axis_size("replica")
    devices = shards * replicas
    columns = owners.shape[0]
    if replicas == 2 and shards == 16 and master.shape[0] // LANES % 48 == 0:
        kept, sent = pack(grads, shards, master.shape[0] // LANES)
        taken = lax.ppermute(sent, "replica", [(0, 1), (1, 0)])
        states = (master, first_moment, second_moment)
        position, *states, pairs = add_pairs(kept, taken, flat_positions(owners), states)
        pieces = lax.all_to_all(pairs, AXES, 0, 0, tiled=True, axis_index_groups=groups(shards, 0))
        *updated, copies = middle(position, pieces, states, devices)
        own = lax.all_to_all(copies, AXES, 0, 0, tiled=True, axis_index_groups=groups(shards, 1))
        other = lax.ppermute(own, "replica", [(0, 1), (1, 0)])
        *flat, model_copy = finish(position, *updated, own, other)
        return (*(x.reshape(-1) for x in flat), model_copy)
    pieces = lax.all_to_all(grads.reshape(devices, -1), AXES, 0, 0, tiled=True)
    gradient = jnp.sum(pieces.astype(jnp.float32), axis=0) / devices
    new_first, new_second, stepped = adam_step(gradient, master, first_moment, second_moment)
    rows = jnp.take(stepped.reshape(-1, columns), flat_positions(owners), axis=1).T.astype(jnp.bfloat16)
    new_master, model_copy = finish_narrow(owners, stepped, spread(rows, AXES, devices))
    return (new_master, new_first, new_second, model_copy)


def solution(mesh):
    placed = (P(AXES, None), P(AXES), P(AXES), P(AXES), P())
    return jax.shard_map(
        on_device,
        mesh=mesh,
        in_specs=placed,
        out_specs=(P(AXES), P(AXES), P(AXES), P()),
        check_vma=False,
    )
```

```python
import functools

import jax
import jax.numpy as jnp
from jax import lax
from jax.experimental import pallas as pl
from jax.experimental.pallas import tpu as pltpu
from jax.sharding import PartitionSpec as P

D = 8192


learning_rate = 0.1
adam_epsilon = 1e-08
norm_epsilon = 1e-06
first_correction = 1.0 - 0.9**20
second_correction = 1.0 - 0.95**20
AXES = ("shard", "replica")
LANES = 128
FIRST = (11, 10)
PLANE = 4


def adam_step(gradient, master, first_moment, second_moment):
    new_first = 0.9 * first_moment + 0.1 * gradient
    new_second = 0.95 * second_moment + 0.05 * gradient * gradient
    stepped = master - learning_rate * (new_first / first_correction) / (
        jnp.sqrt(new_second / second_correction) + adam_epsilon
    )
    return (new_first, new_second, stepped)


def flat_positions(owners):
    column_ids = jnp.arange(owners.shape[0], dtype=jnp.int32)
    ranked_below = owners[None, :] < owners[:, None]
    same_before = (owners[None, :] == owners[:, None]) & (column_ids[None, :] < column_ids[:, None])
    return jnp.sum((ranked_below | same_before).astype(jnp.int32), axis=1)


def small(**more):
    return pltpu.CompilerParams(vmem_limit_bytes=6 * 2**20, **more)


def place_of(chip, first):
    by_layer = chip ^ first
    return by_layer, by_layer % PLANE * PLANE + by_layer // PLANE


def groups(chips, first):
    lists = [[0] * chips, [0] * chips]
    for chip in range(chips):
        for core, place in enumerate(place_of(chip, first)):
            lists[core][place] = 2 * chip + core
    return lists


def slot(chip, core, first):
    places = place_of(chip, first)
    return jnp.where(core == 0, places[0], places[1])


def pack_kernel(grads_ref, kept_ref, sent_ref):
    chips, lines, lanes = kept_ref.shape
    core = lax.axis_index("replica")
    width = lines * lanes
    for k in range(chips):
        for ref, place in ((kept_ref, core), (sent_ref, 1 - core)):
            start = pl.multiple_of((2 * k + place) * width, width)
            row = grads_ref[:, pl.ds(start, width)].astype(jnp.float32)
            ref[slot(k, place, FIRST[0])] = row.reshape(lines, lanes).astype(jnp.bfloat16)


def pack(grads, chips, lines):
    packed = jax.ShapeDtypeStruct((chips, lines, LANES), jnp.bfloat16)
    return pl.pallas_call(pack_kernel, out_shape=(packed, packed), compiler_params=small())(grads)


def pair_kernel(kept_ref, taken_ref, *refs):
    *held, pairs_ref = refs
    pairs = kept_ref[...].astype(jnp.float32) + taken_ref[...].astype(jnp.float32)
    pairs_ref[...] = pairs.astype(jnp.bfloat16)
    for source, target in zip(held[:4], held[4:]):
        target[...] = source[...]


def add_pairs(kept, taken, position, states):
    flat = jax.ShapeDtypeStruct(kept.shape[1:], jnp.float32)
    position = position[None, :]
    small_shapes = (jax.ShapeDtypeStruct(position.shape, position.dtype), flat, flat, flat)
    return pl.pallas_call(
        pair_kernel,
        out_shape=(*small_shapes, jax.ShapeDtypeStruct(kept.shape, jnp.bfloat16)),
        compiler_params=small(),
    )(kept, taken, position, *(x.reshape(flat.shape) for x in states))


def down_column(row_ref):
    columns = row_ref.shape[1]
    square = (columns, columns)
    same = lax.broadcasted_iota(jnp.int32, square, 0) == lax.broadcasted_iota(jnp.int32, square, 1)
    row = jnp.broadcast_to(row_ref[...].astype(jnp.float32), square)
    return jnp.sum(jnp.where(same, row, 0.0), axis=1, keepdims=True).astype(jnp.int32)


def middle_kernel(
    devices, position_ref, pieces_ref, master_ref, first_ref, second_ref,
    new_first_ref, new_second_ref, stepped_ref, copies_ref,
):
    copies, columns, width = copies_ref.shape
    total = pieces_ref[0].astype(jnp.float32)
    for k in range(1, pieces_ref.shape[0]):
        total = total + pieces_ref[k].astype(jnp.float32)
    gradient = total / devices
    new_first_ref[...], new_second_ref[...], stepped_ref[...] = adam_step(
        gradient, master_ref[...], first_ref[...], second_ref[...]
    )
    period = columns // 8
    span = period * LANES
    group = span // columns
    lines = stepped_ref.shape[0] // period
    wide = [stepped_ref[pl.ds(b, lines, stride=period), :].astype(jnp.bfloat16) for b in range(period)]
    wide = jnp.concatenate(wide, axis=1)
    line = lax.broadcasted_iota(jnp.int32, (lines, width), 0)
    row = lax.broadcasted_iota(jnp.int32, (lines, width), 1)
    repeat = (row // group == line).astype(jnp.bfloat16)
    spread = lax.dot_general(wide, repeat, (((0,), (0,)), ((), ())), preferred_element_type=jnp.float32)
    entry = lax.broadcasted_iota(jnp.int32, (span, width), 0)
    row = lax.broadcasted_iota(jnp.int32, (span, width), 1)
    kept = jnp.where(entry // columns == row % group, spread, 0.0).astype(jnp.bfloat16)
    column = lax.broadcasted_iota(jnp.int32, (columns, span), 1) % columns
    pick = (column == down_column(position_ref)).astype(jnp.bfloat16)
    rows = jnp.dot(pick, kept, preferred_element_type=jnp.float32).astype(jnp.bfloat16)
    for k in range(copies):
        copies_ref[k] = rows


def middle(position, pieces, states, devices):
    columns = position.shape[1]
    flat = jax.ShapeDtypeStruct(pieces.shape[1:], jnp.float32)
    width = flat.size // columns
    return pl.pallas_call(
        functools.partial(middle_kernel, devices),
        out_shape=(flat, flat, flat, jax.ShapeDtypeStruct((pieces.shape[0], columns, width), jnp.bfloat16)),
        compiler_params=small(),
    )(position, pieces, *states)


def finish_kernel(
    position_ref, new_first_ref, new_second_ref, stepped_ref, own_ref, other_ref,
    master_out, first_out, second_out, copy_out, master_ref, scaled_ref, sems,
):
    core = lax.axis_index("replica")
    chips, columns, width = own_ref.shape
    parts = sems.shape[0] - 3
    copies = [
        pltpu.make_async_copy(new_first_ref, first_out, sems.at[0]),
        pltpu.make_async_copy(new_second_ref, second_out, sems.at[1]),
    ]
    for copy in copies:
        copy.start()
    total = jnp.zeros((columns, width), jnp.float32)
    for ref in (own_ref, other_ref):
        for k in range(chips):
            value = ref[k].astype(jnp.float32)
            total = total + value * value
    factor = lax.rsqrt(jnp.sum(total, axis=1, keepdims=True) / D + norm_epsilon)
    each = chips // parts
    for p in range(parts):
        for k in range(p * each, (p + 1) * each):
            for ref, place in ((own_ref, core), (other_ref, 1 - core)):
                start = pl.multiple_of((2 * k + place) * width, width)
                scaled = ref[slot(k, place, FIRST[1])].astype(jnp.float32) * factor
                scaled_ref[:, pl.ds(start, width)] = scaled.astype(jnp.bfloat16)
        part = pl.ds(p * 2 * each * width, 2 * each * width)
        copies.append(pltpu.make_async_copy(scaled_ref.at[:, part], copy_out.at[:, part], sems.at[3 + p]))
        copies[-1].start()
    position = down_column(position_ref)
    period = columns // 8
    lane = lax.broadcasted_iota(jnp.int32, (1, LANES), 1)
    line = lax.broadcasted_iota(jnp.int32, stepped_ref.shape, 0) % period
    spread = jnp.zeros(stepped_ref.shape, jnp.float32)
    for p in range(period):
        flat_column = (p * LANES + lane) % columns
        picked = jnp.sum(jnp.where(position == flat_column, factor, 0.0), axis=0, keepdims=True)
        spread = jnp.where(line == p, picked, spread)
    master_ref[...] = stepped_ref[...] * spread
    copies.append(pltpu.make_async_copy(master_ref, master_out, sems.at[2]))
    copies[-1].start()
    for copy in copies:
        copy.wait()


def finish(position, new_first, new_second, stepped, own, other):
    chips, columns, width = own.shape
    wide = (columns, 2 * chips * width)
    parts = 4 if chips % 4 == 0 else 1
    flat = jax.ShapeDtypeStruct(stepped.shape, jnp.float32)
    return pl.pallas_call(
        finish_kernel,
        in_specs=[pl.BlockSpec(memory_space=pltpu.VMEM)] * 6,
        out_specs=(pl.BlockSpec(memory_space=pl.ANY),) * 4,
        out_shape=(flat, flat, flat, jax.ShapeDtypeStruct(wide, jnp.bfloat16)),
        scratch_shapes=[
            pltpu.VMEM(stepped.shape, jnp.float32),
            pltpu.VMEM(wide, jnp.bfloat16),
            pltpu.SemaphoreType.DMA((3 + parts,)),
        ],
        compiler_params=small(),
    )(position, new_first, new_second, stepped, own, other)


def finish_narrow(owners, stepped, blocks):
    columns = owners.shape[0]
    blocks = blocks.astype(jnp.float32)
    factor = lax.rsqrt(jnp.sum(blocks * blocks, axis=(0, 2)) / D + norm_epsilon)
    scaled = jnp.transpose(blocks * factor[None, :, None], (1, 0, 2))
    flat_factor = jnp.zeros((columns,), jnp.float32).at[flat_positions(owners)].set(factor)
    new_master = (stepped.reshape(-1, columns) * flat_factor).reshape(stepped.shape)
    return (new_master, scaled.reshape(columns, -1).astype(jnp.bfloat16))


def spread(value, axes, size):
    return lax.all_to_all(jnp.broadcast_to(value[None], (size,) + value.shape), axes, 0, 0, tiled=True)


def on_device(grads, master, first_moment, second_moment, owners):
    shards, replicas = lax.axis_size("shard"), lax.axis_size("replica")
    devices = shards * replicas
    columns = owners.shape[0]
    if replicas == 2 and shards == 16 and master.shape[0] // LANES % 48 == 0:
        kept, sent = pack(grads, shards, master.shape[0] // LANES)
        taken = lax.ppermute(sent, "replica", [(0, 1), (1, 0)])
        states = (master, first_moment, second_moment)
        position, *states, pairs = add_pairs(kept, taken, flat_positions(owners), states)
        lists = groups(shards, FIRST[0])
        pieces = lax.all_to_all(pairs, AXES, 0, 0, tiled=True, axis_index_groups=lists)
        *updated, copies = middle(position, pieces, states, devices)
        lists = groups(shards, FIRST[1])
        own = lax.all_to_all(copies, AXES, 0, 0, tiled=True, axis_index_groups=lists)
        other = lax.ppermute(own, "replica", [(0, 1), (1, 0)])
        *flat, model_copy = finish(position, *updated, own, other)
        return (*(x.reshape(-1) for x in flat), model_copy)
    pieces = lax.all_to_all(grads.reshape(devices, -1), AXES, 0, 0, tiled=True)
    gradient = jnp.sum(pieces.astype(jnp.float32), axis=0) / devices
    new_first, new_second, stepped = adam_step(gradient, master, first_moment, second_moment)
    rows = jnp.take(stepped.reshape(-1, columns), flat_positions(owners), axis=1).T.astype(jnp.bfloat16)
    new_master, model_copy = finish_narrow(owners, stepped, spread(rows, AXES, devices))
    return (new_master, new_first, new_second, model_copy)


def solution(mesh):
    placed = (P(AXES, None), P(AXES), P(AXES), P(AXES), P())
    return jax.shard_map(
        on_device,
        mesh=mesh,
        in_specs=placed,
        out_specs=(P(AXES), P(AXES), P(AXES), P()),
        check_vma=False,
    )
```
